128 devices in a mesh: scan: 16 (over y, x), band: 8 (over z, core).
Axes of the slice: x: 4, y: 4, z: 4, core: 2. Of those that a mesh axis runs over, the one named last changes fastest.
Arguments:
- objects: float32 [4, 2048, 8192], P(None, 'band', 'scan'), may hold values from -5 to 5
- probe_field: float32 [2, 256, 256], replicated, may hold values from -5 to 5
- propagator_phase: float32 [256, 256], replicated, may hold values from -3.140625 to 3.140625
- patterns: float32 [8, 16, 4, 256, 256], P('band', 'scan'), may hold values from 0.05 to 4
- offset_row: int32 [8, 64], P('band', 'scan'), may hold values from 0 to 255
- offset_column: int32 [8, 64], P('band', 'scan'), may hold values from 0 to 511
- live_counts: int32 [8, 16], P('band', 'scan'), may hold values from 2 to 4, as said below
Outputs:
- object_out: float32 [4, 2048, 8192], P(None, 'band', 'scan')
- probe_out: float32 [2, 256, 256], replicated
The draws below stay inside these ranges and needn't reach their ends.
Inputs may be any that keep to these rules, and one draw needn't show every extreme that they name: `live_counts`: every tile has at least 2 live slots and at most 4; some tile has exactly 4.
All inputs are finite; a program needn't handle non-finite values.
Results may differ from the reference program's by a relative error of at most 0.0003.
Values sent between devices are 32-bit elements; how exact they have to be, the bound alone decides.
No kernel may reach another device: no remote copies, remote signals or barrier semaphores. Data moves between devices by JAX's collectives and lax.ppermute only.
A program may use at most 128 MiB of HBM per device.

```python
import math
import jax
import jax.numpy as jnp
from jax import lax

W = 256
TH = 256
TW = 512
CAP = 4
ITERS = 2
NR = 2048
NC = 8192
N_SCAN = 16
N_BAND = 8


def draw_live_counts(key, part):
    key = jax.random.fold_in(key, 7)
    key_extra, key_spot = jax.random.split(key, 2)
    extra = jax.random.randint(key_extra, (N_BAND, N_SCAN), 0, CAP // 2 + 1)
    counts = CAP // 2 + extra
    counts = jnp.minimum(counts, CAP)
    spot = jax.random.randint(key_spot, (), 0, N_BAND * N_SCAN)
    flat = counts.reshape(-1)
    flat = jnp.where(jnp.arange(N_BAND * N_SCAN) == spot, CAP, flat)
    return flat.reshape(N_BAND, N_SCAN).astype(jnp.int32)


def set_ends(result, own_key, least, high):
    place = [jax.random.randint(jax.random.fold_in(own_key, axis), (), 0, length) for axis, length in enumerate(result.shape)]
    longest = result.shape.index(max(result.shape))
    next_to = place[:longest] + [(place[longest] + 1) % result.shape[longest]] + place[longest + 1:]
    return result.at[tuple(place)].set(least).at[tuple(next_to)].set(high)


def level_of(stream_key, dims, cuts, smallest, high):
    level = 1.0
    for dim, parts in cuts:
        heights = jax.random.uniform(jax.random.fold_in(jax.random.fold_in(stream_key, 6), dim), (parts,), jnp.float32, smallest / len(cuts), high / len(cuts))
        level = level * jnp.repeat(jnp.exp(heights), dims[dim] // parts).reshape((-1,) + (1,) * (len(dims) - 1 - dim))
    return level


def normal_values(stream_key, dims, scale, bound, shards=(), held_as=jnp.bfloat16):
    entries = jax.random.normal(stream_key, dims, jnp.float32) * scale
    if len(shards) > 0:
        entries = level_of(stream_key, dims, shards, -0.22, 0.18) * entries
    return jnp.clip(entries, min=-bound, max=bound).astype(held_as)


def setup_inputs(seed: int = 0) -> dict:
    splits = jax.random.split(jax.random.key(seed), 8)
    objects = normal_values(splits[0], (4, NR, NC), 0.7, 5.0, ((1, 8), (2, 16)), jnp.float32)
    probe_field = normal_values(splits[1], (2, W, W), 0.7, 5.0, (), jnp.float32)
    propagator_phase = jnp.clip(jax.random.uniform(splits[2], (W, W), jnp.float32, -3.140625, 3.140625), -3.140625, 3.140625)
    patterns = jnp.clip(jnp.exp(math.log(4.0) - 4.3820266 * jax.random.uniform(splits[3], (N_BAND, N_SCAN, CAP, W, W), jnp.float32) ** level_of(splits[3], (N_BAND, N_SCAN, CAP, W, W), ((0, 8), (1, 16)), -0.2, 0.2)), 0.05, 4.0)
    offset_row = set_ends(jax.random.randint(splits[4], (N_BAND, N_SCAN * CAP), 0, TH), jax.random.fold_in(splits[4], 1), 0, TH - 1).astype(jnp.int32)
    offset_column = set_ends(jax.random.randint(splits[5], (N_BAND, N_SCAN * CAP), 0, TW), jax.random.fold_in(splits[5], 1), 0, TW - 1).astype(jnp.int32)
    live_counts = draw_live_counts(jax.random.fold_in(splits[7], 71), 0)
    return dict(objects=objects, probe_field=probe_field, propagator_phase=propagator_phase, patterns=patterns, offset_row=offset_row, offset_column=offset_column, live_counts=live_counts)


object_rate = 0.1
probe_rate = 2.0
power_eps = 1e-06

def reference(objects, probe_field, propagator_phase, patterns, offset_row, offset_column, live_counts):
    band_start = jnp.arange(N_BAND, dtype=jnp.int32)[:, None, None] * TH
    scan_start = jnp.arange(N_SCAN, dtype=jnp.int32)[None, :, None] * TW
    rows_all = (offset_row.reshape(N_BAND, N_SCAN, CAP) + band_start).reshape(-1).astype(jnp.int32)
    cols_all = (offset_column.reshape(N_BAND, N_SCAN, CAP) + scan_start).reshape(-1).astype(jnp.int32)
    slot_index = jnp.arange(CAP, dtype=jnp.int32)[None, None, :]
    live = (slot_index < live_counts[:, :, None]).astype(jnp.float32).reshape(-1)
    flat_patterns = patterns.reshape(-1, W, W)
    total = jnp.sum(live)
    first = objects[0] + 1j * objects[1]
    second = objects[2] + 1j * objects[3]
    probe = probe_field[0] + 1j * probe_field[1]
    kernel = jnp.cos(propagator_phase) + 1j * jnp.sin(propagator_phase)
    for step in range(ITERS):
        first_pad = jnp.pad(first, ((0, W), (0, W)))
        second_pad = jnp.pad(second, ((0, W), (0, W)))

        def one_slot(carry, item):
            grad_first, grad_second, grad_probe = carry
            row, column, pattern, alive = item
            piece_one = lax.dynamic_slice(first_pad, (row, column), (W, W))
            piece_two = lax.dynamic_slice(second_pad, (row, column), (W, W))
            spread = jnp.fft.ifft2(kernel * jnp.fft.fft2(probe * piece_one, norm='ortho'), norm='ortho')
            far = jnp.fft.fft2(spread * piece_two, norm='ortho')
            misfit = (jnp.real(far) * jnp.real(far) + jnp.imag(far) * jnp.imag(far) - pattern) * alive
            back_two = jnp.fft.ifft2(misfit * far, norm='ortho')
            grad_two = jnp.conj(spread) * back_two
            back_spread = jnp.conj(piece_two) * back_two
            back_one = jnp.fft.ifft2(jnp.conj(kernel) * jnp.fft.fft2(back_spread, norm='ortho'), norm='ortho')
            grad_one = jnp.conj(probe) * back_one
            grad_probe = grad_probe + jnp.conj(piece_one) * back_one
            current = lax.dynamic_slice(grad_first, (row, column), (W, W))
            grad_first = lax.dynamic_update_slice(grad_first, current + grad_one, (row, column))
            current = lax.dynamic_slice(grad_second, (row, column), (W, W))
            grad_second = lax.dynamic_update_slice(grad_second, current + grad_two, (row, column))
            return ((grad_first, grad_second, grad_probe), None)
        start = (jnp.zeros(first_pad.shape, first_pad.dtype), jnp.zeros(first_pad.shape, first_pad.dtype), jnp.zeros(probe.shape, first_pad.dtype))
        sums, unused = lax.scan(one_slot, start, (rows_all, cols_all, flat_patterns, live))
        first = first - object_rate * sums[0][:NR, :NC]
        second = second - object_rate * sums[1][:NR, :NC]
        moved = probe - probe_rate / total * sums[2]
        power = jnp.sum(jnp.real(moved) * jnp.real(moved) + jnp.imag(moved) * jnp.imag(moved))
        probe = moved * jnp.sqrt(W * W / (power + power_eps))
    object_out = jnp.stack([jnp.real(first), jnp.imag(first), jnp.real(second), jnp.imag(second)])
    probe_out = jnp.stack([jnp.real(probe), jnp.imag(probe)])
    return (object_out, probe_out)
```

```python
import functools
import math

import jax
import jax.numpy as jnp
import ml_dtypes
import numpy as np
from jax import lax
from jax.experimental import pallas as pl
from jax.experimental.pallas import tpu as pltpu
from jax.sharding import PartitionSpec as P

ITERS = 2
SIDE = 256
HALF = SIDE // 2
TALL = 264
WIDE = 384

object_rate = 0.1
probe_rate = 2.0
power_eps = 1e-06

f32 = jnp.float32
bf16 = jnp.bfloat16


def halves(matrix):
    high = matrix.astype(ml_dtypes.bfloat16)
    low = (matrix - high.astype(np.float64)).astype(ml_dtypes.bfloat16)
    return [high, low]


def tables():
    point = np.arange(HALF)[None, :]
    result = []
    for parity in (0, 1):
        frequency = 2 * np.arange(HALF)[:, None] + parity
        angle = -2.0 * np.pi / SIDE * (frequency * point % SIDE)
        real = np.cos(angle) / math.sqrt(SIDE)
        imag = np.sin(angle) / math.sqrt(SIDE)
        matrix = np.block([[real, -imag], [imag, real]])
        result += halves(matrix) + halves(matrix.T)
    return np.stack(result)


E_HI, E_LO, ET_HI, ET_LO, O_HI, O_LO, OT_HI, OT_LO = range(8)


def dot(a, b):
    return jnp.dot(a, b, preferred_element_type=f32)


def split(x):
    high = x.astype(bf16)
    low = (x - high.astype(f32)).astype(bf16)
    return high, low


def mul_left(m, hi, x):
    high, low = split(x)
    return dot(m[hi], high) + dot(m[hi], low) + dot(m[hi + 1], high)


def mul_right(x, m, hi):
    high, low = split(x)
    return dot(high, m[hi]) + dot(low, m[hi]) + dot(high, m[hi + 1])


def rows(*parts):
    return jnp.concatenate(parts, axis=0)


def cols(*parts):
    return jnp.concatenate(parts, axis=1)


def forward(re, im, m):
    even = mul_left(m, E_HI, rows(re[:HALF] + re[HALF:], im[:HALF] + im[HALF:]))
    odd = mul_left(m, O_HI, rows(re[:HALF] - re[HALF:], im[:HALF] - im[HALF:]))
    re = rows(even[:HALF], odd[:HALF])
    im = rows(even[HALF:], odd[HALF:])
    u = mul_right(cols(re[:, :HALF] + re[:, HALF:], im[:, :HALF] + im[:, HALF:]), m, ET_HI)
    v = mul_right(cols(re[:, :HALF] - re[:, HALF:], im[:, :HALF] - im[:, HALF:]), m, OT_HI)
    return u, v


def backward(u, v, m):
    a = mul_right(u, m, E_HI)
    b = mul_right(v, m, O_HI)
    re = cols(a[:, :HALF] + b[:, :HALF], a[:, :HALF] - b[:, :HALF])
    im = cols(a[:, HALF:] + b[:, HALF:], a[:, HALF:] - b[:, HALF:])
    a = mul_left(m, ET_HI, rows(re[:HALF], im[:HALF]))
    b = mul_left(m, OT_HI, rows(re[HALF:], im[HALF:]))
    re = rows(a[:HALF] + b[:HALF], a[:HALF] - b[:HALF])
    im = rows(a[HALF:] + b[HALF:], a[HALF:] - b[HALF:])
    return re, im


def by_kernel(u, h, place, sign):
    re, im = u[:, :HALF], u[:, HALF:]
    hr = h[0, :, place * HALF : (place + 1) * HALF]
    hi = h[1, :, place * HALF : (place + 1) * HALF]
    if sign > 0:
        return cols(hr * re - hi * im, hr * im + hi * re)
    return cols(hr * re + hi * im, hr * im - hi * re)


def window(ext, plane, spot):
    row0, row_rest, col0, col_rest = spot
    slab = ext[plane, pl.ds(row0, TALL), pl.ds(col0, WIDE)]
    slab = pltpu.roll(slab, lax.rem(WIDE - col_rest, WIDE), 1)[:, :SIDE]
    return pltpu.roll(slab, lax.rem(TALL - row_rest, TALL), 0)[:SIDE]


def place(row_ref, col_ref, slot):
    row = row_ref[slot]
    col = col_ref[slot]
    row_rest = lax.rem(row, 8)
    col_rest = lax.rem(col, 128)
    row0 = pl.multiple_of(row - row_rest, 8)
    col0 = pl.multiple_of(col - col_rest, 128)
    return row0, row_rest, col0, col_rest


def assemble(ext, own, right, lower):
    tile_rows, tile_cols = own.shape[1:]
    ext[:, :tile_rows, :tile_cols] = own[...]
    ext[:, :tile_rows, tile_cols:] = right[...]
    ext[:, tile_rows:, :] = lower[...]


def spread_kernel(row_ref, col_ref, own, right, lower, probe, h, m, psi, piece, ext):
    slot = pl.program_id(0)

    @pl.when(slot == 0)
    def _():
        assemble(ext, own, right, lower)

    spot = place(row_ref, col_ref, slot)
    ar = window(ext, 0, spot)
    ai = window(ext, 1, spot)
    piece[0, 0] = ar
    piece[0, 1] = ai
    pr, pi = probe[0], probe[1]
    u, v = forward(pr * ar - pi * ai, pr * ai + pi * ar, m)
    re, im = backward(by_kernel(u, h, 0, 1), by_kernel(v, h, 1, 1), m)
    psi[0, 0] = re
    psi[0, 1] = im


def add_window(accum, plane, grad, spot):
    row0, row_rest, col0, col_rest = spot
    tall = rows(grad, jnp.zeros((TALL - SIDE, SIDE), f32))
    tall = pltpu.roll(tall, row_rest, 0)
    wide = cols(tall, jnp.zeros((TALL, WIDE - SIDE), f32))
    wide = pltpu.roll(wide, col_rest, 1)
    accum[plane, pl.ds(row0, TALL), pl.ds(col0, WIDE)] += wide


def misfit_kernel(
    row_ref, col_ref, live_ref, own, right, lower, psi, pattern, m, accum, back, ext
):
    slot = pl.program_id(0)

    @pl.when(slot == 0)
    def _():
        assemble(ext, own, right, lower)
        accum[...] = jnp.zeros_like(accum)

    spot = place(row_ref, col_ref, slot)
    ar = window(ext, 0, spot)
    ai = window(ext, 1, spot)
    sr, si = psi[0, 0], psi[0, 1]
    u, v = forward(sr * ar - si * ai, sr * ai + si * ar, m)
    live = (slot < live_ref[0]).astype(f32)

    def weigh(part, measured):
        re, im = part[:, :HALF], part[:, HALF:]
        weight = (re * re + im * im - measured) * live
        return cols(weight * re, weight * im)

    u = weigh(u, pattern[0, :, :HALF])
    v = weigh(v, pattern[0, :, HALF:])
    re, im = backward(u, v, m)
    back[0, 0] = ar * re + ai * im
    back[0, 1] = ar * im - ai * re
    add_window(accum, 0, sr * re + si * im, spot)
    add_window(accum, 1, sr * im - si * re, spot)


def first_kernel(row_ref, col_ref, back, piece, probe, h, m, accum, gprobe):
    slot = pl.program_id(0)

    @pl.when(slot == 0)
    def _():
        accum[...] = jnp.zeros_like(accum)
        gprobe[...] = jnp.zeros_like(gprobe)

    spot = place(row_ref, col_ref, slot)
    u, v = forward(back[0, 0], back[0, 1], m)
    re, im = backward(by_kernel(u, h, 0, -1), by_kernel(v, h, 1, -1), m)
    ar, ai = piece[0, 0], piece[0, 1]
    gprobe[0] += ar * re + ai * im
    gprobe[1] += ar * im - ai * re
    pr, pi = probe[0], probe[1]
    add_window(accum, 0, pr * re + pi * im, spot)
    add_window(accum, 1, pr * im - pi * re, spot)


def picked(value, move):
    total = None
    for _ in range(3):
        part = value.astype(bf16)
        value = value - part.astype(f32)
        moved = move(part)
        total = moved if total is None else total + moved
    return total


def order_kernel(x, swap, out):
    value = picked(x[0], lambda part: dot(part, swap[0]))
    out[0] = picked(value, lambda part: dot(swap[1], part))


SMEM = pl.BlockSpec(memory_space=pltpu.SMEM)


def whole(shape):
    return pl.BlockSpec(shape, lambda i: (0,) * len(shape))


def per_slot(shape):
    return pl.BlockSpec((1,) + shape, lambda i: (i,) + (0,) * len(shape))


def call(kernel, name, slots, in_specs, out_specs, out_shape, scratch, flops, size):
    return pl.pallas_call(
        kernel,
        name=name,
        grid=(slots,),
        in_specs=in_specs,
        out_specs=out_specs,
        out_shape=out_shape,
        scratch_shapes=scratch,
        compiler_params=pltpu.CompilerParams(vmem_limit_bytes=48 * 1024 * 1024),
        cost_estimate=pl.CostEstimate(flops=flops, bytes_accessed=size, transcendentals=0),
    )


def shape(*dims):
    return jax.ShapeDtypeStruct(dims, f32)


FIELD = (2, SIDE, SIDE)
MATS = (8, SIDE, SIDE)
EXT = (2, 2 * SIDE, 3 * SIDE)
PIECES = [whole((2, SIDE, 2 * SIDE)), whole((2, SIDE, SIDE)), whole((2, SIDE, 3 * SIDE))]
TWO_TRANSFORMS = 24 * 2 * SIDE**3


def spread_call(slots):
    return call(
        spread_kernel, "spread", slots,
        [SMEM, SMEM, *PIECES, whole(FIELD), whole(FIELD), whole(MATS)],
        [per_slot(FIELD), per_slot(FIELD)],
        [shape(slots, *FIELD), shape(slots, *FIELD)],
        [pltpu.VMEM(EXT, f32)],
        slots * TWO_TRANSFORMS, 9 << 20,
    )


def misfit_call(slots):
    return call(
        misfit_kernel, "misfit", slots,
        [SMEM, SMEM, SMEM, *PIECES, per_slot(FIELD), per_slot((SIDE, SIDE)), whole(MATS)],
        [whole(EXT), per_slot(FIELD)],
        [shape(*EXT), shape(slots, *FIELD)],
        [pltpu.VMEM(EXT, f32)],
        slots * TWO_TRANSFORMS, 12 << 20,
    )


def first_call(slots):
    return call(
        first_kernel, "first", slots,
        [SMEM, SMEM, per_slot(FIELD), per_slot(FIELD), whole(FIELD), whole(FIELD), whole(MATS)],
        [whole(EXT), whole(FIELD)],
        [shape(*EXT), shape(*FIELD)],
        [],
        slots * TWO_TRANSFORMS, 9 << 20,
    )


def order_call(count):
    return call(
        order_kernel, "order", count,
        [per_slot((SIDE, SIDE)), whole((2, SIDE, SIDE))],
        per_slot((SIDE, SIDE)),
        shape(count, SIDE, SIDE),
        [],
        count * 12 * SIDE**3, 4 << 20,
    )


def shifted(block, axis, distance):
    devices = range(lax.axis_size(axis))
    route = [(i - distance, i) for i in devices if i - distance in devices]
    return lax.ppermute(block, axis, route)


def partners(block, axis, stride, count, hop):
    route = []
    for i in range(lax.axis_size(axis)):
        digit = i // stride % count
        j = i + ((digit - hop) % count - digit) * stride
        route.append((i, j))
    return lax.ppermute(block, axis, route)


STAGES = [("band", 1, 2), ("band", 2, 4), ("scan", 1, 4), ("scan", 4, 4)]


def total_over_devices(x):
    for axis, stride, count in STAGES:
        digit = lax.axis_index(axis) // stride % count
        length = x.shape[0] // count
        total = lax.dynamic_slice_in_dim(x, digit * length, length)
        parts = x.reshape(count, length, *x.shape[1:])
        for hop in range(1, count):
            sent = lax.dynamic_index_in_dim(parts, (digit - hop) % count, 0, False)
            total = total + partners(sent, axis, stride, count, hop)
        x = total
    for axis, stride, count in STAGES[::-1]:
        digit = lax.axis_index(axis) // stride % count
        result = jnp.zeros((count, *x.shape), f32)
        result = lax.dynamic_update_index_in_dim(result, x, digit, 0)
        for hop in range(1, count):
            part = partners(x, axis, stride, count, hop)
            result = lax.dynamic_update_index_in_dim(result, part, (digit + hop) % count, 0)
        x = result.reshape(count * x.shape[0], *x.shape[1:])
    return x


def local(objects, probe_field, propagator_phase, patterns, offset_row, offset_column, live_counts):
    width = probe_field.shape[-1]
    tile_rows, tile_cols = objects.shape[1:]
    slots = patterns.shape[2]
    band_last = lax.axis_index("band") == lax.axis_size("band") - 1
    scan_last = lax.axis_index("scan") == lax.axis_size("scan") - 1
    mats = jnp.asarray(tables())
    index = np.arange(SIDE)
    order = np.concatenate([np.arange(0, SIDE, 2), np.arange(1, SIDE, 2)])
    swap = (index[:, None] == order[None, :]).astype(ml_dtypes.bfloat16)
    swap = jnp.asarray(np.stack([swap, swap.T]))

    rows_here = offset_row[0]
    cols_here = offset_column[0]
    live_here = live_counts[0]
    live = jnp.sum((jnp.arange(slots, dtype=jnp.int32) < live_here[0]).astype(f32))

    slices = [objects[:2], objects[2:]]
    exts = []
    for own in slices:
        right = shifted(own[:, :, :width], "scan", -1)
        lower = shifted(jnp.concatenate([own, right], axis=2), "band", -1)
        exts.append((own, right, lower))

    images = jnp.concatenate(
        [patterns[0, 0], jnp.cos(propagator_phase)[None], jnp.sin(propagator_phase)[None]]
    )
    ordered = order_call(slots + 2)(images, swap)
    measured, kernel = ordered[:slots], ordered[slots:]
    probe = probe_field

    for step in range(ITERS):
        last = step == ITERS - 1
        psi, piece = spread_call(slots)(rows_here, cols_here, *exts[0], probe, kernel, mats)
        grad_two, back = misfit_call(slots)(
            rows_here, cols_here, live_here, *exts[1], psi, measured, mats
        )
        grad_one, gprobe = first_call(slots)(
            rows_here, cols_here, back, piece, probe, kernel, mats
        )
        flat = gprobe.reshape(-1, 128)
        if step == 0:
            count_rows = jnp.broadcast_to(live, (flat.shape[0] // 2, 128))
            flat = total_over_devices(jnp.concatenate([flat, count_rows]))
            total = flat[-1, 0]
            summed = flat[: 4 * width].reshape(2, width, width)
        else:
            summed = total_over_devices(flat).reshape(2, width, width)
        moved = probe - probe_rate / total * summed
        power = jnp.sum(moved * moved)
        probe = moved * jnp.sqrt(width * width / (power + power_eps))

        grads = [grad_one, grad_two]
        if not last:
            results = []
            for g, (own, right, lower) in zip(grads, exts):
                from_left = shifted(g[:, :, tile_cols:], "scan", 1)
                from_right = shifted(g[:, :, :width], "scan", -1)
                middle = g[:, :, width:tile_cols]
                g = jnp.concatenate(
                    [g[:, :, :width] + from_left, middle, g[:, :, tile_cols:] + from_right], axis=2
                )
                from_above = shifted(g[:, tile_rows:], "band", 1)
                from_below = shifted(g[:, :tile_rows], "band", -1)
                top = g[:, :tile_rows] + from_above
                bottom = g[:, tile_rows:] + from_below
                own = own - object_rate * top[:, :, :tile_cols]
                right = jnp.where(scan_last, 0.0, right - object_rate * top[:, :, tile_cols:])
                bottom = lower - object_rate * bottom
                outside = scan_last & (jnp.arange(3 * width) >= tile_cols)
                lower = jnp.where(band_last | outside, 0.0, bottom)
                results.append((own, right, lower))
            exts = results
        else:
            results = []
            for g, (own, right, lower) in zip(grads, exts):
                from_above = shifted(g[:, tile_rows:], "band", 1)
                top = g[:, :tile_rows] + from_above
                from_left = shifted(top[:, :, tile_cols:], "scan", 1)
                own = own - object_rate * jnp.concatenate(
                    [top[:, :, :width] + from_left, top[:, :, width:tile_cols]], axis=2
                )
                results.append(own)
            objects = jnp.concatenate(results)
    return (objects, probe)


def solution(mesh):
    return jax.shard_map(
        local,
        mesh=mesh,
        in_specs=(
            P(None, "band", "scan"),
            P(),
            P(),
            P("band", "scan", None, None, None),
            P("band", "scan"),
            P("band", "scan"),
            P("band", "scan"),
        ),
        out_specs=(P(None, "band", "scan"), P()),
        check_vma=False,
    )
```

```python
import functools
import math

import jax
import jax.numpy as jnp
import ml_dtypes
import numpy as np
from jax import lax
from jax.experimental import pallas as pl
from jax.experimental.pallas import tpu as pltpu
from jax.sharding import PartitionSpec as P

ITERS = 2
SIDE = 256
HALF = SIDE // 2
TALL = 264
WIDE = 384

object_rate = 0.1
probe_rate = 2.0
power_eps = 1e-06

f32 = jnp.float32
bf16 = jnp.bfloat16


def halves(matrix):
    high = matrix.astype(ml_dtypes.bfloat16)
    low = (matrix - high.astype(np.float64)).astype(ml_dtypes.bfloat16)
    return [high, low]


def tables():
    point = np.arange(HALF)[None, :]
    result = []
    for parity in (0, 1):
        frequency = 2 * np.arange(HALF)[:, None] + parity
        angle = -2.0 * np.pi / SIDE * (frequency * point % SIDE)
        real = np.cos(angle) / math.sqrt(SIDE)
        imag = np.sin(angle) / math.sqrt(SIDE)
        matrix = np.block([[real, -imag], [imag, real]])
        result += halves(matrix) + halves(matrix.T)
    return np.stack(result)


E_HI, E_LO, ET_HI, ET_LO, O_HI, O_LO, OT_HI, OT_LO = range(8)


def dot(a, b):
    return jnp.dot(a, b, preferred_element_type=f32)


def split(x):
    high = x.astype(bf16)
    low = (x - high.astype(f32)).astype(bf16)
    return high, low


def mul_left(m, hi, x):
    high, low = split(x)
    return dot(m[hi], high) + dot(m[hi], low) + dot(m[hi + 1], high)


def mul_right(x, m, hi):
    high, low = split(x)
    return dot(high, m[hi]) + dot(low, m[hi]) + dot(high, m[hi + 1])


def rows(*parts):
    return jnp.concatenate(parts, axis=0)


def cols(*parts):
    return jnp.concatenate(parts, axis=1)


def forward(re, im, m):
    even = mul_left(m, E_HI, rows(re[:HALF] + re[HALF:], im[:HALF] + im[HALF:]))
    odd = mul_left(m, O_HI, rows(re[:HALF] - re[HALF:], im[:HALF] - im[HALF:]))
    re = rows(even[:HALF], odd[:HALF])
    im = rows(even[HALF:], odd[HALF:])
    u = mul_right(cols(re[:, :HALF] + re[:, HALF:], im[:, :HALF] + im[:, HALF:]), m, ET_HI)
    v = mul_right(cols(re[:, :HALF] - re[:, HALF:], im[:, :HALF] - im[:, HALF:]), m, OT_HI)
    return u, v


def backward(u, v, m):
    a = mul_right(u, m, E_HI)
    b = mul_right(v, m, O_HI)
    re = cols(a[:, :HALF] + b[:, :HALF], a[:, :HALF] - b[:, :HALF])
    im = cols(a[:, HALF:] + b[:, HALF:], a[:, HALF:] - b[:, HALF:])
    a = mul_left(m, ET_HI, rows(re[:HALF], im[:HALF]))
    b = mul_left(m, OT_HI, rows(re[HALF:], im[HALF:]))
    re = rows(a[:HALF] + b[:HALF], a[:HALF] - b[:HALF])
    im = rows(a[HALF:] + b[HALF:], a[HALF:] - b[HALF:])
    return re, im


def by_kernel(u, h, place, sign):
    re, im = u[:, :HALF], u[:, HALF:]
    hr = h[0, :, place * HALF : (place + 1) * HALF]
    hi = h[1, :, place * HALF : (place + 1) * HALF]
    if sign > 0:
        return cols(hr * re - hi * im, hr * im + hi * re)
    return cols(hr * re + hi * im, hr * im - hi * re)


def window(ext, plane, spot):
    row0, row_rest, col0, col_rest = spot
    slab = ext[plane, pl.ds(row0, TALL), pl.ds(col0, WIDE)]
    slab = pltpu.roll(slab, lax.rem(WIDE - col_rest, WIDE), 1)[:, :SIDE]
    return pltpu.roll(slab, lax.rem(TALL - row_rest, TALL), 0)[:SIDE]


def place(row_ref, col_ref, slot):
    row = row_ref[slot]
    col = col_ref[slot]
    row_rest = lax.rem(row, 8)
    col_rest = lax.rem(col, 128)
    row0 = pl.multiple_of(row - row_rest, 8)
    col0 = pl.multiple_of(col - col_rest, 128)
    return row0, row_rest, col0, col_rest


def join_pieces(ext, scale, own, right, lower):
    tile_rows, tile_cols = own.shape[1:]
    ext[:, :tile_rows, :tile_cols] = own[...]
    ext[:, :tile_rows, tile_cols:] = right[...]
    ext[:, tile_rows:, :] = lower[...]


def join_sides(ext, scale, base, left_top, left_bottom, right_top, right_bottom):
    inside_right, inside_lower = scale[0], scale[1]
    for rows_at, from_left, from_right, factor in (
        (0, left_top, right_top, object_rate),
        (SIDE, left_bottom, right_bottom, object_rate * inside_lower),
    ):
        at = pl.ds(rows_at, SIDE)
        ext[:, at, :SIDE] = base[:, at, :SIDE] - factor * from_left[...]
        ext[:, at, SIDE : 2 * SIDE] = base[:, at, SIDE : 2 * SIDE]
        ext[:, at, 2 * SIDE :] = base[:, at, 2 * SIDE :] - factor * inside_right * from_right[...]


def join_ends(ext, scale, base, from_above, from_below):
    inside_right, inside_lower = scale[0], scale[1]
    for rows_at, come, factor in (
        (0, from_above, object_rate),
        (SIDE, from_below, object_rate * inside_lower),
    ):
        at = pl.ds(rows_at, SIDE)
        ext[:, at, : 2 * SIDE] = base[:, at, : 2 * SIDE] - factor * come[:, :, : 2 * SIDE]
        ext[:, at, 2 * SIDE :] = (
            base[:, at, 2 * SIDE :] - factor * inside_right * come[:, :, 2 * SIDE :]
        )


def spread_kernel(join, count, row_ref, col_ref, scale, *refs):
    slot = pl.program_id(0)
    parts, (probe, h, m, psi, piece, *rest) = refs[:count], refs[count:]
    own, ext = rest if len(rest) == 2 else (None, rest[0])

    @pl.when(slot == 0)
    def _():
        join(ext, scale, *parts)
        if own is not None:
            own[...] = ext[:, : own.shape[1], : own.shape[2]]

    spot = place(row_ref, col_ref, slot)
    ar = window(ext, 0, spot)
    ai = window(ext, 1, spot)
    piece[0, 0] = ar
    piece[0, 1] = ai
    pr, pi = probe[0], probe[1]
    u, v = forward(pr * ar - pi * ai, pr * ai + pi * ar, m)
    re, im = backward(by_kernel(u, h, 0, 1), by_kernel(v, h, 1, 1), m)
    psi[0, 0] = re
    psi[0, 1] = im


def add_window(accum, plane, grad, spot):
    row0, row_rest, col0, col_rest = spot
    tall = rows(grad, jnp.zeros((TALL - SIDE, SIDE), f32))
    tall = pltpu.roll(tall, row_rest, 0)
    wide = cols(tall, jnp.zeros((TALL, WIDE - SIDE), f32))
    wide = pltpu.roll(wide, col_rest, 1)
    accum[plane, pl.ds(row0, TALL), pl.ds(col0, WIDE)] += wide


def misfit_kernel(join, count, row_ref, col_ref, scale, live_ref, *refs):
    slot = pl.program_id(0)
    parts, (psi, pattern, m, back, left, mid, right, *rest) = refs[:count], refs[count:]
    own, ext, accum = rest if len(rest) == 3 else (None, *rest)

    @pl.when(slot == 0)
    def _():
        join(ext, scale, *parts)
        if own is not None:
            own[...] = ext[:, : own.shape[1], : own.shape[2]]
        accum[...] = jnp.zeros_like(accum)

    spot = place(row_ref, col_ref, slot)
    ar = window(ext, 0, spot)
    ai = window(ext, 1, spot)
    sr, si = psi[0, 0], psi[0, 1]
    u, v = forward(sr * ar - si * ai, sr * ai + si * ar, m)
    live = (slot < live_ref[0]).astype(f32)

    def weigh(part, measured):
        re, im = part[:, :HALF], part[:, HALF:]
        weight = (re * re + im * im - measured) * live
        return cols(weight * re, weight * im)

    u = weigh(u, pattern[0, :, :HALF])
    v = weigh(v, pattern[0, :, HALF:])
    re, im = backward(u, v, m)
    back[0, 0] = ar * re + ai * im
    back[0, 1] = ar * im - ai * re
    add_window(accum, 0, sr * re + si * im, spot)
    add_window(accum, 1, sr * im - si * re, spot)

    @pl.when(slot == pl.num_programs(0) - 1)
    def _():
        left[...] = accum[:, :, :SIDE]
        mid[...] = accum[:, :, SIDE : 2 * SIDE]
        right[...] = accum[:, :, 2 * SIDE :]


def first_kernel(
    row_ref, col_ref, live_ref, back, piece, probe, h, m, top, bottom, gprobe, accum
):
    slot = pl.program_id(0)

    @pl.when(slot == 0)
    def _():
        accum[...] = jnp.zeros_like(accum)
        gprobe[: 4 * SIDE] = jnp.zeros((4 * SIDE, HALF), f32)
        if gprobe.shape[0] > 4 * SIDE:
            live = jnp.minimum(live_ref[0], pl.num_programs(0)).astype(f32)
            gprobe[4 * SIDE :] = jnp.full((gprobe.shape[0] - 4 * SIDE, HALF), live)

    spot = place(row_ref, col_ref, slot)
    u, v = forward(back[0, 0], back[0, 1], m)
    re, im = backward(by_kernel(u, h, 0, -1), by_kernel(v, h, 1, -1), m)
    ar, ai = piece[0, 0], piece[0, 1]
    for at, value in enumerate((ar * re + ai * im, ar * im - ai * re)):
        for side in (0, 1):
            part = value[:, side * HALF : (side + 1) * HALF]
            gprobe[(2 * at + side) * SIDE : (2 * at + side + 1) * SIDE] += part
    pr, pi = probe[0], probe[1]
    add_window(accum, 0, pr * re + pi * im, spot)
    add_window(accum, 1, pr * im - pi * re, spot)

    @pl.when(slot == pl.num_programs(0) - 1)
    def _():
        top[...] = accum[:, :SIDE]
        bottom[...] = accum[:, SIDE:]


def picked(value, move):
    total = None
    for _ in range(3):
        part = value.astype(bf16)
        value = value - part.astype(f32)
        moved = move(part)
        total = moved if total is None else total + moved
    return total


def order_kernel(x, swap, out):
    value = picked(x[0], lambda part: dot(part, swap[0]))
    out[0] = picked(value, lambda part: dot(swap[1], part))


SMEM = pl.BlockSpec(memory_space=pltpu.SMEM)


def whole(shape):
    return pl.BlockSpec(shape, lambda i: (0,) * len(shape))


def per_slot(shape):
    return pl.BlockSpec((1,) + shape, lambda i: (i,) + (0,) * len(shape))


def call(kernel, name, slots, in_specs, out_specs, out_shape, scratch, flops, size):
    return pl.pallas_call(
        kernel,
        name=name,
        grid=(slots,),
        in_specs=in_specs,
        out_specs=out_specs,
        out_shape=out_shape,
        scratch_shapes=scratch,
        compiler_params=pltpu.CompilerParams(vmem_limit_bytes=32 * 1024 * 1024),
        cost_estimate=pl.CostEstimate(flops=flops, bytes_accessed=size, transcendentals=0),
    )


def shape(*dims):
    return jax.ShapeDtypeStruct(dims, f32)


FIELD = (2, SIDE, SIDE)
MATS = (8, SIDE, SIDE)
EXT = (2, 2 * SIDE, 3 * SIDE)
OWN = (2, SIDE, 2 * SIDE)
SIDES = (2, 2 * SIDE, SIDE)
ENDS = (2, SIDE, 3 * SIDE)
JOINS = {
    "pieces": (join_pieces, [OWN, FIELD, ENDS]),
    "sides": (join_sides, [EXT, FIELD, FIELD, FIELD, FIELD]),
    "ends": (join_ends, [EXT, ENDS, ENDS]),
}
TWO_TRANSFORMS = 24 * 2 * SIDE**3


def specs(shapes):
    return [whole(dims) for dims in shapes]


def shapes_of(shapes):
    return [shape(*dims) for dims in shapes]


def spread_call(slots, how):
    join, parts = JOINS[how]
    extra = [OWN] if how != "pieces" else []
    return call(
        functools.partial(spread_kernel, join, len(parts)), "spread", slots,
        [SMEM, SMEM, SMEM, *specs(parts), whole(FIELD), whole(FIELD), whole(MATS)],
        [per_slot(FIELD), per_slot(FIELD), *specs(extra)],
        [shape(slots, *FIELD), shape(slots, *FIELD), *shapes_of(extra)],
        [pltpu.VMEM(EXT, f32)],
        slots * TWO_TRANSFORMS, 9 << 20,
    )


def misfit_call(slots, how):
    join, parts = JOINS[how]
    extra = [OWN] if how != "pieces" else []
    return call(
        functools.partial(misfit_kernel, join, len(parts)), "misfit", slots,
        [SMEM, SMEM, SMEM, SMEM, *specs(parts), per_slot(FIELD), per_slot((SIDE, SIDE)), whole(MATS)],
        [per_slot(FIELD), *specs([SIDES] * 3 + extra)],
        [shape(slots, *FIELD), *shapes_of([SIDES] * 3 + extra)],
        [pltpu.VMEM(EXT, f32), pltpu.VMEM(EXT, f32)],
        slots * TWO_TRANSFORMS, 12 << 20,
    )


def first_call(slots, sum_rows):
    return call(
        first_kernel, "first", slots,
        [SMEM, SMEM, SMEM, per_slot(FIELD), per_slot(FIELD), whole(FIELD), whole(FIELD), whole(MATS)],
        specs([ENDS, ENDS, (sum_rows, HALF)]),
        shapes_of([ENDS, ENDS, (sum_rows, HALF)]),
        [pltpu.VMEM(EXT, f32)],
        slots * TWO_TRANSFORMS, 9 << 20,
    )


def order_call(count):
    return call(
        order_kernel, "order", count,
        [per_slot((SIDE, SIDE)), whole((2, SIDE, SIDE))],
        per_slot((SIDE, SIDE)),
        shape(count, SIDE, SIDE),
        [],
        count * 12 * SIDE**3, 4 << 20,
    )


def shifted(block, axis, distance):
    devices = range(lax.axis_size(axis))
    route = [(i - distance, i) for i in devices if i - distance in devices]
    return lax.ppermute(block, axis, route)


def partners(block, axis, stride, count, hop):
    route = []
    for i in range(lax.axis_size(axis)):
        digit = i // stride % count
        j = i + ((digit - hop) % count - digit) * stride
        route.append((i, j))
    return lax.ppermute(block, axis, route)


CORE, Z, X, Y = ("band", 1, 2), ("band", 2, 4), ("scan", 1, 4), ("scan", 4, 4)


def scatter_sum(x, ring):
    axis, stride, count = ring
    digit = lax.axis_index(axis) // stride % count
    parts = x.reshape(count, x.shape[0] // count, *x.shape[1:])
    total = lax.dynamic_index_in_dim(parts, digit, 0, False)
    for hop in range(1, count):
        sent = lax.dynamic_index_in_dim(parts, (digit - hop) % count, 0, False)
        total = total + partners(sent, axis, stride, count, hop)
    return total


def gather(x, ring):
    axis, stride, count = ring
    digit = lax.axis_index(axis) // stride % count
    result = jnp.zeros((count, *x.shape), f32)
    result = lax.dynamic_update_index_in_dim(result, x, digit, 0)
    for hop in range(1, count):
        part = partners(x, axis, stride, count, hop)
        result = lax.dynamic_update_index_in_dim(result, part, (digit + hop) % count, 0)
    return result.reshape(count * x.shape[0], *x.shape[1:])


def ring_sum(x, ring):
    axis, stride, count = ring
    one, two, three = (partners(x, axis, stride, count, hop) for hop in (1, 2, 3))
    return (x + two) + (one + three)


def after(value, *others):
    return lax.optimization_barrier((value, *others))[0]


def side_by_side(*parts):
    return jnp.concatenate(parts, axis=2)


def local(objects, probe_field, propagator_phase, patterns, offset_row, offset_column, live_counts):
    width = probe_field.shape[-1]
    tile_rows, tile_cols = objects.shape[1:]
    slots = patterns.shape[2]
    inside_lower = (lax.axis_index("band") < lax.axis_size("band") - 1).astype(f32)
    inside_right = (lax.axis_index("scan") < lax.axis_size("scan") - 1).astype(f32)
    scale = jnp.stack([inside_right, inside_lower])
    mats = jnp.asarray(tables())
    index = np.arange(SIDE)
    order = np.concatenate([np.arange(0, SIDE, 2), np.arange(1, SIDE, 2)])
    swap = (index[:, None] == order[None, :]).astype(ml_dtypes.bfloat16)
    swap = jnp.asarray(np.stack([swap, swap.T]))

    spots = (offset_row[0], offset_column[0], scale)
    live_here = live_counts[0]

    own_one, own_two = objects[:2], objects[2:]
    right_one = shifted(own_one[:, :, :width], "scan", -1)
    lower_two = shifted(own_two, "band", -1)
    lower_one = shifted(side_by_side(own_one, right_one), "band", -1)
    side_two = jnp.concatenate([own_two[:, :, :width], lower_two[:, :, :width]], axis=1)
    side_two = shifted(side_two, "scan", -1)

    images = jnp.concatenate(
        [patterns[0, 0], jnp.cos(propagator_phase)[None], jnp.sin(propagator_phase)[None]]
    )
    ordered = order_call(slots + 2)(images, swap)
    measured, kernel = ordered[:slots], ordered[slots:]
    probe = probe_field

    def moved_probe(probe, summed, total):
        halves_of = summed.reshape(2, 2, width, width // 2)
        summed = side_by_side(halves_of[:, 0], halves_of[:, 1])
        moved = probe - probe_rate / total * summed
        power = jnp.sum(moved * moved)
        return moved * jnp.sqrt(width * width / (power + power_eps))

    def base_of(own, right, lower, top, bottom):
        rate = object_rate
        upper = side_by_side(
            own - rate * top[:, :, :tile_cols],
            right - rate * inside_right * top[:, :, tile_cols:],
        )
        column = jnp.where(jnp.arange(3 * width) < tile_cols, 1.0, inside_right)
        return jnp.concatenate([upper, lower - (rate * inside_lower) * column * bottom], axis=1)

    psi, piece = spread_call(slots, "pieces")(
        *spots, own_one, right_one, lower_one, probe, kernel, mats
    )
    side_two, lower_two = after(side_two, psi), after(lower_two, psi)
    right_two = side_two[:, :tile_rows]
    lower_two = side_by_side(lower_two, side_two[:, tile_rows:])
    back, left, middle, right = misfit_call(slots, "pieces")(
        *spots, live_here, own_two, right_two, lower_two, psi, measured, mats
    )
    two_from_left = shifted(right, "scan", 1)
    two_from_right = shifted(left, "scan", -1)
    top, bottom, gprobe = first_call(slots, 4 * SIDE + 64)(
        *spots[:2], live_here, back, piece, probe, kernel, mats
    )
    one_from_above = shifted(bottom, "band", 1)
    one_from_below = shifted(top, "band", -1)

    share = scatter_sum(gprobe, CORE)
    share = scatter_sum(share, Y)
    share, two_from_left, two_from_right, one_from_above, one_from_below = (
        lax.optimization_barrier(
            (share, two_from_left, two_from_right, one_from_above, one_from_below)
        )
    )
    share = ring_sum(share, X)

    top, bottom = top + one_from_above, bottom + one_from_below
    one_from_left, one_from_right = [], []
    for part in (top, bottom):
        one_from_left.append(shifted(after(part[:, :, tile_cols:], share), "scan", 1))
        one_from_right.append(shifted(after(part[:, :, :width], share), "scan", -1))

    share = ring_sum(share, Z)

    left, right = left + two_from_left, right + two_from_right
    two_top = side_by_side(left[:, :tile_rows], middle[:, :tile_rows], right[:, :tile_rows])
    two_bottom = side_by_side(left[:, tile_rows:], middle[:, tile_rows:], right[:, tile_rows:])
    two_from_above = shifted(after(two_bottom, share), "band", 1)
    two_from_below = shifted(after(two_top, share), "band", -1)

    share, one_from_left[0], one_from_right[0] = lax.optimization_barrier(
        (share, one_from_left[0], one_from_right[0])
    )
    share = gather(share, Y)
    share, one_from_left[1], one_from_right[1] = lax.optimization_barrier(
        (share, one_from_left[1], one_from_right[1])
    )
    both = gather(share, CORE)
    total = both[-1, 0]
    probe = moved_probe(probe, both[: 4 * width], total)
    base_one = base_of(own_one, right_one, lower_one, top, bottom)
    base_two = base_of(own_two, right_two, lower_two, two_top, two_bottom)

    psi, piece, own_one = spread_call(slots, "sides")(
        *spots, base_one, *one_from_left, *one_from_right, probe, kernel, mats
    )
    back, left, middle, right, own_two = misfit_call(slots, "ends")(
        *spots, live_here, base_two, two_from_above, two_from_below, psi, measured, mats
    )
    two_from_left = shifted(right, "scan", 1)
    top, bottom, gprobe = first_call(slots, 4 * SIDE)(
        *spots[:2], live_here, back, piece, probe, kernel, mats
    )
    one_from_above = shifted(bottom, "band", 1)
    share = scatter_sum(gprobe, CORE)
    share = scatter_sum(share, Y)
    share, one_from_above = lax.optimization_barrier((share, one_from_above))
    share = ring_sum(share, Z)
    share, two_from_left = lax.optimization_barrier((share, two_from_left))
    left = left + two_from_left
    two_bottom = side_by_side(left[:, tile_rows:], middle[:, tile_rows:])
    two_from_above = shifted(after(two_bottom, share), "band", 1)
    share = ring_sum(share, X)
    top = top + one_from_above
    one_from_left = shifted(after(top[:, :, tile_cols:], share), "scan", 1)
    share, two_from_above = lax.optimization_barrier((share, two_from_above))
    share = gather(share, Y)
    share, one_from_left = lax.optimization_barrier((share, one_from_left))
    probe = moved_probe(probe, gather(share, CORE), total)

    own_one = own_one - object_rate * side_by_side(
        top[:, :, :width] + one_from_left, top[:, :, width:tile_cols]
    )
    own_two = own_two - object_rate * (
        side_by_side(left[:, :tile_rows], middle[:, :tile_rows]) + two_from_above
    )
    return (jnp.concatenate([own_one, own_two]), probe)


def solution(mesh):
    return jax.shard_map(
        local,
        mesh=mesh,
        in_specs=(
            P(None, "band", "scan"),
            P(),
            P(),
            P("band", "scan", None, None, None),
            P("band", "scan"),
            P("band", "scan"),
            P("band", "scan"),
        ),
        out_specs=(P(None, "band", "scan"), P()),
        check_vma=False,
    )
```

```python
import functools
import math

import jax
import jax.numpy as jnp
import ml_dtypes
import numpy as np
from jax import lax
from jax.experimental import pallas as pl
from jax.experimental.pallas import tpu as pltpu
from jax.sharding import PartitionSpec as P

ITERS = 2
SIDE = 256
HALF = SIDE // 2
TALL = 264
WIDE = 384

object_rate = 0.1
probe_rate = 2.0
power_eps = 1e-06

f32 = jnp.float32
bf16 = jnp.bfloat16


def halves(matrix):
    high = matrix.astype(ml_dtypes.bfloat16)
    low = (matrix - high.astype(np.float64)).astype(ml_dtypes.bfloat16)
    return [high, low]


def tables():
    point = np.arange(HALF)[None, :]
    result = []
    for parity in (0, 1):
        frequency = 2 * np.arange(HALF)[:, None] + parity
        angle = -2.0 * np.pi / SIDE * (frequency * point % SIDE)
        real = np.cos(angle) / math.sqrt(SIDE)
        imag = np.sin(angle) / math.sqrt(SIDE)
        matrix = np.block([[real, -imag], [imag, real]])
        result += halves(matrix) + halves(matrix.T)
    return np.stack(result)


E_HI, E_LO, ET_HI, ET_LO, O_HI, O_LO, OT_HI, OT_LO = range(8)


def dot(a, b):
    return jnp.dot(a, b, preferred_element_type=f32)


def split(x):
    high = x.astype(bf16)
    low = (x - high.astype(f32)).astype(bf16)
    return high, low


def mul_left(m, hi, x):
    high, low = split(x)
    return dot(m[hi], high) + dot(m[hi], low) + dot(m[hi + 1], high)


def mul_right(x, m, hi):
    high, low = split(x)
    return dot(high, m[hi]) + dot(low, m[hi]) + dot(high, m[hi + 1])


def rows(*parts):
    return jnp.concatenate(parts, axis=0)


def cols(*parts):
    return jnp.concatenate(parts, axis=1)


def forward(re, im, m):
    even = mul_left(m, E_HI, rows(re[:HALF] + re[HALF:], im[:HALF] + im[HALF:]))
    odd = mul_left(m, O_HI, rows(re[:HALF] - re[HALF:], im[:HALF] - im[HALF:]))
    re = rows(even[:HALF], odd[:HALF])
    im = rows(even[HALF:], odd[HALF:])
    u = mul_right(cols(re[:, :HALF] + re[:, HALF:], im[:, :HALF] + im[:, HALF:]), m, ET_HI)
    v = mul_right(cols(re[:, :HALF] - re[:, HALF:], im[:, :HALF] - im[:, HALF:]), m, OT_HI)
    return u, v


def backward(u, v, m):
    a = mul_right(u, m, E_HI)
    b = mul_right(v, m, O_HI)
    re = cols(a[:, :HALF] + b[:, :HALF], a[:, :HALF] - b[:, :HALF])
    im = cols(a[:, HALF:] + b[:, HALF:], a[:, HALF:] - b[:, HALF:])
    a = mul_left(m, ET_HI, rows(re[:HALF], im[:HALF]))
    b = mul_left(m, OT_HI, rows(re[HALF:], im[HALF:]))
    re = rows(a[:HALF] + b[:HALF], a[:HALF] - b[:HALF])
    im = rows(a[HALF:] + b[HALF:], a[HALF:] - b[HALF:])
    return re, im


def by_kernel(u, h, place, sign):
    re, im = u[:, :HALF], u[:, HALF:]
    hr = h[0, :, place * HALF : (place + 1) * HALF]
    hi = h[1, :, place * HALF : (place + 1) * HALF]
    if sign > 0:
        return cols(hr * re - hi * im, hr * im + hi * re)
    return cols(hr * re + hi * im, hr * im - hi * re)


def window(ext, plane, spot):
    row0, row_rest, col0, col_rest = spot
    slab = ext[plane, pl.ds(row0, TALL), pl.ds(col0, WIDE)]
    slab = pltpu.roll(slab, lax.rem(WIDE - col_rest, WIDE), 1)[:, :SIDE]
    return pltpu.roll(slab, lax.rem(TALL - row_rest, TALL), 0)[:SIDE]


def place(row_ref, col_ref, slot):
    row = row_ref[slot]
    col = col_ref[slot]
    row_rest = lax.rem(row, 8)
    col_rest = lax.rem(col, 128)
    row0 = pl.multiple_of(row - row_rest, 8)
    col0 = pl.multiple_of(col - col_rest, 128)
    return row0, row_rest, col0, col_rest


def join_pieces(ext, scale, own, right, lower):
    tile_rows, tile_cols = own.shape[1:]
    ext[:, :tile_rows, :tile_cols] = own[...]
    ext[:, :tile_rows, tile_cols:] = right[...]
    ext[:, tile_rows:, :] = lower[...]


def join_sides(ext, scale, base, from_left, from_right):
    inside_right, inside_lower = scale[0], scale[1]
    for rows_at, factor in ((0, object_rate), (SIDE, object_rate * inside_lower)):
        at = pl.ds(rows_at, SIDE)
        ext[:, at, :SIDE] = base[:, at, :SIDE] - factor * from_left[:, at]
        ext[:, at, SIDE : 2 * SIDE] = base[:, at, SIDE : 2 * SIDE]
        ext[:, at, 2 * SIDE :] = base[:, at, 2 * SIDE :] - factor * inside_right * from_right[:, at]


def join_ends(ext, scale, base, from_above, from_below):
    inside_right, inside_lower = scale[0], scale[1]
    for rows_at, come, factor in (
        (0, from_above, object_rate),
        (SIDE, from_below, object_rate * inside_lower),
    ):
        at = pl.ds(rows_at, SIDE)
        ext[:, at, : 2 * SIDE] = base[:, at, : 2 * SIDE] - factor * come[:, :, : 2 * SIDE]
        ext[:, at, 2 * SIDE :] = (
            base[:, at, 2 * SIDE :] - factor * inside_right * come[:, :, 2 * SIDE :]
        )


def spread_kernel(join, count, row_ref, col_ref, scale, *refs):
    slot = pl.program_id(0)
    parts, (probe, h, m, psi, piece, *rest) = refs[:count], refs[count:]
    own, ext = rest if len(rest) == 2 else (None, rest[0])

    @pl.when(slot == 0)
    def _():
        join(ext, scale, *parts)
        if own is not None:
            own[...] = ext[:, : own.shape[1], : own.shape[2]]

    spot = place(row_ref, col_ref, slot)
    ar = window(ext, 0, spot)
    ai = window(ext, 1, spot)
    piece[0, 0] = ar
    piece[0, 1] = ai
    pr, pi = probe[0], probe[1]
    u, v = forward(pr * ar - pi * ai, pr * ai + pi * ar, m)
    re, im = backward(by_kernel(u, h, 0, 1), by_kernel(v, h, 1, 1), m)
    psi[0, 0] = re
    psi[0, 1] = im


def add_window(accum, plane, grad, spot):
    row0, row_rest, col0, col_rest = spot
    tall = rows(grad, jnp.zeros((TALL - SIDE, SIDE), f32))
    tall = pltpu.roll(tall, row_rest, 0)
    wide = cols(tall, jnp.zeros((TALL, WIDE - SIDE), f32))
    wide = pltpu.roll(wide, col_rest, 1)
    accum[plane, pl.ds(row0, TALL), pl.ds(col0, WIDE)] += wide


def misfit_kernel(join, count, row_ref, col_ref, scale, live_ref, *refs):
    slot = pl.program_id(0)
    parts, (psi, pattern, m, back, left, mid, right, *rest) = refs[:count], refs[count:]
    own, ext, accum = rest if len(rest) == 3 else (None, *rest)

    @pl.when(slot == 0)
    def _():
        join(ext, scale, *parts)
        if own is not None:
            own[...] = ext[:, : own.shape[1], : own.shape[2]]
        accum[...] = jnp.zeros_like(accum)

    spot = place(row_ref, col_ref, slot)
    ar = window(ext, 0, spot)
    ai = window(ext, 1, spot)
    sr, si = psi[0, 0], psi[0, 1]
    u, v = forward(sr * ar - si * ai, sr * ai + si * ar, m)
    live = (slot < live_ref[0]).astype(f32)

    def weigh(part, measured):
        re, im = part[:, :HALF], part[:, HALF:]
        weight = (re * re + im * im - measured) * live
        return cols(weight * re, weight * im)

    u = weigh(u, pattern[0, :, :HALF])
    v = weigh(v, pattern[0, :, HALF:])
    re, im = backward(u, v, m)
    back[0, 0] = ar * re + ai * im
    back[0, 1] = ar * im - ai * re
    add_window(accum, 0, sr * re + si * im, spot)
    add_window(accum, 1, sr * im - si * re, spot)

    @pl.when(slot == pl.num_programs(0) - 1)
    def _():
        left[...] = accum[:, :, :SIDE]
        mid[...] = accum[:, :, SIDE : 2 * SIDE]
        right[...] = accum[:, :, 2 * SIDE :]


def first_kernel(
    row_ref, col_ref, live_ref, back, piece, probe, h, m, top, bottom, gprobe, accum
):
    slot = pl.program_id(0)

    @pl.when(slot == 0)
    def _():
        accum[...] = jnp.zeros_like(accum)
        gprobe[: 4 * SIDE] = jnp.zeros((4 * SIDE, HALF), f32)
        if gprobe.shape[0] > 4 * SIDE:
            live = jnp.minimum(live_ref[0], pl.num_programs(0)).astype(f32)
            gprobe[4 * SIDE :] = jnp.full((gprobe.shape[0] - 4 * SIDE, HALF), live)

    spot = place(row_ref, col_ref, slot)
    u, v = forward(back[0, 0], back[0, 1], m)
    re, im = backward(by_kernel(u, h, 0, -1), by_kernel(v, h, 1, -1), m)
    ar, ai = piece[0, 0], piece[0, 1]
    for at, value in enumerate((ar * re + ai * im, ar * im - ai * re)):
        for side in (0, 1):
            part = value[:, side * HALF : (side + 1) * HALF]
            gprobe[(2 * at + side) * SIDE : (2 * at + side + 1) * SIDE] += part
    pr, pi = probe[0], probe[1]
    add_window(accum, 0, pr * re + pi * im, spot)
    add_window(accum, 1, pr * im - pi * re, spot)

    @pl.when(slot == pl.num_programs(0) - 1)
    def _():
        top[...] = accum[:, :SIDE]
        bottom[...] = accum[:, SIDE:]


def picked(value, move):
    total = None
    for _ in range(3):
        part = value.astype(bf16)
        value = value - part.astype(f32)
        moved = move(part)
        total = moved if total is None else total + moved
    return total


def order_kernel(x, swap, out):
    value = picked(x[0], lambda part: dot(part, swap[0]))
    out[0] = picked(value, lambda part: dot(swap[1], part))


SMEM = pl.BlockSpec(memory_space=pltpu.SMEM)


def whole(shape):
    return pl.BlockSpec(shape, lambda i: (0,) * len(shape))


def per_slot(shape):
    return pl.BlockSpec((1,) + shape, lambda i: (i,) + (0,) * len(shape))


def call(kernel, name, slots, in_specs, out_specs, out_shape, scratch, flops, size):
    return pl.pallas_call(
        kernel,
        name=name,
        grid=(slots,),
        in_specs=in_specs,
        out_specs=out_specs,
        out_shape=out_shape,
        scratch_shapes=scratch,
        compiler_params=pltpu.CompilerParams(vmem_limit_bytes=32 * 1024 * 1024),
        cost_estimate=pl.CostEstimate(flops=flops, bytes_accessed=size, transcendentals=0),
    )


def shape(*dims):
    return jax.ShapeDtypeStruct(dims, f32)


FIELD = (2, SIDE, SIDE)
MATS = (8, SIDE, SIDE)
EXT = (2, 2 * SIDE, 3 * SIDE)
OWN = (2, SIDE, 2 * SIDE)
SIDES = (2, 2 * SIDE, SIDE)
ENDS = (2, SIDE, 3 * SIDE)
JOINS = {
    "pieces": (join_pieces, [OWN, FIELD, ENDS]),
    "sides": (join_sides, [EXT, SIDES, SIDES]),
    "ends": (join_ends, [EXT, ENDS, ENDS]),
}
TWO_TRANSFORMS = 24 * 2 * SIDE**3


def specs(shapes):
    return [whole(dims) for dims in shapes]


def shapes_of(shapes):
    return [shape(*dims) for dims in shapes]


def spread_call(slots, how):
    join, parts = JOINS[how]
    extra = [OWN] if how != "pieces" else []
    return call(
        functools.partial(spread_kernel, join, len(parts)), "spread", slots,
        [SMEM, SMEM, SMEM, *specs(parts), whole(FIELD), whole(FIELD), whole(MATS)],
        [per_slot(FIELD), per_slot(FIELD), *specs(extra)],
        [shape(slots, *FIELD), shape(slots, *FIELD), *shapes_of(extra)],
        [pltpu.VMEM(EXT, f32)],
        slots * TWO_TRANSFORMS, 9 << 20,
    )


def misfit_call(slots, how):
    join, parts = JOINS[how]
    extra = [OWN] if how != "pieces" else []
    return call(
        functools.partial(misfit_kernel, join, len(parts)), "misfit", slots,
        [SMEM, SMEM, SMEM, SMEM, *specs(parts), per_slot(FIELD), per_slot((SIDE, SIDE)), whole(MATS)],
        [per_slot(FIELD), *specs([SIDES] * 3 + extra)],
        [shape(slots, *FIELD), *shapes_of([SIDES] * 3 + extra)],
        [pltpu.VMEM(EXT, f32), pltpu.VMEM(EXT, f32)],
        slots * TWO_TRANSFORMS, 12 << 20,
    )


def first_call(slots, sum_rows):
    return call(
        first_kernel, "first", slots,
        [SMEM, SMEM, SMEM, per_slot(FIELD), per_slot(FIELD), whole(FIELD), whole(FIELD), whole(MATS)],
        specs([ENDS, ENDS, (sum_rows, HALF)]),
        shapes_of([ENDS, ENDS, (sum_rows, HALF)]),
        [pltpu.VMEM(EXT, f32)],
        slots * TWO_TRANSFORMS, 9 << 20,
    )


def order_call(count):
    return call(
        order_kernel, "order", count,
        [per_slot((SIDE, SIDE)), whole((2, SIDE, SIDE))],
        per_slot((SIDE, SIDE)),
        shape(count, SIDE, SIDE),
        [],
        count * 12 * SIDE**3, 4 << 20,
    )


def shifted(block, axis, distance):
    devices = range(lax.axis_size(axis))
    route = [(i - distance, i) for i in devices if i - distance in devices]
    return lax.ppermute(block, axis, route)


def partners(block, axis, stride, count, hop):
    route = []
    for i in range(lax.axis_size(axis)):
        digit = i // stride % count
        j = i + ((digit - hop) % count - digit) * stride
        route.append((i, j))
    return lax.ppermute(block, axis, route)


CORE, Z, X, Y = ("band", 1, 2), ("band", 2, 4), ("scan", 1, 4), ("scan", 4, 4)


def scatter_sum(x, ring):
    axis, stride, count = ring
    digit = lax.axis_index(axis) // stride % count
    parts = x.reshape(count, x.shape[0] // count, *x.shape[1:])
    total = lax.dynamic_index_in_dim(parts, digit, 0, False)
    for hop in range(1, count):
        sent = lax.dynamic_index_in_dim(parts, (digit - hop) % count, 0, False)
        total = total + partners(sent, axis, stride, count, hop)
    return total


def gather(x, ring):
    axis, stride, count = ring
    digit = lax.axis_index(axis) // stride % count
    result = jnp.zeros((count, *x.shape), f32)
    result = lax.dynamic_update_index_in_dim(result, x, digit, 0)
    for hop in range(1, count):
        part = partners(x, axis, stride, count, hop)
        result = lax.dynamic_update_index_in_dim(result, part, (digit + hop) % count, 0)
    return result.reshape(count * x.shape[0], *x.shape[1:])


def ring_sum(x, ring):
    axis, stride, count = ring
    one, two, three = (partners(x, axis, stride, count, hop) for hop in (1, 2, 3))
    return (x + two) + (one + three)


def after(value, *others):
    return lax.optimization_barrier((value, *others))[0]


def tied(*values):
    return lax.optimization_barrier(values)


def side_by_side(*parts):
    return jnp.concatenate(parts, axis=2)


def local(objects, probe_field, propagator_phase, patterns, offset_row, offset_column, live_counts):
    width = probe_field.shape[-1]
    tile_rows, tile_cols = objects.shape[1:]
    slots = patterns.shape[2]
    inside_lower = (lax.axis_index("band") < lax.axis_size("band") - 1).astype(f32)
    inside_right = (lax.axis_index("scan") < lax.axis_size("scan") - 1).astype(f32)
    scale = jnp.stack([inside_right, inside_lower])
    mats = jnp.asarray(tables())
    index = np.arange(SIDE)
    order = np.concatenate([np.arange(0, SIDE, 2), np.arange(1, SIDE, 2)])
    swap = (index[:, None] == order[None, :]).astype(ml_dtypes.bfloat16)
    swap = jnp.asarray(np.stack([swap, swap.T]))

    spots = (offset_row[0], offset_column[0], scale)
    live_here = live_counts[0]

    own_one, own_two = objects[:2], objects[2:]
    right_one = shifted(own_one[:, :, :width], "scan", -1)
    lower_two = shifted(own_two, "band", -1)
    lower_one = shifted(side_by_side(own_one, right_one), "band", -1)
    side_two = jnp.concatenate([own_two[:, :, :width], lower_two[:, :, :width]], axis=1)
    side_two = shifted(side_two, "scan", -1)

    images = jnp.concatenate(
        [patterns[0, 0], jnp.cos(propagator_phase)[None], jnp.sin(propagator_phase)[None]]
    )
    ordered = order_call(slots + 2)(images, swap)
    measured, kernel = ordered[:slots], ordered[slots:]
    probe = probe_field

    def moved_probe(probe, summed, total):
        halves_of = summed.reshape(2, 2, width, width // 2)
        summed = side_by_side(halves_of[:, 0], halves_of[:, 1])
        moved = probe - probe_rate / total * summed
        power = jnp.sum(moved * moved)
        return moved * jnp.sqrt(width * width / (power + power_eps))

    def base_of(own, right, lower, top, bottom):
        rate = object_rate
        upper = side_by_side(
            own - rate * top[:, :, :tile_cols],
            right - rate * inside_right * top[:, :, tile_cols:],
        )
        column = jnp.where(jnp.arange(3 * width) < tile_cols, 1.0, inside_right)
        return jnp.concatenate([upper, lower - (rate * inside_lower) * column * bottom], axis=1)

    psi, piece = spread_call(slots, "pieces")(
        *spots, own_one, right_one, lower_one, probe, kernel, mats
    )
    side_two, lower_two = after(side_two, psi), after(lower_two, psi)
    right_two = side_two[:, :tile_rows]
    lower_two = side_by_side(lower_two, side_two[:, tile_rows:])
    back, left, middle, right = misfit_call(slots, "pieces")(
        *spots, live_here, own_two, right_two, lower_two, psi, measured, mats
    )
    upper, under = slice(0, tile_rows), slice(tile_rows, 2 * tile_rows)
    two_from_left = shifted(right, "scan", 1)
    two_from_right = shifted(left, "scan", -1)
    top, bottom, gprobe = first_call(slots, 4 * SIDE + 64)(
        *spots[:2], live_here, back, piece, probe, kernel, mats
    )
    one_from_above = shifted(bottom, "band", 1)
    one_from_below = shifted(top, "band", -1)
    share, two_from_left, two_from_right = tied(gprobe, two_from_left, two_from_right)
    share = scatter_sum(share, CORE)
    share = scatter_sum(share, X)
    share, one_from_above, one_from_below = tied(share, one_from_above, one_from_below)
    share = ring_sum(share, Y)
    share = gather(share, X)
    one_left = jnp.concatenate(
        [
            top[:, :, :width] + one_from_above[:, :, :width],
            bottom[:, :, :width] + one_from_below[:, :, :width],
        ],
        axis=1,
    )
    one_right = jnp.concatenate(
        [
            top[:, :, tile_cols:] + one_from_above[:, :, tile_cols:],
            bottom[:, :, tile_cols:] + one_from_below[:, :, tile_cols:],
        ],
        axis=1,
    )
    one_from_left = shifted(after(one_right, share), "scan", 1)
    one_from_right = shifted(after(one_left, share), "scan", -1)
    share = ring_sum(share, Z)
    two_ends = [
        side_by_side(
            left[:, part] + two_from_left[:, part],
            middle[:, part],
            right[:, part] + two_from_right[:, part],
        )
        for part in (upper, under)
    ]
    two_from_above = shifted(after(two_ends[1], share), "band", 1)
    two_from_below = shifted(after(two_ends[0], share), "band", -1)
    share, one_from_left, one_from_right = tied(share, one_from_left, one_from_right)
    both = gather(share, CORE)
    total = both[-1, 0]
    probe = moved_probe(probe, both[: 4 * width], total)
    base_one = base_of(own_one, right_one, lower_one, top + one_from_above, bottom + one_from_below)
    base_two = base_of(own_two, right_two, lower_two, *two_ends)

    psi, piece, own_one = spread_call(slots, "sides")(
        *spots, base_one, one_from_left, one_from_right, probe, kernel, mats
    )
    back, left, middle, right, own_two = misfit_call(slots, "ends")(
        *spots, live_here, base_two, two_from_above, two_from_below, psi, measured, mats
    )
    two_from_left = shifted(right, "scan", 1)
    top, bottom, gprobe = first_call(slots, 4 * SIDE)(
        *spots[:2], live_here, back, piece, probe, kernel, mats
    )
    one_from_above = shifted(bottom, "band", 1)
    share, two_from_left = tied(gprobe, two_from_left)
    share = scatter_sum(share, CORE)
    share = scatter_sum(share, X)
    two_bottom = side_by_side(left[:, under] + two_from_left[:, under], middle[:, under])
    two_from_above = shifted(two_bottom, "band", 1)
    share = ring_sum(share, Y)
    share, one_from_above = tied(share, one_from_above)
    share = gather(share, X)
    one_right = top[:, :, tile_cols:] + one_from_above[:, :, tile_cols:]
    one_from_left = shifted(after(one_right, share), "scan", 1)
    share, two_from_above = tied(share, two_from_above)
    share = ring_sum(share, Z)
    share, one_from_left = tied(share, one_from_left)
    probe = moved_probe(probe, gather(share, CORE), total)
    top = top + one_from_above
    two_top = side_by_side(left[:, upper] + two_from_left[:, upper], middle[:, upper])

    own_one = own_one - object_rate * side_by_side(
        top[:, :, :width] + one_from_left, top[:, :, width:tile_cols]
    )
    own_two = own_two - object_rate * (two_top + two_from_above)
    return (jnp.concatenate([own_one, own_two]), probe)


def solution(mesh):
    return jax.shard_map(
        local,
        mesh=mesh,
        in_specs=(
            P(None, "band", "scan"),
            P(),
            P(),
            P("band", "scan", None, None, None),
            P("band", "scan"),
            P("band", "scan"),
            P("band", "scan"),
        ),
        out_specs=(P(None, "band", "scan"), P()),
        check_vma=False,
    )
```

```python
import functools
import math

import jax
import jax.numpy as jnp
import ml_dtypes
import numpy as np
from jax import lax
from jax.experimental import pallas as pl
from jax.experimental.pallas import tpu as pltpu
from jax.sharding import PartitionSpec as P

ITERS = 2
SIDE = 256
HALF = SIDE // 2
TALL = 264
WIDE = 384

object_rate = 0.1
probe_rate = 2.0
power_eps = 1e-06

f32 = jnp.float32
bf16 = jnp.bfloat16


def halves(matrix):
    high = matrix.astype(ml_dtypes.bfloat16)
    low = (matrix - high.astype(np.float64)).astype(ml_dtypes.bfloat16)
    return [high, low]


def tables():
    point = np.arange(HALF)[None, :]
    result = []
    for parity in (0, 1):
        frequency = 2 * np.arange(HALF)[:, None] + parity
        angle = -2.0 * np.pi / SIDE * (frequency * point % SIDE)
        real = np.cos(angle) / math.sqrt(SIDE)
        imag = np.sin(angle) / math.sqrt(SIDE)
        matrix = np.block([[real, -imag], [imag, real]])
        result += halves(matrix) + halves(matrix.T)
    return np.stack(result)


E_HI, E_LO, ET_HI, ET_LO, O_HI, O_LO, OT_HI, OT_LO = range(8)


def dot(a, b):
    return jnp.dot(a, b, preferred_element_type=f32)


def split(x):
    high = x.astype(bf16)
    low = (x - high.astype(f32)).astype(bf16)
    return high, low


def mul_left(m, hi, x):
    high, low = split(x)
    return dot(m[hi], high) + dot(m[hi], low) + dot(m[hi + 1], high)


def mul_right(x, m, hi):
    high, low = split(x)
    return dot(high, m[hi]) + dot(low, m[hi]) + dot(high, m[hi + 1])


def rows(*parts):
    return jnp.concatenate(parts, axis=0)


def cols(*parts):
    return jnp.concatenate(parts, axis=1)


def forward(re, im, m):
    even = mul_left(m, E_HI, rows(re[:HALF] + re[HALF:], im[:HALF] + im[HALF:]))
    odd = mul_left(m, O_HI, rows(re[:HALF] - re[HALF:], im[:HALF] - im[HALF:]))
    re = rows(even[:HALF], odd[:HALF])
    im = rows(even[HALF:], odd[HALF:])
    u = mul_right(cols(re[:, :HALF] + re[:, HALF:], im[:, :HALF] + im[:, HALF:]), m, ET_HI)
    v = mul_right(cols(re[:, :HALF] - re[:, HALF:], im[:, :HALF] - im[:, HALF:]), m, OT_HI)
    return u, v


def backward(u, v, m):
    a = mul_right(u, m, E_HI)
    b = mul_right(v, m, O_HI)
    re = cols(a[:, :HALF] + b[:, :HALF], a[:, :HALF] - b[:, :HALF])
    im = cols(a[:, HALF:] + b[:, HALF:], a[:, HALF:] - b[:, HALF:])
    a = mul_left(m, ET_HI, rows(re[:HALF], im[:HALF]))
    b = mul_left(m, OT_HI, rows(re[HALF:], im[HALF:]))
    re = rows(a[:HALF] + b[:HALF], a[:HALF] - b[:HALF])
    im = rows(a[HALF:] + b[HALF:], a[HALF:] - b[HALF:])
    return re, im


def by_kernel(u, h, place, sign):
    re, im = u[:, :HALF], u[:, HALF:]
    hr = h[0, :, place * HALF : (place + 1) * HALF]
    hi = h[1, :, place * HALF : (place + 1) * HALF]
    if sign > 0:
        return cols(hr * re - hi * im, hr * im + hi * re)
    return cols(hr * re + hi * im, hr * im - hi * re)


def window(ext, plane, spot):
    row0, row_rest, col0, col_rest = spot
    slab = ext[plane, pl.ds(row0, TALL), pl.ds(col0, WIDE)]
    slab = pltpu.roll(slab, lax.rem(WIDE - col_rest, WIDE), 1)[:, :SIDE]
    return pltpu.roll(slab, lax.rem(TALL - row_rest, TALL), 0)[:SIDE]


def place(row_ref, col_ref, slot):
    row = row_ref[slot]
    col = col_ref[slot]
    row_rest = lax.rem(row, 8)
    col_rest = lax.rem(col, 128)
    row0 = pl.multiple_of(row - row_rest, 8)
    col0 = pl.multiple_of(col - col_rest, 128)
    return row0, row_rest, col0, col_rest


def fetch(copies, sems):
    moves = [pltpu.make_async_copy(src, dst, sems.at[k]) for k, (src, dst) in enumerate(copies)]
    for move in moves:
        move.start()
    return moves


def join_pieces(which, ext, scale, sems, own, right, lower, corner):
    planes = pl.ds(2 * which, 2)
    head, tail = pl.ds(0, SIDE), pl.ds(SIDE, SIDE)
    near, far = pl.ds(0, 2 * SIDE), pl.ds(2 * SIDE, SIDE)
    moves = fetch(
        [
            (own.at[planes], ext.at[:, head, near]),
            (right, ext.at[:, head, far]),
            (lower.at[planes], ext.at[:, tail, near]),
            (corner, ext.at[:, tail, far]),
        ],
        sems,
    )
    for move in moves:
        move.wait()


def join_sides(which, ext, scale, sems, base, from_left, from_right):
    moves = fetch([(base, ext)], sems)
    for move in moves:
        move.wait()
    inside_right, inside_lower = scale[0], scale[1]
    for rows_at, factor in ((0, object_rate), (SIDE, object_rate * inside_lower)):
        at = pl.ds(rows_at, SIDE)
        ext[:, at, :SIDE] -= factor * from_left[:, at]
        ext[:, at, 2 * SIDE :] -= factor * inside_right * from_right[:, at]


def join_ends(which, ext, scale, sems, base, from_above, from_below):
    moves = fetch([(base, ext)], sems)
    for move in moves:
        move.wait()
    inside_right, inside_lower = scale[0], scale[1]
    for rows_at, come, factor in (
        (0, from_above, object_rate),
        (SIDE, from_below, object_rate * inside_lower),
    ):
        at = pl.ds(rows_at, SIDE)
        ext[:, at, : 2 * SIDE] -= factor * come[:, :, : 2 * SIDE]
        ext[:, at, 2 * SIDE :] -= factor * inside_right * come[:, :, 2 * SIDE :]


def spread_kernel(join, count, row_ref, col_ref, scale, *refs):
    slot = pl.program_id(0)
    parts, (probe, h, m, psi, piece, *rest, ext, sems) = refs[:count], refs[count:]
    own = rest[0] if rest else None

    @pl.when(slot == 0)
    def _():
        join(ext, scale, sems, *parts)
        if own is not None:
            own[...] = ext[:, : own.shape[1], : own.shape[2]]

    for k in range(PER):
        spot = place(row_ref, col_ref, slot * PER + k)
        ar = window(ext, 0, spot)
        ai = window(ext, 1, spot)
        piece[k, 0] = ar
        piece[k, 1] = ai
        pr, pi = probe[0], probe[1]
        u, v = forward(pr * ar - pi * ai, pr * ai + pi * ar, m)
        re, im = backward(by_kernel(u, h, 0, 1), by_kernel(v, h, 1, 1), m)
        psi[k, 0] = re
        psi[k, 1] = im


def add_window(accum, plane, grad, spot):
    row0, row_rest, col0, col_rest = spot
    tall = rows(grad, jnp.zeros((TALL - SIDE, SIDE), f32))
    tall = pltpu.roll(tall, row_rest, 0)
    wide = cols(tall, jnp.zeros((TALL, WIDE - SIDE), f32))
    wide = pltpu.roll(wide, col_rest, 1)
    accum[plane, pl.ds(row0, TALL), pl.ds(col0, WIDE)] += wide


def misfit_kernel(join, count, row_ref, col_ref, scale, live_ref, *refs):
    slot = pl.program_id(0)
    parts, (psi, pattern, m, back, *sums, ext, accum, sems) = refs[:count], refs[count:]
    own = sums.pop() if count == 3 else None

    @pl.when(slot == 0)
    def _():
        join(ext, scale, sems, *parts)
        if own is not None:
            own[...] = ext[:, : own.shape[1], : own.shape[2]]
        accum[...] = jnp.zeros_like(accum)

    for k in range(PER):
        spot = place(row_ref, col_ref, slot * PER + k)
        ar = window(ext, 0, spot)
        ai = window(ext, 1, spot)
        sr, si = psi[k, 0], psi[k, 1]
        u, v = forward(sr * ar - si * ai, sr * ai + si * ar, m)
        live = (slot * PER + k < live_ref[0]).astype(f32)

        def weigh(part, measured):
            re, im = part[:, :HALF], part[:, HALF:]
            weight = (re * re + im * im - measured) * live
            return cols(weight * re, weight * im)

        u = weigh(u, pattern[k, :, :HALF])
        v = weigh(v, pattern[k, :, HALF:])
        re, im = backward(u, v, m)
        back[k, 0] = ar * re + ai * im
        back[k, 1] = ar * im - ai * re
        add_window(accum, 0, sr * re + si * im, spot)
        add_window(accum, 1, sr * im - si * re, spot)

    @pl.when(slot == pl.num_programs(0) - 1)
    def _():
        for k, part in enumerate(sums):
            part[...] = accum[:, :, k * SIDE : (k + 1) * SIDE]


def first_kernel(
    row_ref, col_ref, live_ref, back, piece, probe, h, m, top, bottom, gprobe, accum
):
    slot = pl.program_id(0)

    @pl.when(slot == 0)
    def _():
        accum[...] = jnp.zeros_like(accum)
        gprobe[: 4 * SIDE] = jnp.zeros((4 * SIDE, HALF), f32)
        if gprobe.shape[0] > 4 * SIDE:
            live = jnp.minimum(live_ref[0], PER * pl.num_programs(0)).astype(f32)
            gprobe[4 * SIDE :] = jnp.full((gprobe.shape[0] - 4 * SIDE, HALF), live)

    for k in range(PER):
        spot = place(row_ref, col_ref, slot * PER + k)
        u, v = forward(back[k, 0], back[k, 1], m)
        re, im = backward(by_kernel(u, h, 0, -1), by_kernel(v, h, 1, -1), m)
        ar, ai = piece[k, 0], piece[k, 1]
        for at, value in enumerate((ar * re + ai * im, ar * im - ai * re)):
            for side in (0, 1):
                part = value[:, side * HALF : (side + 1) * HALF]
                gprobe[(2 * at + side) * SIDE : (2 * at + side + 1) * SIDE] += part
        pr, pi = probe[0], probe[1]
        add_window(accum, 0, pr * re + pi * im, spot)
        add_window(accum, 1, pr * im - pi * re, spot)

    @pl.when(slot == pl.num_programs(0) - 1)
    def _():
        top[...] = accum[:, :SIDE]
        bottom[...] = accum[:, SIDE:]


def picked(value, move):
    total = None
    for _ in range(3):
        part = value.astype(bf16)
        value = value - part.astype(f32)
        moved = move(part)
        total = moved if total is None else total + moved
    return total


def order_kernel(x, swap, out):
    value = picked(x[0], lambda part: dot(part, swap[0]))
    out[0] = picked(value, lambda part: dot(swap[1], part))


SMEM = pl.BlockSpec(memory_space=pltpu.SMEM)


def whole(shape):
    return pl.BlockSpec(shape, lambda i: (0,) * len(shape))


PER = 4


def per_slot(shape):
    return pl.BlockSpec((PER,) + shape, lambda i: (i,) + (0,) * len(shape))


def call(kernel, name, slots, in_specs, out_specs, out_shape, scratch, flops, size):
    return pl.pallas_call(
        kernel,
        name=name,
        grid=(slots // PER,),
        in_specs=in_specs,
        out_specs=out_specs,
        out_shape=out_shape,
        scratch_shapes=scratch,
        compiler_params=pltpu.CompilerParams(vmem_limit_bytes=24 * 1024 * 1024),
        cost_estimate=pl.CostEstimate(flops=flops, bytes_accessed=size, transcendentals=0),
    )


def shape(*dims):
    return jax.ShapeDtypeStruct(dims, f32)


FIELD = (2, SIDE, SIDE)
MATS = (8, SIDE, SIDE)
EXT = (2, 2 * SIDE, 3 * SIDE)
OWN = (2, SIDE, 2 * SIDE)
SIDES = (2, 2 * SIDE, SIDE)
ENDS = (2, SIDE, 3 * SIDE)
JOINS = {
    "pieces": (join_pieces, [OWN, FIELD, OWN, FIELD]),
    "sides": (join_sides, [EXT, SIDES, SIDES]),
    "ends": (join_ends, [EXT, ENDS, ENDS]),
}
TWO_TRANSFORMS = 24 * 2 * SIDE**3


def specs(shapes):
    return [whole(dims) for dims in shapes]


ANY = pl.BlockSpec(memory_space=pl.ANY)


def part_specs(how, parts):
    return [ANY] * 4 if how == "pieces" else [ANY, *specs(parts[1:])]


def shapes_of(shapes):
    return [shape(*dims) for dims in shapes]


def spread_call(slots, how):
    join, parts = JOINS[how]
    extra = [OWN] if how != "pieces" else []
    return call(
        functools.partial(spread_kernel, functools.partial(join, 0), len(parts)), "spread", slots,
        [SMEM, SMEM, SMEM, *part_specs(how, parts), whole(FIELD), whole(FIELD), whole(MATS)],
        [per_slot(FIELD), per_slot(FIELD), *specs(extra)],
        [shape(slots, *FIELD), shape(slots, *FIELD), *shapes_of(extra)],
        [pltpu.VMEM(EXT, f32), pltpu.SemaphoreType.DMA((4,))],
        slots * TWO_TRANSFORMS, 9 << 20,
    )


def misfit_call(slots, how):
    join, parts = JOINS[how]
    extra = [SIDES] * 3 + ([OWN] if how != "pieces" else [])
    return call(
        functools.partial(misfit_kernel, functools.partial(join, 1), len(parts)), "misfit", slots,
        [SMEM, SMEM, SMEM, SMEM, *part_specs(how, parts), per_slot(FIELD), per_slot((SIDE, SIDE)), whole(MATS)],
        [per_slot(FIELD), *specs(extra)],
        [shape(slots, *FIELD), *shapes_of(extra)],
        [pltpu.VMEM(EXT, f32), pltpu.VMEM(EXT, f32), pltpu.SemaphoreType.DMA((4,))],
        slots * TWO_TRANSFORMS, 12 << 20,
    )


def first_call(slots, sum_rows):
    return call(
        first_kernel, "first", slots,
        [SMEM, SMEM, SMEM, per_slot(FIELD), per_slot(FIELD), whole(FIELD), whole(FIELD), whole(MATS)],
        specs([ENDS, ENDS, (sum_rows, HALF)]),
        shapes_of([ENDS, ENDS, (sum_rows, HALF)]),
        [pltpu.VMEM(EXT, f32)],
        slots * TWO_TRANSFORMS, 9 << 20,
    )


def order_call(count):
    return call(
        order_kernel, "order", count * PER,
        [pl.BlockSpec((1, SIDE, SIDE), lambda i: (i, 0, 0)), whole((2, SIDE, SIDE))],
        pl.BlockSpec((1, SIDE, SIDE), lambda i: (i, 0, 0)),
        shape(count, SIDE, SIDE),
        [],
        count * 12 * SIDE**3, 4 << 20,
    )


def shifted(block, axis, distance):
    devices = range(lax.axis_size(axis))
    route = [(i - distance, i) for i in devices if i - distance in devices]
    return lax.ppermute(block, axis, route)


def partners(block, axis, stride, count, hop):
    route = []
    for i in range(lax.axis_size(axis)):
        digit = i // stride % count
        j = i + ((digit - hop) % count - digit) * stride
        route.append((i, j))
    return lax.ppermute(block, axis, route)


CORE, Z, X, Y = ("band", 1, 2), ("band", 2, 4), ("scan", 1, 4), ("scan", 4, 4)


def scatter_sum(x, ring):
    axis, stride, count = ring
    digit = lax.axis_index(axis) // stride % count
    parts = x.reshape(count, x.shape[0] // count, *x.shape[1:])
    total = lax.dynamic_index_in_dim(parts, digit, 0, False)
    for hop in range(1, count):
        sent = lax.dynamic_index_in_dim(parts, (digit - hop) % count, 0, False)
        total = total + partners(sent, axis, stride, count, hop)
    return total


def gather(x, ring):
    axis, stride, count = ring
    digit = lax.axis_index(axis) // stride % count
    result = jnp.zeros((count, *x.shape), f32)
    result = lax.dynamic_update_index_in_dim(result, x, digit, 0)
    for hop in range(1, count):
        part = partners(x, axis, stride, count, hop)
        result = lax.dynamic_update_index_in_dim(result, part, (digit + hop) % count, 0)
    return result.reshape(count * x.shape[0], *x.shape[1:])


def ring_sum(x, ring):
    axis, stride, count = ring
    one, two, three = (partners(x, axis, stride, count, hop) for hop in (1, 2, 3))
    return (x + two) + (one + three)


def after(value, *others):
    return lax.optimization_barrier((value, *others))[0]


def tied(*values):
    return lax.optimization_barrier(values)


def side_by_side(*parts):
    return jnp.concatenate(parts, axis=2)


def local(objects, probe_field, propagator_phase, patterns, offset_row, offset_column, live_counts):
    width = probe_field.shape[-1]
    tile_rows, tile_cols = objects.shape[1:]
    slots = patterns.shape[2]
    inside_lower = (lax.axis_index("band") < lax.axis_size("band") - 1).astype(f32)
    inside_right = (lax.axis_index("scan") < lax.axis_size("scan") - 1).astype(f32)
    scale = jnp.stack([inside_right, inside_lower])
    mats = jnp.asarray(tables())
    index = np.arange(SIDE)
    order = np.concatenate([np.arange(0, SIDE, 2), np.arange(1, SIDE, 2)])
    swap = (index[:, None] == order[None, :]).astype(ml_dtypes.bfloat16)
    swap = jnp.asarray(np.stack([swap, swap.T]))

    spots = (offset_row[0], offset_column[0], scale)
    live_here = live_counts[0]

    images = jnp.concatenate(
        [patterns[0, 0], jnp.cos(propagator_phase)[None], jnp.sin(propagator_phase)[None]]
    )
    ordered = order_call(slots + 2)(images, swap)
    measured, kernel = ordered[:slots], ordered[slots:]

    lower = shifted(objects, "band", -1)
    right_one = shifted(objects[:2, :, :width], "scan", -1)
    right_two = shifted(objects[2:, :, :width], "scan", -1)
    corner_one = shifted(after(right_one, ordered), "band", -1)
    corner_two = shifted(right_two, "band", -1)
    own_one, own_two = objects[:2], objects[2:]
    lower_one, lower_two = lower[:2], lower[2:]

    probe = probe_field

    def moved_probe(probe, summed, total):
        halves_of = summed.reshape(2, 2, width, width // 2)
        summed = side_by_side(halves_of[:, 0], halves_of[:, 1])
        moved = probe - probe_rate / total * summed
        power = jnp.sum(moved * moved)
        return moved * jnp.sqrt(width * width / (power + power_eps))

    def base_of(own, right, lower, corner, top, bottom):
        rate = object_rate
        upper = side_by_side(
            own - rate * top[:, :, :tile_cols],
            right - (rate * inside_right) * top[:, :, tile_cols:],
        )
        under = side_by_side(
            lower - (rate * inside_lower) * bottom[:, :, :tile_cols],
            corner - (rate * inside_lower * inside_right) * bottom[:, :, tile_cols:],
        )
        return jnp.concatenate([upper, under], axis=1)

    psi, piece = spread_call(slots, "pieces")(
        *spots, objects, right_one, lower, corner_one, probe, kernel, mats
    )
    back, left, middle, right = misfit_call(slots, "pieces")(
        *spots, live_here, objects, right_two, lower, corner_two, psi, measured, mats
    )
    upper, under = slice(0, tile_rows), slice(tile_rows, 2 * tile_rows)
    two_from_left = shifted(right, "scan", 1)
    two_from_right = shifted(left, "scan", -1)
    top, bottom, gprobe = first_call(slots, 4 * SIDE + 64)(
        *spots[:2], live_here, back, piece, probe, kernel, mats
    )
    one_from_above = shifted(bottom, "band", 1)
    one_from_below = shifted(top, "band", -1)
    share, two_from_left, two_from_right = tied(gprobe, two_from_left, two_from_right)
    share = scatter_sum(share, CORE)
    share = scatter_sum(share, X)
    share, one_from_above, one_from_below = tied(share, one_from_above, one_from_below)
    share = ring_sum(share, Y)
    share = ring_sum(share, Z)
    one_left = jnp.concatenate(
        [
            top[:, :, :width] + one_from_above[:, :, :width],
            bottom[:, :, :width] + one_from_below[:, :, :width],
        ],
        axis=1,
    )
    one_right = jnp.concatenate(
        [
            top[:, :, tile_cols:] + one_from_above[:, :, tile_cols:],
            bottom[:, :, tile_cols:] + one_from_below[:, :, tile_cols:],
        ],
        axis=1,
    )
    share, one_left, one_right = tied(share, one_left, one_right)
    share = gather(share, X)
    one_from_left = shifted(after(one_right, share), "scan", 1)
    one_from_right = shifted(after(one_left, share), "scan", -1)
    both = gather(share, CORE)
    total = both[-1, 0]
    left, middle, right, both = tied(left, middle, right, both)
    two_ends = [
        side_by_side(
            left[:, part] + two_from_left[:, part],
            middle[:, part],
            right[:, part] + two_from_right[:, part],
        )
        for part in (upper, under)
    ]
    two_from_above = shifted(two_ends[1], "band", 1)
    two_from_below = shifted(two_ends[0], "band", -1)
    probe = moved_probe(probe, both[: 4 * width], total)
    top, bottom, probe = tied(top, bottom, probe)
    base_one = base_of(
        own_one, right_one, lower_one, corner_one, top + one_from_above, bottom + one_from_below
    )
    base_two = base_of(own_two, right_two, lower_two, corner_two, *two_ends)

    psi, piece, own_one = spread_call(slots, "sides")(
        *spots, base_one, one_from_left, one_from_right, probe, kernel, mats
    )
    back, left, middle, right, own_two = misfit_call(slots, "ends")(
        *spots, live_here, base_two, two_from_above, two_from_below, psi, measured, mats
    )
    two_from_left = shifted(right, "scan", 1)
    top, bottom, gprobe = first_call(slots, 4 * SIDE)(
        *spots[:2], live_here, back, piece, probe, kernel, mats
    )
    one_from_above = shifted(bottom, "band", 1)
    share, two_from_left = tied(gprobe, two_from_left)
    share = scatter_sum(share, CORE)
    share = scatter_sum(share, X)
    share = ring_sum(share, Y)
    share, one_from_above = tied(share, one_from_above)
    one_right = top[:, :, tile_cols:] + one_from_above[:, :, tile_cols:]
    one_from_left = shifted(one_right, "scan", 1)
    share = ring_sum(share, Z)
    two_bottom = side_by_side(left[:, under] + two_from_left[:, under], middle[:, under])
    two_from_above = shifted(after(two_bottom, share), "band", 1)
    share, one_from_left = tied(share, one_from_left)
    share = gather(share, X)
    probe = moved_probe(probe, gather(share, CORE), total)

    change = top[:, :, :tile_cols] + one_from_above[:, :, :tile_cols]
    change = side_by_side(change[:, :, :width] + one_from_left, change[:, :, width:])
    own_one = own_one - object_rate * change
    change = side_by_side(left[:, upper] + two_from_left[:, upper], middle[:, upper])
    own_two = own_two - object_rate * (change + two_from_above)
    return (jnp.concatenate([own_one, own_two]), probe)


def solution(mesh):
    return jax.shard_map(
        local,
        mesh=mesh,
        in_specs=(
            P(None, "band", "scan"),
            P(),
            P(),
            P("band", "scan", None, None, None),
            P("band", "scan"),
            P("band", "scan"),
            P("band", "scan"),
        ),
        out_specs=(P(None, "band", "scan"), P()),
        check_vma=False,
    )
```

```python
import functools
import math

import jax
import jax.numpy as jnp
import ml_dtypes
import numpy as np
from jax import lax
from jax.experimental import pallas as pl
from jax.experimental.pallas import tpu as pltpu
from jax.sharding import PartitionSpec as P

ITERS = 2
SIDE = 256
HALF = SIDE // 2
TALL = 264
WIDE = 384

object_rate = 0.1
probe_rate = 2.0
power_eps = 1e-06

f32 = jnp.float32
bf16 = jnp.bfloat16


def halves(matrix):
    high = matrix.astype(ml_dtypes.bfloat16)
    low = (matrix - high.astype(np.float64)).astype(ml_dtypes.bfloat16)
    return [high, low]


def tables():
    point = np.arange(HALF)[None, :]
    result = []
    for parity in (0, 1):
        frequency = 2 * np.arange(HALF)[:, None] + parity
        angle = -2.0 * np.pi / SIDE * (frequency * point % SIDE)
        real = np.cos(angle) / math.sqrt(SIDE)
        imag = np.sin(angle) / math.sqrt(SIDE)
        matrix = np.block([[real, -imag], [imag, real]])
        result += halves(matrix) + halves(matrix.T)
    return np.stack(result)


E_HI, E_LO, ET_HI, ET_LO, O_HI, O_LO, OT_HI, OT_LO = range(8)


def dot(a, b):
    return jnp.dot(a, b, preferred_element_type=f32)


def split(x):
    high = x.astype(bf16)
    low = (x - high.astype(f32)).astype(bf16)
    return high, low


def mul_left(m, hi, x):
    high, low = split(x)
    return dot(m[hi], high) + dot(m[hi], low) + dot(m[hi + 1], high)


def mul_right(x, m, hi):
    high, low = split(x)
    return dot(high, m[hi]) + dot(low, m[hi]) + dot(high, m[hi + 1])


def rows(*parts):
    return jnp.concatenate(parts, axis=0)


def cols(*parts):
    return jnp.concatenate(parts, axis=1)


def forward(re, im, m):
    even = mul_left(m, E_HI, rows(re[:HALF] + re[HALF:], im[:HALF] + im[HALF:]))
    odd = mul_left(m, O_HI, rows(re[:HALF] - re[HALF:], im[:HALF] - im[HALF:]))
    re = rows(even[:HALF], odd[:HALF])
    im = rows(even[HALF:], odd[HALF:])
    u = mul_right(cols(re[:, :HALF] + re[:, HALF:], im[:, :HALF] + im[:, HALF:]), m, ET_HI)
    v = mul_right(cols(re[:, :HALF] - re[:, HALF:], im[:, :HALF] - im[:, HALF:]), m, OT_HI)
    return u, v


def backward(u, v, m):
    a = mul_right(u, m, E_HI)
    b = mul_right(v, m, O_HI)
    re = cols(a[:, :HALF] + b[:, :HALF], a[:, :HALF] - b[:, :HALF])
    im = cols(a[:, HALF:] + b[:, HALF:], a[:, HALF:] - b[:, HALF:])
    a = mul_left(m, ET_HI, rows(re[:HALF], im[:HALF]))
    b = mul_left(m, OT_HI, rows(re[HALF:], im[HALF:]))
    re = rows(a[:HALF] + b[:HALF], a[:HALF] - b[:HALF])
    im = rows(a[HALF:] + b[HALF:], a[HALF:] - b[HALF:])
    return re, im


def by_kernel(u, h, place, sign):
    re, im = u[:, :HALF], u[:, HALF:]
    hr = h[0, :, place * HALF : (place + 1) * HALF]
    hi = h[1, :, place * HALF : (place + 1) * HALF]
    if sign > 0:
        return cols(hr * re - hi * im, hr * im + hi * re)
    return cols(hr * re + hi * im, hr * im - hi * re)


def window(ext, plane, spot):
    row0, row_rest, col0, col_rest = spot
    slab = ext[plane, pl.ds(row0, TALL), pl.ds(col0, WIDE)]
    slab = pltpu.roll(slab, lax.rem(WIDE - col_rest, WIDE), 1)[:, :SIDE]
    return pltpu.roll(slab, lax.rem(TALL - row_rest, TALL), 0)[:SIDE]


def place(row_ref, col_ref, slot):
    row = row_ref[slot]
    col = col_ref[slot]
    row_rest = lax.rem(row, 8)
    col_rest = lax.rem(col, 128)
    row0 = pl.multiple_of(row - row_rest, 8)
    col0 = pl.multiple_of(col - col_rest, 128)
    return row0, row_rest, col0, col_rest


def fetch(copies, sems):
    moves = [pltpu.make_async_copy(src, dst, sems.at[k]) for k, (src, dst) in enumerate(copies)]
    for move in moves:
        move.start()
    return moves


def join_pieces(which, ext, scale, sems, own, right, lower, corner):
    planes = pl.ds(2 * which, 2)
    head, tail = pl.ds(0, SIDE), pl.ds(SIDE, SIDE)
    near, far = pl.ds(0, 2 * SIDE), pl.ds(2 * SIDE, SIDE)
    moves = fetch(
        [
            (own.at[planes], ext.at[:, head, near]),
            (right, ext.at[:, head, far]),
            (lower.at[planes], ext.at[:, tail, near]),
            (corner, ext.at[:, tail, far]),
        ],
        sems,
    )
    for move in moves:
        move.wait()


def join_first(which, ext, scale, sems, own, right, lower, corner, top, bottom, above, below, left_in, right_in):
    join_pieces(which, ext, scale, sems, own, right, lower, corner)
    inside_right, inside_lower = scale[0], scale[1]
    for rows_at, mine, come, factor in (
        (0, top, above, object_rate),
        (SIDE, bottom, below, object_rate * inside_lower),
    ):
        at = pl.ds(rows_at, SIDE)
        ext[:, at, :SIDE] -= factor * (mine[:, :, :SIDE] + come[:, :, :SIDE] + left_in[:, at])
        ext[:, at, SIDE : 2 * SIDE] -= factor * (
            mine[:, :, SIDE : 2 * SIDE] + come[:, :, SIDE : 2 * SIDE]
        )
        ext[:, at, 2 * SIDE :] -= (factor * inside_right) * (
            mine[:, :, 2 * SIDE :] + come[:, :, 2 * SIDE :] + right_in[:, at]
        )


def join_second(which, ext, scale, sems, own, right, lower, corner, top, bottom, above, below):
    join_pieces(which, ext, scale, sems, own, right, lower, corner)
    inside_right, inside_lower = scale[0], scale[1]
    for rows_at, mine, come, factor in (
        (0, top, above, object_rate),
        (SIDE, bottom, below, object_rate * inside_lower),
    ):
        at = pl.ds(rows_at, SIDE)
        near = slice(0, 2 * SIDE)
        ext[:, at, near] -= factor * (mine[:, :, near] + come[:, :, near])
        ext[:, at, 2 * SIDE :] -= (factor * inside_right) * (
            mine[:, :, 2 * SIDE :] + come[:, :, 2 * SIDE :]
        )


def spread_kernel(join, count, row_ref, col_ref, scale, *refs):
    slot = pl.program_id(0)
    parts, (probe, h, m, psi, piece, *rest, ext, sems) = refs[:count], refs[count:]
    own = rest[0] if rest else None

    @pl.when(slot == 0)
    def _():
        join(ext, scale, sems, *parts)
        if own is not None:
            own[...] = ext[:, : own.shape[1], : own.shape[2]]

    for k in range(PER):
        spot = place(row_ref, col_ref, slot * PER + k)
        ar = window(ext, 0, spot)
        ai = window(ext, 1, spot)
        piece[k, 0] = ar
        piece[k, 1] = ai
        pr, pi = probe[0], probe[1]
        u, v = forward(pr * ar - pi * ai, pr * ai + pi * ar, m)
        re, im = backward(by_kernel(u, h, 0, 1), by_kernel(v, h, 1, 1), m)
        psi[k, 0] = re
        psi[k, 1] = im


def add_window(accum, plane, grad, spot):
    row0, row_rest, col0, col_rest = spot
    tall = rows(grad, jnp.zeros((TALL - SIDE, SIDE), f32))
    tall = pltpu.roll(tall, row_rest, 0)
    wide = cols(tall, jnp.zeros((TALL, WIDE - SIDE), f32))
    wide = pltpu.roll(wide, col_rest, 1)
    accum[plane, pl.ds(row0, TALL), pl.ds(col0, WIDE)] += wide


def misfit_kernel(join, count, row_ref, col_ref, scale, live_ref, *refs):
    slot = pl.program_id(0)
    parts, (psi, pattern, m, back, *sums, ext, accum, sems) = refs[:count], refs[count:]
    own = sums.pop() if count > 4 else None

    @pl.when(slot == 0)
    def _():
        join(ext, scale, sems, *parts)
        if own is not None:
            own[...] = ext[:, : own.shape[1], : own.shape[2]]
        accum[...] = jnp.zeros_like(accum)

    for k in range(PER):
        spot = place(row_ref, col_ref, slot * PER + k)
        ar = window(ext, 0, spot)
        ai = window(ext, 1, spot)
        sr, si = psi[k, 0], psi[k, 1]
        u, v = forward(sr * ar - si * ai, sr * ai + si * ar, m)
        live = (slot * PER + k < live_ref[0]).astype(f32)

        def weigh(part, measured):
            re, im = part[:, :HALF], part[:, HALF:]
            weight = (re * re + im * im - measured) * live
            return cols(weight * re, weight * im)

        u = weigh(u, pattern[k, :, :HALF])
        v = weigh(v, pattern[k, :, HALF:])
        re, im = backward(u, v, m)
        back[k, 0] = ar * re + ai * im
        back[k, 1] = ar * im - ai * re
        add_window(accum, 0, sr * re + si * im, spot)
        add_window(accum, 1, sr * im - si * re, spot)

    @pl.when(slot == pl.num_programs(0) - 1)
    def _():
        for k, part in enumerate(sums):
            part[...] = accum[:, :, k * SIDE : (k + 1) * SIDE]


def first_kernel(
    row_ref, col_ref, live_ref, back, piece, probe, h, m, top, bottom, gprobe, accum
):
    slot = pl.program_id(0)

    @pl.when(slot == 0)
    def _():
        accum[...] = jnp.zeros_like(accum)
        gprobe[: 4 * SIDE] = jnp.zeros((4 * SIDE, HALF), f32)
        if gprobe.shape[0] > 4 * SIDE:
            live = jnp.minimum(live_ref[0], PER * pl.num_programs(0)).astype(f32)
            gprobe[4 * SIDE :] = jnp.full((gprobe.shape[0] - 4 * SIDE, HALF), live)

    for k in range(PER):
        spot = place(row_ref, col_ref, slot * PER + k)
        u, v = forward(back[k, 0], back[k, 1], m)
        re, im = backward(by_kernel(u, h, 0, -1), by_kernel(v, h, 1, -1), m)
        ar, ai = piece[k, 0], piece[k, 1]
        for at, value in enumerate((ar * re + ai * im, ar * im - ai * re)):
            for side in (0, 1):
                part = value[:, side * HALF : (side + 1) * HALF]
                gprobe[(2 * at + side) * SIDE : (2 * at + side + 1) * SIDE] += part
        pr, pi = probe[0], probe[1]
        add_window(accum, 0, pr * re + pi * im, spot)
        add_window(accum, 1, pr * im - pi * re, spot)

    @pl.when(slot == pl.num_programs(0) - 1)
    def _():
        top[...] = accum[:, :SIDE]
        bottom[...] = accum[:, SIDE:]


def picked(value, move):
    total = None
    for _ in range(3):
        part = value.astype(bf16)
        value = value - part.astype(f32)
        moved = move(part)
        total = moved if total is None else total + moved
    return total


def order_kernel(x, swap, out):
    value = picked(x[0], lambda part: dot(part, swap[0]))
    out[0] = picked(value, lambda part: dot(swap[1], part))


SMEM = pl.BlockSpec(memory_space=pltpu.SMEM)


def whole(shape):
    return pl.BlockSpec(
        shape, lambda i: (0,) * len(shape), pipeline_mode=pl.Buffered(buffer_count=1)
    )


PER = 2


def per_slot(shape):
    return pl.BlockSpec((PER,) + shape, lambda i: (i,) + (0,) * len(shape))


def call(kernel, name, slots, in_specs, out_specs, out_shape, scratch, flops, size):
    return pl.pallas_call(
        kernel,
        name=name,
        grid=(slots // PER,),
        in_specs=in_specs,
        out_specs=out_specs,
        out_shape=out_shape,
        scratch_shapes=scratch,
        compiler_params=pltpu.CompilerParams(vmem_limit_bytes=28 * 1024 * 1024),
        cost_estimate=pl.CostEstimate(flops=flops, bytes_accessed=size, transcendentals=0),
    )


def shape(*dims):
    return jax.ShapeDtypeStruct(dims, f32)


FIELD = (2, SIDE, SIDE)
MATS = (8, SIDE, SIDE)
EXT = (2, 2 * SIDE, 3 * SIDE)
OWN = (2, SIDE, 2 * SIDE)
SIDES = (2, 2 * SIDE, SIDE)
ENDS = (2, SIDE, 3 * SIDE)
JOINS = {
    "pieces": (join_pieces, [OWN, FIELD, OWN, FIELD]),
    "sides": (join_first, [OWN, FIELD, OWN, FIELD, ENDS, ENDS, ENDS, ENDS, SIDES, SIDES]),
    "ends": (join_second, [OWN, FIELD, OWN, FIELD, ENDS, ENDS, ENDS, ENDS]),
}
TWO_TRANSFORMS = 24 * 2 * SIDE**3


def specs(shapes):
    return [whole(dims) for dims in shapes]


ANY = pl.BlockSpec(memory_space=pl.ANY)


def part_specs(how, parts):
    return [ANY] * 4 + specs(parts[4:])


def shapes_of(shapes):
    return [shape(*dims) for dims in shapes]


def spread_call(slots, how):
    join, parts = JOINS[how]
    extra = [OWN] if how != "pieces" else []
    return call(
        functools.partial(spread_kernel, functools.partial(join, 0), len(parts)), "spread", slots,
        [SMEM, SMEM, SMEM, *part_specs(how, parts), whole(FIELD), whole(FIELD), whole(MATS)],
        [per_slot(FIELD), per_slot(FIELD), *specs(extra)],
        [shape(slots, *FIELD), shape(slots, *FIELD), *shapes_of(extra)],
        [pltpu.VMEM(EXT, f32), pltpu.SemaphoreType.DMA((4,))],
        slots * TWO_TRANSFORMS, 9 << 20,
    )


def misfit_call(slots, how):
    join, parts = JOINS[how]
    extra = [SIDES] * 3 + ([OWN] if how != "pieces" else [])
    return call(
        functools.partial(misfit_kernel, functools.partial(join, 1), len(parts)), "misfit", slots,
        [SMEM, SMEM, SMEM, SMEM, *part_specs(how, parts), per_slot(FIELD), per_slot((SIDE, SIDE)), whole(MATS)],
        [per_slot(FIELD), *specs(extra)],
        [shape(slots, *FIELD), *shapes_of(extra)],
        [pltpu.VMEM(EXT, f32), pltpu.VMEM(EXT, f32), pltpu.SemaphoreType.DMA((4,))],
        slots * TWO_TRANSFORMS, 12 << 20,
    )


def first_call(slots, sum_rows):
    return call(
        first_kernel, "first", slots,
        [SMEM, SMEM, SMEM, per_slot(FIELD), per_slot(FIELD), whole(FIELD), whole(FIELD), whole(MATS)],
        specs([ENDS, ENDS, (sum_rows, HALF)]),
        shapes_of([ENDS, ENDS, (sum_rows, HALF)]),
        [pltpu.VMEM(EXT, f32)],
        slots * TWO_TRANSFORMS, 9 << 20,
    )


def order_call(count):
    return call(
        order_kernel, "order", count * PER,
        [pl.BlockSpec((1, SIDE, SIDE), lambda i: (i, 0, 0)), whole((2, SIDE, SIDE))],
        pl.BlockSpec((1, SIDE, SIDE), lambda i: (i, 0, 0)),
        shape(count, SIDE, SIDE),
        [],
        count * 12 * SIDE**3, 4 << 20,
    )


def shifted(block, axis, distance):
    devices = range(lax.axis_size(axis))
    route = [(i - distance, i) for i in devices if i - distance in devices]
    return lax.ppermute(block, axis, route)


def partners(block, axis, stride, count, hop):
    route = []
    for i in range(lax.axis_size(axis)):
        digit = i // stride % count
        j = i + ((digit - hop) % count - digit) * stride
        route.append((i, j))
    return lax.ppermute(block, axis, route)


CORE, Z, X, Y = ("band", 1, 2), ("band", 2, 4), ("scan", 1, 4), ("scan", 4, 4)


def scatter_sum(x, ring):
    axis, stride, count = ring
    digit = lax.axis_index(axis) // stride % count
    parts = x.reshape(count, x.shape[0] // count, *x.shape[1:])
    total = lax.dynamic_index_in_dim(parts, digit, 0, False)
    for hop in range(1, count):
        sent = lax.dynamic_index_in_dim(parts, (digit - hop) % count, 0, False)
        total = total + partners(sent, axis, stride, count, hop)
    return total


def gather(x, ring):
    axis, stride, count = ring
    digit = lax.axis_index(axis) // stride % count
    result = jnp.zeros((count, *x.shape), f32)
    result = lax.dynamic_update_index_in_dim(result, x, digit, 0)
    for hop in range(1, count):
        part = partners(x, axis, stride, count, hop)
        result = lax.dynamic_update_index_in_dim(result, part, (digit + hop) % count, 0)
    return result.reshape(count * x.shape[0], *x.shape[1:])


def ring_sum(x, ring):
    axis, stride, count = ring
    one, two, three = (partners(x, axis, stride, count, hop) for hop in (1, 2, 3))
    return (x + two) + (one + three)


def in_order(x):
    parts = x.reshape(X[2], CORE[2], -1, x.shape[1])
    return jnp.swapaxes(parts, 0, 1).reshape(x.shape)


def after(value, *others):
    return lax.optimization_barrier((value, *others))[0]


def tied(*values):
    return lax.optimization_barrier(values)


def side_by_side(*parts):
    return jnp.concatenate(parts, axis=2)


def local(objects, probe_field, propagator_phase, patterns, offset_row, offset_column, live_counts):
    width = probe_field.shape[-1]
    tile_rows, tile_cols = objects.shape[1:]
    slots = patterns.shape[2]
    inside_lower = (lax.axis_index("band") < lax.axis_size("band") - 1).astype(f32)
    inside_right = (lax.axis_index("scan") < lax.axis_size("scan") - 1).astype(f32)
    scale = jnp.stack([inside_right, inside_lower])
    mats = jnp.asarray(tables())
    index = np.arange(SIDE)
    order = np.concatenate([np.arange(0, SIDE, 2), np.arange(1, SIDE, 2)])
    swap = (index[:, None] == order[None, :]).astype(ml_dtypes.bfloat16)
    swap = jnp.asarray(np.stack([swap, swap.T]))

    spots = (offset_row[0], offset_column[0], scale)
    live_here = live_counts[0]

    images = jnp.concatenate(
        [patterns[0, 0], jnp.cos(propagator_phase)[None], jnp.sin(propagator_phase)[None]]
    )
    ordered = order_call(slots + 2)(images, swap)
    measured, kernel = ordered[:slots], ordered[slots:]

    lower = shifted(objects, "band", -1)
    right_one = shifted(objects[:2, :, :width], "scan", -1)
    right_two = shifted(objects[2:, :, :width], "scan", -1)
    corner_one = shifted(after(right_one, ordered), "band", -1)
    corner_two = shifted(right_two, "band", -1)

    probe = probe_field

    def moved_probe(probe, summed, total):
        halves_of = summed.reshape(2, 2, width, width // 2)
        summed = side_by_side(halves_of[:, 0], halves_of[:, 1])
        moved = probe - probe_rate / total * summed
        power = jnp.sum(moved * moved)
        return moved * jnp.sqrt(width * width / (power + power_eps))

    psi, piece = spread_call(slots, "pieces")(
        *spots, objects, right_one, lower, corner_one, probe, kernel, mats
    )
    back, left, middle, right = misfit_call(slots, "pieces")(
        *spots, live_here, objects, right_two, lower, corner_two, psi, measured, mats
    )
    upper, under = slice(0, tile_rows), slice(tile_rows, 2 * tile_rows)
    two_from_left = shifted(right, "scan", 1)
    two_from_right = shifted(left, "scan", -1)
    top, bottom, gprobe = first_call(slots, 4 * SIDE + 64)(
        *spots[:2], live_here, back, piece, probe, kernel, mats
    )
    one_from_above = shifted(bottom, "band", 1)
    one_from_below = shifted(top, "band", -1)
    share, two_from_left, two_from_right = tied(gprobe, two_from_left, two_from_right)
    share = scatter_sum(share, CORE)
    share = scatter_sum(share, X)
    share, one_from_above, one_from_below = tied(share, one_from_above, one_from_below)
    share = ring_sum(share, Y)
    share = ring_sum(share, Z)
    one_left = jnp.concatenate(
        [
            top[:, :, :width] + one_from_above[:, :, :width],
            bottom[:, :, :width] + one_from_below[:, :, :width],
        ],
        axis=1,
    )
    one_right = jnp.concatenate(
        [
            top[:, :, tile_cols:] + one_from_above[:, :, tile_cols:],
            bottom[:, :, tile_cols:] + one_from_below[:, :, tile_cols:],
        ],
        axis=1,
    )
    left, middle, right, zone = tied(left, middle, right, share)
    two_ends = [
        side_by_side(
            left[:, part] + two_from_left[:, part],
            middle[:, part],
            right[:, part] + two_from_right[:, part],
        )
        for part in (upper, under)
    ]
    two_from_above = shifted(two_ends[1], "band", 1)
    two_from_below = shifted(two_ends[0], "band", -1)
    share = gather(share, CORE)
    share, one_left, one_right = tied(share, one_left, one_right)
    share = gather(share, X)
    one_from_left = shifted(after(one_right, share), "scan", 1)
    one_from_right = shifted(after(one_left, share), "scan", -1)
    both = in_order(share)
    total = both[-1, 0]
    probe = moved_probe(probe, both[: 4 * width], total)
    top, bottom = after(top, *two_ends), after(bottom, *two_ends)

    psi, piece, own_one = spread_call(slots, "sides")(
        *spots, objects, right_one, lower, corner_one, top, bottom, one_from_above, one_from_below,
        one_from_left, one_from_right, probe, kernel, mats
    )
    back, left, middle, right, own_two = misfit_call(slots, "ends")(
        *spots, live_here, objects, right_two, lower, corner_two, *two_ends, two_from_above,
        two_from_below, psi, measured, mats
    )
    two_from_left = shifted(right, "scan", 1)
    top, bottom, gprobe = first_call(slots, 4 * SIDE)(
        *spots[:2], live_here, back, piece, probe, kernel, mats
    )
    one_from_above = shifted(bottom, "band", 1)
    share, two_from_left = tied(gprobe, two_from_left)
    share = scatter_sum(share, CORE)
    share = scatter_sum(share, X)
    share = ring_sum(share, Y)
    share, one_from_above = tied(share, one_from_above)
    one_right = top[:, :, tile_cols:] + one_from_above[:, :, tile_cols:]
    one_from_left = shifted(one_right, "scan", 1)
    share = ring_sum(share, Z)
    two_bottom = side_by_side(left[:, under] + two_from_left[:, under], middle[:, under])
    two_from_above = shifted(after(two_bottom, share), "band", 1)
    share = gather(share, CORE)
    share, one_from_left = tied(share, one_from_left)
    share = gather(share, X)
    probe = moved_probe(probe, in_order(share), total)

    change = top[:, :, :tile_cols] + one_from_above[:, :, :tile_cols]
    change = side_by_side(change[:, :, :width] + one_from_left, change[:, :, width:])
    own_one = own_one - object_rate * change
    change = side_by_side(left[:, upper] + two_from_left[:, upper], middle[:, upper])
    own_two = own_two - object_rate * (change + two_from_above)
    return (jnp.concatenate([own_one, own_two]), probe)


def solution(mesh):
    return jax.shard_map(
        local,
        mesh=mesh,
        in_specs=(
            P(None, "band", "scan"),
            P(),
            P(),
            P("band", "scan", None, None, None),
            P("band", "scan"),
            P("band", "scan"),
            P("band", "scan"),
        ),
        out_specs=(P(None, "band", "scan"), P()),
        check_vma=False,
    )
```

```python
import functools
import math

import jax
import jax.numpy as jnp
import ml_dtypes
import numpy as np
from jax import lax
from jax.experimental import pallas as pl
from jax.experimental.pallas import tpu as pltpu
from jax.sharding import PartitionSpec as P

ITERS = 2
SIDE = 256
HALF = SIDE // 2
TALL = 264
WIDE = 384

object_rate = 0.1
probe_rate = 2.0
power_eps = 1e-06

f32 = jnp.float32
bf16 = jnp.bfloat16


def halves(matrix):
    high = matrix.astype(ml_dtypes.bfloat16)
    low = (matrix - high.astype(np.float64)).astype(ml_dtypes.bfloat16)
    return [high, low]


def tables():
    point = np.arange(HALF)[None, :]
    result = []
    for parity in (0, 1):
        frequency = 2 * np.arange(HALF)[:, None] + parity
        angle = -2.0 * np.pi / SIDE * (frequency * point % SIDE)
        real = np.cos(angle) / math.sqrt(SIDE)
        imag = np.sin(angle) / math.sqrt(SIDE)
        matrix = np.block([[real, -imag], [imag, real]])
        result += halves(matrix) + halves(matrix.T)
    return np.stack(result)


E_HI, E_LO, ET_HI, ET_LO, O_HI, O_LO, OT_HI, OT_LO = range(8)


def dot(a, b):
    return jnp.dot(a, b, preferred_element_type=f32)


def split(x):
    high = x.astype(bf16)
    low = (x - high.astype(f32)).astype(bf16)
    return high, low


def mul_left(m, hi, x):
    high, low = split(x)
    return dot(m[hi], high) + dot(m[hi], low) + dot(m[hi + 1], high)


def mul_right(x, m, hi):
    high, low = split(x)
    return dot(high, m[hi]) + dot(low, m[hi]) + dot(high, m[hi + 1])


def rows(*parts):
    return jnp.concatenate(parts, axis=0)


def cols(*parts):
    return jnp.concatenate(parts, axis=1)


def forward(re, im, m):
    even = mul_left(m, E_HI, rows(re[:HALF] + re[HALF:], im[:HALF] + im[HALF:]))
    odd = mul_left(m, O_HI, rows(re[:HALF] - re[HALF:], im[:HALF] - im[HALF:]))
    re = rows(even[:HALF], odd[:HALF])
    im = rows(even[HALF:], odd[HALF:])
    u = mul_right(cols(re[:, :HALF] + re[:, HALF:], im[:, :HALF] + im[:, HALF:]), m, ET_HI)
    v = mul_right(cols(re[:, :HALF] - re[:, HALF:], im[:, :HALF] - im[:, HALF:]), m, OT_HI)
    return u, v


def backward(u, v, m):
    a = mul_right(u, m, E_HI)
    b = mul_right(v, m, O_HI)
    re = cols(a[:, :HALF] + b[:, :HALF], a[:, :HALF] - b[:, :HALF])
    im = cols(a[:, HALF:] + b[:, HALF:], a[:, HALF:] - b[:, HALF:])
    a = mul_left(m, ET_HI, rows(re[:HALF], im[:HALF]))
    b = mul_left(m, OT_HI, rows(re[HALF:], im[HALF:]))
    re = rows(a[:HALF] + b[:HALF], a[:HALF] - b[:HALF])
    im = rows(a[HALF:] + b[HALF:], a[HALF:] - b[HALF:])
    return re, im


def by_kernel(u, h, place, sign):
    re, im = u[:, :HALF], u[:, HALF:]
    hr = h[0, :, place * HALF : (place + 1) * HALF]
    hi = h[1, :, place * HALF : (place + 1) * HALF]
    if sign > 0:
        return cols(hr * re - hi * im, hr * im + hi * re)
    return cols(hr * re + hi * im, hr * im - hi * re)


def window(ext, plane, spot):
    row0, row_rest, col0, col_rest = spot
    slab = ext[plane, pl.ds(row0, TALL), pl.ds(col0, WIDE)]
    slab = pltpu.roll(slab, lax.rem(WIDE - col_rest, WIDE), 1)[:, :SIDE]
    return pltpu.roll(slab, lax.rem(TALL - row_rest, TALL), 0)[:SIDE]


def place(row_ref, col_ref, slot):
    row = row_ref[slot]
    col = col_ref[slot]
    row_rest = lax.rem(row, 8)
    col_rest = lax.rem(col, 128)
    row0 = pl.multiple_of(row - row_rest, 8)
    col0 = pl.multiple_of(col - col_rest, 128)
    return row0, row_rest, col0, col_rest


def join_pieces(ext, scale, own, right, lower, corner):
    tile_rows, tile_cols = own.shape[1:]
    ext[:, :tile_rows, :tile_cols] = own[...]
    ext[:, :tile_rows, tile_cols:] = right[...]
    ext[:, tile_rows:, :tile_cols] = lower[...]
    ext[:, tile_rows:, tile_cols:] = corner[...]


def join_sides(ext, scale, base, from_left, from_right):
    inside_right, inside_lower = scale[0], scale[1]
    for rows_at, factor in ((0, object_rate), (SIDE, object_rate * inside_lower)):
        at = pl.ds(rows_at, SIDE)
        ext[:, at, :SIDE] = base[:, at, :SIDE] - factor * from_left[:, at]
        ext[:, at, SIDE : 2 * SIDE] = base[:, at, SIDE : 2 * SIDE]
        ext[:, at, 2 * SIDE :] = base[:, at, 2 * SIDE :] - factor * inside_right * from_right[:, at]


def join_ends(ext, scale, base, from_above, from_below):
    inside_right, inside_lower = scale[0], scale[1]
    for rows_at, come, factor in (
        (0, from_above, object_rate),
        (SIDE, from_below, object_rate * inside_lower),
    ):
        at = pl.ds(rows_at, SIDE)
        ext[:, at, : 2 * SIDE] = base[:, at, : 2 * SIDE] - factor * come[:, :, : 2 * SIDE]
        ext[:, at, 2 * SIDE :] = (
            base[:, at, 2 * SIDE :] - factor * inside_right * come[:, :, 2 * SIDE :]
        )


def spread_kernel(join, count, row_ref, col_ref, scale, *refs):
    slot = pl.program_id(0)
    parts, (probe, h, m, psi, piece, *rest) = refs[:count], refs[count:]
    own, ext = rest if len(rest) == 2 else (None, rest[0])

    @pl.when(slot == 0)
    def _():
        join(ext, scale, *parts)
        if own is not None:
            own[...] = ext[:, : own.shape[1], : own.shape[2]]

    for k in range(PER):
        spot = place(row_ref, col_ref, slot * PER + k)
        ar = window(ext, 0, spot)
        ai = window(ext, 1, spot)
        piece[k, 0] = ar
        piece[k, 1] = ai
        pr, pi = probe[0], probe[1]
        u, v = forward(pr * ar - pi * ai, pr * ai + pi * ar, m)
        re, im = backward(by_kernel(u, h, 0, 1), by_kernel(v, h, 1, 1), m)
        psi[k, 0] = re
        psi[k, 1] = im


def add_window(accum, plane, grad, spot):
    row0, row_rest, col0, col_rest = spot
    tall = rows(grad, jnp.zeros((TALL - SIDE, SIDE), f32))
    tall = pltpu.roll(tall, row_rest, 0)
    wide = cols(tall, jnp.zeros((TALL, WIDE - SIDE), f32))
    wide = pltpu.roll(wide, col_rest, 1)
    accum[plane, pl.ds(row0, TALL), pl.ds(col0, WIDE)] += wide


def misfit_kernel(join, count, row_ref, col_ref, scale, live_ref, *refs):
    slot = pl.program_id(0)
    parts, (psi, pattern, m, back, left, mid, right, *rest) = refs[:count], refs[count:]
    own, ext, accum = rest if len(rest) == 3 else (None, *rest)

    @pl.when(slot == 0)
    def _():
        join(ext, scale, *parts)
        if own is not None:
            own[...] = ext[:, : own.shape[1], : own.shape[2]]
        accum[...] = jnp.zeros_like(accum)

    for k in range(PER):
        spot = place(row_ref, col_ref, slot * PER + k)
        ar = window(ext, 0, spot)
        ai = window(ext, 1, spot)
        sr, si = psi[k, 0], psi[k, 1]
        u, v = forward(sr * ar - si * ai, sr * ai + si * ar, m)
        live = (slot * PER + k < live_ref[0]).astype(f32)

        def weigh(part, measured):
            re, im = part[:, :HALF], part[:, HALF:]
            weight = (re * re + im * im - measured) * live
            return cols(weight * re, weight * im)

        u = weigh(u, pattern[k, :, :HALF])
        v = weigh(v, pattern[k, :, HALF:])
        re, im = backward(u, v, m)
        back[k, 0] = ar * re + ai * im
        back[k, 1] = ar * im - ai * re
        add_window(accum, 0, sr * re + si * im, spot)
        add_window(accum, 1, sr * im - si * re, spot)

    @pl.when(slot == pl.num_programs(0) - 1)
    def _():
        left[...] = accum[:, :, :SIDE]
        mid[...] = accum[:, :, SIDE : 2 * SIDE]
        right[...] = accum[:, :, 2 * SIDE :]


def first_kernel(
    row_ref, col_ref, live_ref, back, piece, probe, h, m, top, bottom, gprobe, accum
):
    slot = pl.program_id(0)

    @pl.when(slot == 0)
    def _():
        accum[...] = jnp.zeros_like(accum)
        gprobe[: 4 * SIDE] = jnp.zeros((4 * SIDE, HALF), f32)
        if gprobe.shape[0] > 4 * SIDE:
            live = jnp.minimum(live_ref[0], PER * pl.num_programs(0)).astype(f32)
            gprobe[4 * SIDE :] = jnp.full((gprobe.shape[0] - 4 * SIDE, HALF), live)

    for k in range(PER):
        spot = place(row_ref, col_ref, slot * PER + k)
        u, v = forward(back[k, 0], back[k, 1], m)
        re, im = backward(by_kernel(u, h, 0, -1), by_kernel(v, h, 1, -1), m)
        ar, ai = piece[k, 0], piece[k, 1]
        for at, value in enumerate((ar * re + ai * im, ar * im - ai * re)):
            for side in (0, 1):
                part = value[:, side * HALF : (side + 1) * HALF]
                gprobe[(2 * at + side) * SIDE : (2 * at + side + 1) * SIDE] += part
        pr, pi = probe[0], probe[1]
        add_window(accum, 0, pr * re + pi * im, spot)
        add_window(accum, 1, pr * im - pi * re, spot)

    @pl.when(slot == pl.num_programs(0) - 1)
    def _():
        top[...] = accum[:, :SIDE]
        bottom[...] = accum[:, SIDE:]


def picked(value, move):
    total = None
    for _ in range(3):
        part = value.astype(bf16)
        value = value - part.astype(f32)
        moved = move(part)
        total = moved if total is None else total + moved
    return total


def order_kernel(x, swap, out):
    value = picked(x[0], lambda part: dot(part, swap[0]))
    out[0] = picked(value, lambda part: dot(swap[1], part))


SMEM = pl.BlockSpec(memory_space=pltpu.SMEM)


def whole(shape):
    return pl.BlockSpec(shape, lambda i: (0,) * len(shape))


PER = 4


def per_slot(shape):
    return pl.BlockSpec((PER,) + shape, lambda i: (i,) + (0,) * len(shape))


def call(kernel, name, slots, in_specs, out_specs, out_shape, scratch, flops, size):
    return pl.pallas_call(
        kernel,
        name=name,
        grid=(slots // PER,),
        in_specs=in_specs,
        out_specs=out_specs,
        out_shape=out_shape,
        scratch_shapes=scratch,
        compiler_params=pltpu.CompilerParams(vmem_limit_bytes=32 * 1024 * 1024),
        cost_estimate=pl.CostEstimate(flops=flops, bytes_accessed=size, transcendentals=0),
    )


def shape(*dims):
    return jax.ShapeDtypeStruct(dims, f32)


FIELD = (2, SIDE, SIDE)
MATS = (8, SIDE, SIDE)
EXT = (2, 2 * SIDE, 3 * SIDE)
OWN = (2, SIDE, 2 * SIDE)
SIDES = (2, 2 * SIDE, SIDE)
ENDS = (2, SIDE, 3 * SIDE)
JOINS = {
    "pieces": (join_pieces, [OWN, FIELD, OWN, FIELD]),
    "sides": (join_sides, [EXT, SIDES, SIDES]),
    "ends": (join_ends, [EXT, ENDS, ENDS]),
}
TWO_TRANSFORMS = 24 * 2 * SIDE**3


def specs(shapes):
    return [whole(dims) for dims in shapes]


def two_planes(dims, which):
    return pl.BlockSpec(dims, lambda i: (which, 0, 0))


def part_specs(how, parts, which):
    if how != "pieces":
        return specs(parts)
    return [two_planes(d, which) if d == OWN else whole(d) for d in parts]


def shapes_of(shapes):
    return [shape(*dims) for dims in shapes]


def spread_call(slots, how):
    join, parts = JOINS[how]
    extra = [OWN] if how != "pieces" else []
    return call(
        functools.partial(spread_kernel, join, len(parts)), "spread", slots,
        [SMEM, SMEM, SMEM, *part_specs(how, parts, 0), whole(FIELD), whole(FIELD), whole(MATS)],
        [per_slot(FIELD), per_slot(FIELD), *specs(extra)],
        [shape(slots, *FIELD), shape(slots, *FIELD), *shapes_of(extra)],
        [pltpu.VMEM(EXT, f32)],
        slots * TWO_TRANSFORMS, 9 << 20,
    )


def misfit_call(slots, how):
    join, parts = JOINS[how]
    extra = [OWN] if how != "pieces" else []
    return call(
        functools.partial(misfit_kernel, join, len(parts)), "misfit", slots,
        [SMEM, SMEM, SMEM, SMEM, *part_specs(how, parts, 1), per_slot(FIELD), per_slot((SIDE, SIDE)), whole(MATS)],
        [per_slot(FIELD), *specs([SIDES] * 3 + extra)],
        [shape(slots, *FIELD), *shapes_of([SIDES] * 3 + extra)],
        [pltpu.VMEM(EXT, f32), pltpu.VMEM(EXT, f32)],
        slots * TWO_TRANSFORMS, 12 << 20,
    )


def first_call(slots, sum_rows):
    return call(
        first_kernel, "first", slots,
        [SMEM, SMEM, SMEM, per_slot(FIELD), per_slot(FIELD), whole(FIELD), whole(FIELD), whole(MATS)],
        specs([ENDS, ENDS, (sum_rows, HALF)]),
        shapes_of([ENDS, ENDS, (sum_rows, HALF)]),
        [pltpu.VMEM(EXT, f32)],
        slots * TWO_TRANSFORMS, 9 << 20,
    )


def order_call(count):
    return call(
        order_kernel, "order", count * PER,
        [pl.BlockSpec((1, SIDE, SIDE), lambda i: (i, 0, 0)), whole((2, SIDE, SIDE))],
        pl.BlockSpec((1, SIDE, SIDE), lambda i: (i, 0, 0)),
        shape(count, SIDE, SIDE),
        [],
        count * 12 * SIDE**3, 4 << 20,
    )


def shifted(block, axis, distance):
    devices = range(lax.axis_size(axis))
    route = [(i - distance, i) for i in devices if i - distance in devices]
    return lax.ppermute(block, axis, route)


def partners(block, axis, stride, count, hop):
    route = []
    for i in range(lax.axis_size(axis)):
        digit = i // stride % count
        j = i + ((digit - hop) % count - digit) * stride
        route.append((i, j))
    return lax.ppermute(block, axis, route)


CORE, Z, X, Y = ("band", 1, 2), ("band", 2, 4), ("scan", 1, 4), ("scan", 4, 4)


def scatter_sum(x, ring):
    axis, stride, count = ring
    digit = lax.axis_index(axis) // stride % count
    parts = x.reshape(count, x.shape[0] // count, *x.shape[1:])
    total = lax.dynamic_index_in_dim(parts, digit, 0, False)
    for hop in range(1, count):
        sent = lax.dynamic_index_in_dim(parts, (digit - hop) % count, 0, False)
        total = total + partners(sent, axis, stride, count, hop)
    return total


def gather(x, ring):
    axis, stride, count = ring
    digit = lax.axis_index(axis) // stride % count
    result = jnp.zeros((count, *x.shape), f32)
    result = lax.dynamic_update_index_in_dim(result, x, digit, 0)
    for hop in range(1, count):
        part = partners(x, axis, stride, count, hop)
        result = lax.dynamic_update_index_in_dim(result, part, (digit + hop) % count, 0)
    return result.reshape(count * x.shape[0], *x.shape[1:])


def ring_sum(x, ring):
    axis, stride, count = ring
    one, two, three = (partners(x, axis, stride, count, hop) for hop in (1, 2, 3))
    return (x + two) + (one + three)


def after(value, *others):
    return lax.optimization_barrier((value, *others))[0]


def tied(*values):
    return lax.optimization_barrier(values)


def side_by_side(*parts):
    return jnp.concatenate(parts, axis=2)


def local(objects, probe_field, propagator_phase, patterns, offset_row, offset_column, live_counts):
    width = probe_field.shape[-1]
    tile_rows, tile_cols = objects.shape[1:]
    slots = patterns.shape[2]
    inside_lower = (lax.axis_index("band") < lax.axis_size("band") - 1).astype(f32)
    inside_right = (lax.axis_index("scan") < lax.axis_size("scan") - 1).astype(f32)
    scale = jnp.stack([inside_right, inside_lower])
    mats = jnp.asarray(tables())
    index = np.arange(SIDE)
    order = np.concatenate([np.arange(0, SIDE, 2), np.arange(1, SIDE, 2)])
    swap = (index[:, None] == order[None, :]).astype(ml_dtypes.bfloat16)
    swap = jnp.asarray(np.stack([swap, swap.T]))

    spots = (offset_row[0], offset_column[0], scale)
    live_here = live_counts[0]

    own_one, own_two = objects[:2], objects[2:]
    lower = shifted(objects, "band", -1)
    right_one = shifted(own_one[:, :, :width], "scan", -1)
    right_two = shifted(own_two[:, :, :width], "scan", -1)
    lower_one, lower_two = lower[:2], lower[2:]
    images = jnp.concatenate(
        [patterns[0, 0], jnp.cos(propagator_phase)[None], jnp.sin(propagator_phase)[None]]
    )
    ordered = order_call(slots + 2)(images, swap)
    measured, kernel = ordered[:slots], ordered[slots:]
    corner_one = shifted(after(right_one, ordered), "band", -1)
    corner_two = shifted(right_two, "band", -1)
    probe = probe_field

    def moved_probe(probe, summed, total):
        halves_of = summed.reshape(2, 2, width, width // 2)
        summed = side_by_side(halves_of[:, 0], halves_of[:, 1])
        moved = probe - probe_rate / total * summed
        power = jnp.sum(moved * moved)
        return moved * jnp.sqrt(width * width / (power + power_eps))

    def base_of(own, right, lower, corner, top, bottom):
        rate = object_rate
        upper = side_by_side(
            own - rate * top[:, :, :tile_cols],
            right - (rate * inside_right) * top[:, :, tile_cols:],
        )
        under = side_by_side(
            lower - (rate * inside_lower) * bottom[:, :, :tile_cols],
            corner - (rate * inside_lower * inside_right) * bottom[:, :, tile_cols:],
        )
        return jnp.concatenate([upper, under], axis=1)

    psi, piece = spread_call(slots, "pieces")(
        *spots, objects, right_one, lower, corner_one, probe, kernel, mats
    )
    back, left, middle, right = misfit_call(slots, "pieces")(
        *spots, live_here, objects, right_two, lower, corner_two, psi, measured, mats
    )
    upper, under = slice(0, tile_rows), slice(tile_rows, 2 * tile_rows)
    two_from_left = shifted(right, "scan", 1)
    two_from_right = shifted(left, "scan", -1)
    top, bottom, gprobe = first_call(slots, 4 * SIDE + 64)(
        *spots[:2], live_here, back, piece, probe, kernel, mats
    )
    one_from_above = shifted(bottom, "band", 1)
    one_from_below = shifted(top, "band", -1)
    share, two_from_left, two_from_right = tied(gprobe, two_from_left, two_from_right)
    share = scatter_sum(share, CORE)
    share = scatter_sum(share, X)
    share, one_from_above, one_from_below = tied(share, one_from_above, one_from_below)
    share = ring_sum(share, Y)
    share = ring_sum(share, Z)
    share = gather(share, X)
    one_left = jnp.concatenate(
        [
            top[:, :, :width] + one_from_above[:, :, :width],
            bottom[:, :, :width] + one_from_below[:, :, :width],
        ],
        axis=1,
    )
    one_right = jnp.concatenate(
        [
            top[:, :, tile_cols:] + one_from_above[:, :, tile_cols:],
            bottom[:, :, tile_cols:] + one_from_below[:, :, tile_cols:],
        ],
        axis=1,
    )
    one_from_left = shifted(after(one_right, share), "scan", 1)
    one_from_right = shifted(after(one_left, share), "scan", -1)
    both = gather(share, CORE)
    total = both[-1, 0]
    left, middle, right, both = tied(left, middle, right, both)
    two_ends = [
        side_by_side(
            left[:, part] + two_from_left[:, part],
            middle[:, part],
            right[:, part] + two_from_right[:, part],
        )
        for part in (upper, under)
    ]
    two_from_above = shifted(two_ends[1], "band", 1)
    two_from_below = shifted(two_ends[0], "band", -1)
    probe = moved_probe(probe, both[: 4 * width], total)
    top, bottom, probe = tied(top, bottom, probe)
    base_one = base_of(
        own_one, right_one, lower_one, corner_one, top + one_from_above, bottom + one_from_below
    )
    base_two = base_of(own_two, right_two, lower_two, corner_two, *two_ends)

    psi, piece, own_one = spread_call(slots, "sides")(
        *spots, base_one, one_from_left, one_from_right, probe, kernel, mats
    )
    back, left, middle, right, own_two = misfit_call(slots, "ends")(
        *spots, live_here, base_two, two_from_above, two_from_below, psi, measured, mats
    )
    two_from_left = shifted(right, "scan", 1)
    top, bottom, gprobe = first_call(slots, 4 * SIDE)(
        *spots[:2], live_here, back, piece, probe, kernel, mats
    )
    one_from_above = shifted(bottom, "band", 1)
    share, two_from_left = tied(gprobe, two_from_left)
    share = scatter_sum(share, CORE)
    share = scatter_sum(share, X)
    share = ring_sum(share, Y)
    share, one_from_above = tied(share, one_from_above)
    one_right = top[:, :, tile_cols:] + one_from_above[:, :, tile_cols:]
    one_from_left = shifted(one_right, "scan", 1)
    share = ring_sum(share, Z)
    two_bottom = side_by_side(left[:, under] + two_from_left[:, under], middle[:, under])
    two_from_above = shifted(after(two_bottom, share), "band", 1)
    share, one_from_left = tied(share, one_from_left)
    share = gather(share, X)
    probe = moved_probe(probe, gather(share, CORE), total)
    top = top + one_from_above
    two_top = side_by_side(left[:, upper] + two_from_left[:, upper], middle[:, upper])

    own_one = own_one - object_rate * side_by_side(
        top[:, :, :width] + one_from_left, top[:, :, width:tile_cols]
    )
    own_two = own_two - object_rate * (two_top + two_from_above)
    return (jnp.concatenate([own_one, own_two]), probe)


def solution(mesh):
    return jax.shard_map(
        local,
        mesh=mesh,
        in_specs=(
            P(None, "band", "scan"),
            P(),
            P(),
            P("band", "scan", None, None, None),
            P("band", "scan"),
            P("band", "scan"),
            P("band", "scan"),
        ),
        out_specs=(P(None, "band", "scan"), P()),
        check_vma=False,
    )
```

```python
import functools
import math

import jax
import jax.numpy as jnp
import ml_dtypes
import numpy as np
from jax import lax
from jax.experimental import pallas as pl
from jax.experimental.pallas import tpu as pltpu
from jax.sharding import PartitionSpec as P

ITERS = 2
SIDE = 256
HALF = SIDE // 2
TALL = 264
WIDE = 384

object_rate = 0.1
probe_rate = 2.0
power_eps = 1e-06

f32 = jnp.float32
bf16 = jnp.bfloat16


def halves(matrix):
    high = matrix.astype(ml_dtypes.bfloat16)
    low = (matrix - high.astype(np.float64)).astype(ml_dtypes.bfloat16)
    return [high, low]


def tables():
    point = np.arange(HALF)[None, :]
    result = []
    for parity in (0, 1):
        frequency = 2 * np.arange(HALF)[:, None] + parity
        angle = -2.0 * np.pi / SIDE * (frequency * point % SIDE)
        real = np.cos(angle) / math.sqrt(SIDE)
        imag = np.sin(angle) / math.sqrt(SIDE)
        matrix = np.block([[real, -imag], [imag, real]])
        result += halves(matrix) + halves(matrix.T)
    return np.stack(result)


E_HI, E_LO, ET_HI, ET_LO, O_HI, O_LO, OT_HI, OT_LO = range(8)


def dot(a, b):
    return jnp.dot(a, b, preferred_element_type=f32)


def split(x):
    high = x.astype(bf16)
    low = (x - high.astype(f32)).astype(bf16)
    return high, low


def mul_left(m, hi, x):
    high, low = split(x)
    return dot(m[hi], high) + dot(m[hi], low) + dot(m[hi + 1], high)


def mul_right(x, m, hi):
    high, low = split(x)
    return dot(high, m[hi]) + dot(low, m[hi]) + dot(high, m[hi + 1])


def rows(*parts):
    return jnp.concatenate(parts, axis=0)


def cols(*parts):
    return jnp.concatenate(parts, axis=1)


def forward(re, im, m):
    even = mul_left(m, E_HI, rows(re[:HALF] + re[HALF:], im[:HALF] + im[HALF:]))
    odd = mul_left(m, O_HI, rows(re[:HALF] - re[HALF:], im[:HALF] - im[HALF:]))
    re = rows(even[:HALF], odd[:HALF])
    im = rows(even[HALF:], odd[HALF:])
    u = mul_right(cols(re[:, :HALF] + re[:, HALF:], im[:, :HALF] + im[:, HALF:]), m, ET_HI)
    v = mul_right(cols(re[:, :HALF] - re[:, HALF:], im[:, :HALF] - im[:, HALF:]), m, OT_HI)
    return u, v


def backward(u, v, m):
    a = mul_right(u, m, E_HI)
    b = mul_right(v, m, O_HI)
    re = cols(a[:, :HALF] + b[:, :HALF], a[:, :HALF] - b[:, :HALF])
    im = cols(a[:, HALF:] + b[:, HALF:], a[:, HALF:] - b[:, HALF:])
    a = mul_left(m, ET_HI, rows(re[:HALF], im[:HALF]))
    b = mul_left(m, OT_HI, rows(re[HALF:], im[HALF:]))
    re = rows(a[:HALF] + b[:HALF], a[:HALF] - b[:HALF])
    im = rows(a[HALF:] + b[HALF:], a[HALF:] - b[HALF:])
    return re, im


def by_kernel(u, h, place, sign):
    re, im = u[:, :HALF], u[:, HALF:]
    hr = h[0, :, place * HALF : (place + 1) * HALF]
    hi = h[1, :, place * HALF : (place + 1) * HALF]
    if sign > 0:
        return cols(hr * re - hi * im, hr * im + hi * re)
    return cols(hr * re + hi * im, hr * im - hi * re)


def window(ext, plane, spot):
    row0, row_rest, col0, col_rest = spot
    slab = ext[plane, pl.ds(row0, TALL), pl.ds(col0, WIDE)]
    slab = pltpu.roll(slab, lax.rem(WIDE - col_rest, WIDE), 1)[:, :SIDE]
    return pltpu.roll(slab, lax.rem(TALL - row_rest, TALL), 0)[:SIDE]


def place(row_ref, col_ref, slot):
    row = row_ref[slot]
    col = col_ref[slot]
    row_rest = lax.rem(row, 8)
    col_rest = lax.rem(col, 128)
    row0 = pl.multiple_of(row - row_rest, 8)
    col0 = pl.multiple_of(col - col_rest, 128)
    return row0, row_rest, col0, col_rest


def join_pieces(ext, scale, own, right, lower, corner):
    tile_rows, tile_cols = own.shape[1:]
    ext[:, :tile_rows, :tile_cols] = own[...]
    ext[:, :tile_rows, tile_cols:] = right[...]
    ext[:, tile_rows:, :tile_cols] = lower[...]
    ext[:, tile_rows:, tile_cols:] = corner[...]


def join_sides(ext, scale, base, from_left, from_right):
    inside_right, inside_lower = scale[0], scale[1]
    for rows_at, factor in ((0, object_rate), (SIDE, object_rate * inside_lower)):
        at = pl.ds(rows_at, SIDE)
        ext[:, at, :SIDE] = base[:, at, :SIDE] - factor * from_left[:, at]
        ext[:, at, SIDE : 2 * SIDE] = base[:, at, SIDE : 2 * SIDE]
        ext[:, at, 2 * SIDE :] = base[:, at, 2 * SIDE :] - factor * inside_right * from_right[:, at]


def join_ends(ext, scale, base, from_above, from_below):
    inside_right, inside_lower = scale[0], scale[1]
    for rows_at, come, factor in (
        (0, from_above, object_rate),
        (SIDE, from_below, object_rate * inside_lower),
    ):
        at = pl.ds(rows_at, SIDE)
        ext[:, at, : 2 * SIDE] = base[:, at, : 2 * SIDE] - factor * come[:, :, : 2 * SIDE]
        ext[:, at, 2 * SIDE :] = (
            base[:, at, 2 * SIDE :] - factor * inside_right * come[:, :, 2 * SIDE :]
        )


def spread_kernel(join, count, row_ref, col_ref, scale, *refs):
    slot = pl.program_id(0)
    parts, (probe, h, m, psi, piece, *rest) = refs[:count], refs[count:]
    own, ext = rest if len(rest) == 2 else (None, rest[0])

    @pl.when(slot == 0)
    def _():
        join(ext, scale, *parts)
        if own is not None:
            own[...] = ext[:, : own.shape[1], : own.shape[2]]

    for k in range(PER):
        spot = place(row_ref, col_ref, slot * PER + k)
        ar = window(ext, 0, spot)
        ai = window(ext, 1, spot)
        piece[k, 0] = ar
        piece[k, 1] = ai
        pr, pi = probe[0], probe[1]
        u, v = forward(pr * ar - pi * ai, pr * ai + pi * ar, m)
        re, im = backward(by_kernel(u, h, 0, 1), by_kernel(v, h, 1, 1), m)
        psi[k, 0] = re
        psi[k, 1] = im


def add_window(accum, plane, grad, spot):
    row0, row_rest, col0, col_rest = spot
    tall = rows(grad, jnp.zeros((TALL - SIDE, SIDE), f32))
    tall = pltpu.roll(tall, row_rest, 0)
    wide = cols(tall, jnp.zeros((TALL, WIDE - SIDE), f32))
    wide = pltpu.roll(wide, col_rest, 1)
    accum[plane, pl.ds(row0, TALL), pl.ds(col0, WIDE)] += wide


def misfit_kernel(join, count, row_ref, col_ref, scale, live_ref, *refs):
    slot = pl.program_id(0)
    parts, (psi, pattern, m, back, left, mid, right, *rest) = refs[:count], refs[count:]
    own, ext, accum = rest if len(rest) == 3 else (None, *rest)

    @pl.when(slot == 0)
    def _():
        join(ext, scale, *parts)
        if own is not None:
            own[...] = ext[:, : own.shape[1], : own.shape[2]]
        accum[...] = jnp.zeros_like(accum)

    for k in range(PER):
        spot = place(row_ref, col_ref, slot * PER + k)
        ar = window(ext, 0, spot)
        ai = window(ext, 1, spot)
        sr, si = psi[k, 0], psi[k, 1]
        u, v = forward(sr * ar - si * ai, sr * ai + si * ar, m)
        live = (slot * PER + k < live_ref[0]).astype(f32)

        def weigh(part, measured):
            re, im = part[:, :HALF], part[:, HALF:]
            weight = (re * re + im * im - measured) * live
            return cols(weight * re, weight * im)

        u = weigh(u, pattern[k, :, :HALF])
        v = weigh(v, pattern[k, :, HALF:])
        re, im = backward(u, v, m)
        back[k, 0] = ar * re + ai * im
        back[k, 1] = ar * im - ai * re
        add_window(accum, 0, sr * re + si * im, spot)
        add_window(accum, 1, sr * im - si * re, spot)

    @pl.when(slot == pl.num_programs(0) - 1)
    def _():
        left[...] = accum[:, :, :SIDE]
        mid[...] = accum[:, :, SIDE : 2 * SIDE]
        right[...] = accum[:, :, 2 * SIDE :]


def first_kernel(
    row_ref, col_ref, live_ref, back, piece, probe, h, m, top, bottom, gprobe, accum
):
    slot = pl.program_id(0)

    @pl.when(slot == 0)
    def _():
        accum[...] = jnp.zeros_like(accum)
        gprobe[: 4 * SIDE] = jnp.zeros((4 * SIDE, HALF), f32)
        if gprobe.shape[0] > 4 * SIDE:
            live = jnp.minimum(live_ref[0], PER * pl.num_programs(0)).astype(f32)
            gprobe[4 * SIDE :] = jnp.full((gprobe.shape[0] - 4 * SIDE, HALF), live)

    for k in range(PER):
        spot = place(row_ref, col_ref, slot * PER + k)
        u, v = forward(back[k, 0], back[k, 1], m)
        re, im = backward(by_kernel(u, h, 0, -1), by_kernel(v, h, 1, -1), m)
        ar, ai = piece[k, 0], piece[k, 1]
        for at, value in enumerate((ar * re + ai * im, ar * im - ai * re)):
            for side in (0, 1):
                part = value[:, side * HALF : (side + 1) * HALF]
                gprobe[(2 * at + side) * SIDE : (2 * at + side + 1) * SIDE] += part
        pr, pi = probe[0], probe[1]
        add_window(accum, 0, pr * re + pi * im, spot)
        add_window(accum, 1, pr * im - pi * re, spot)

    @pl.when(slot == pl.num_programs(0) - 1)
    def _():
        top[...] = accum[:, :SIDE]
        bottom[...] = accum[:, SIDE:]


def picked(value, move):
    total = None
    for _ in range(3):
        part = value.astype(bf16)
        value = value - part.astype(f32)
        moved = move(part)
        total = moved if total is None else total + moved
    return total


def order_kernel(x, swap, out):
    value = picked(x[0], lambda part: dot(part, swap[0]))
    out[0] = picked(value, lambda part: dot(swap[1], part))


SMEM = pl.BlockSpec(memory_space=pltpu.SMEM)


def whole(shape):
    return pl.BlockSpec(shape, lambda i: (0,) * len(shape))


PER = 4


def per_slot(shape):
    return pl.BlockSpec((PER,) + shape, lambda i: (i,) + (0,) * len(shape))


def call(kernel, name, slots, in_specs, out_specs, out_shape, scratch, flops, size):
    return pl.pallas_call(
        kernel,
        name=name,
        grid=(slots // PER,),
        in_specs=in_specs,
        out_specs=out_specs,
        out_shape=out_shape,
        scratch_shapes=scratch,
        compiler_params=pltpu.CompilerParams(vmem_limit_bytes=32 * 1024 * 1024),
        cost_estimate=pl.CostEstimate(flops=flops, bytes_accessed=size, transcendentals=0),
    )


def shape(*dims):
    return jax.ShapeDtypeStruct(dims, f32)


FIELD = (2, SIDE, SIDE)
MATS = (8, SIDE, SIDE)
EXT = (2, 2 * SIDE, 3 * SIDE)
OWN = (2, SIDE, 2 * SIDE)
SIDES = (2, 2 * SIDE, SIDE)
ENDS = (2, SIDE, 3 * SIDE)
JOINS = {
    "pieces": (join_pieces, [OWN, FIELD, OWN, FIELD]),
    "sides": (join_sides, [EXT, SIDES, SIDES]),
    "ends": (join_ends, [EXT, ENDS, ENDS]),
}
TWO_TRANSFORMS = 24 * 2 * SIDE**3


def specs(shapes):
    return [whole(dims) for dims in shapes]


def two_planes(dims, which):
    return pl.BlockSpec(dims, lambda i: (which, 0, 0))


def part_specs(how, parts, which):
    if how != "pieces":
        return specs(parts)
    return [
        two_planes(parts[0], which),
        whole(parts[1]),
        two_planes(parts[2], 1 - which),
        whole(parts[3]),
    ]


def shapes_of(shapes):
    return [shape(*dims) for dims in shapes]


KERNEL = pl.BlockSpec(FIELD, lambda i: (2, 0, 0))


def spread_call(slots, how):
    join, parts = JOINS[how]
    extra = [OWN] if how != "pieces" else []
    return call(
        functools.partial(spread_kernel, join, len(parts)), "spread", slots,
        [SMEM, SMEM, SMEM, *part_specs(how, parts, 0), whole(FIELD), KERNEL, whole(MATS)],
        [per_slot(FIELD), per_slot(FIELD), *specs(extra)],
        [shape(slots, *FIELD), shape(slots, *FIELD), *shapes_of(extra)],
        [pltpu.VMEM(EXT, f32)],
        slots * TWO_TRANSFORMS, 9 << 20,
    )


def misfit_call(slots, how):
    join, parts = JOINS[how]
    extra = [OWN] if how != "pieces" else []
    return call(
        functools.partial(misfit_kernel, join, len(parts)), "misfit", slots,
        [SMEM, SMEM, SMEM, SMEM, *part_specs(how, parts, 1), per_slot(FIELD), per_slot((SIDE, SIDE)), whole(MATS)],
        [per_slot(FIELD), *specs([SIDES] * 3 + extra)],
        [shape(slots, *FIELD), *shapes_of([SIDES] * 3 + extra)],
        [pltpu.VMEM(EXT, f32), pltpu.VMEM(EXT, f32)],
        slots * TWO_TRANSFORMS, 12 << 20,
    )


def first_call(slots, sum_rows):
    return call(
        first_kernel, "first", slots,
        [SMEM, SMEM, SMEM, per_slot(FIELD), per_slot(FIELD), whole(FIELD), KERNEL, whole(MATS)],
        specs([ENDS, ENDS, (sum_rows, HALF)]),
        shapes_of([ENDS, ENDS, (sum_rows, HALF)]),
        [pltpu.VMEM(EXT, f32)],
        slots * TWO_TRANSFORMS, 9 << 20,
    )


def order_call(count):
    return call(
        order_kernel, "order", count * PER,
        [pl.BlockSpec((1, SIDE, SIDE), lambda i: (i, 0, 0)), whole((2, SIDE, SIDE))],
        pl.BlockSpec((1, SIDE, SIDE), lambda i: (i, 0, 0)),
        shape(count, SIDE, SIDE),
        [],
        count * 12 * SIDE**3, 4 << 20,
    )


def shifted(block, axis, distance):
    devices = range(lax.axis_size(axis))
    route = [(i - distance, i) for i in devices if i - distance in devices]
    return lax.ppermute(block, axis, route)


def partners(block, axis, stride, count, hop):
    route = []
    for i in range(lax.axis_size(axis)):
        digit = i // stride % count
        j = i + ((digit - hop) % count - digit) * stride
        route.append((i, j))
    return lax.ppermute(block, axis, route)


CORE, Z, X, Y = ("band", 1, 2), ("band", 2, 4), ("scan", 1, 4), ("scan", 4, 4)


def scatter_sum(x, ring):
    axis, stride, count = ring
    digit = lax.axis_index(axis) // stride % count
    parts = x.reshape(count, x.shape[0] // count, *x.shape[1:])
    total = lax.dynamic_index_in_dim(parts, digit, 0, False)
    for hop in range(1, count):
        sent = lax.dynamic_index_in_dim(parts, (digit - hop) % count, 0, False)
        total = total + partners(sent, axis, stride, count, hop)
    return total


def gather(x, ring):
    axis, stride, count = ring
    digit = lax.axis_index(axis) // stride % count
    result = jnp.zeros((count, *x.shape), f32)
    result = lax.dynamic_update_index_in_dim(result, x, digit, 0)
    for hop in range(1, count):
        part = partners(x, axis, stride, count, hop)
        result = lax.dynamic_update_index_in_dim(result, part, (digit + hop) % count, 0)
    return result.reshape(count * x.shape[0], *x.shape[1:])


def ring_sum(x, ring):
    axis, stride, count = ring
    one, two, three = (partners(x, axis, stride, count, hop) for hop in (1, 2, 3))
    return (x + two) + (one + three)


def in_order(x):
    parts = x.reshape(X[2], CORE[2], -1, x.shape[1])
    return jnp.swapaxes(parts, 0, 1).reshape(x.shape)


def after(value, *others):
    return lax.optimization_barrier((value, *others))[0]


def tied(*values):
    return lax.optimization_barrier(values)


def side_by_side(*parts):
    return jnp.concatenate(parts, axis=2)


def local(objects, probe_field, propagator_phase, patterns, offset_row, offset_column, live_counts):
    width = probe_field.shape[-1]
    tile_rows, tile_cols = objects.shape[1:]
    slots = patterns.shape[2]
    inside_lower = (lax.axis_index("band") < lax.axis_size("band") - 1).astype(f32)
    inside_right = (lax.axis_index("scan") < lax.axis_size("scan") - 1).astype(f32)
    scale = jnp.stack([inside_right, inside_lower])
    mats = jnp.asarray(tables())
    index = np.arange(SIDE)
    order = np.concatenate([np.arange(0, SIDE, 2), np.arange(1, SIDE, 2)])
    swap = (index[:, None] == order[None, :]).astype(ml_dtypes.bfloat16)
    swap = jnp.asarray(np.stack([swap, swap.T]))

    spots = (offset_row[0], offset_column[0], scale)
    live_here = live_counts[0]

    own_one, own_two = objects[:2], objects[2:]
    lower = shifted(jnp.concatenate([own_two, own_one]), "band", -1)
    right_one = shifted(own_one[:, :, :width], "scan", -1)
    right_two = shifted(own_two[:, :, :width], "scan", -1)
    lower_two, lower_one = lower[:2], lower[2:]
    images = jnp.concatenate(
        [patterns[0, 0], jnp.cos(propagator_phase)[None], jnp.sin(propagator_phase)[None]]
    )
    ordered = order_call(slots + 2)(images, swap)
    corner_one = shifted(after(right_one, ordered), "band", -1)
    corner_two = shifted(right_two, "band", -1)
    probe = probe_field

    def moved_probe(probe, summed, total):
        halves_of = summed.reshape(2, 2, width, width // 2)
        summed = side_by_side(halves_of[:, 0], halves_of[:, 1])
        moved = probe - probe_rate / total * summed
        power = jnp.sum(moved * moved)
        return moved * jnp.sqrt(width * width / (power + power_eps))

    def base_of(own, right, lower, corner, top, bottom):
        rate = object_rate
        upper = side_by_side(
            own - rate * top[:, :, :tile_cols],
            right - (rate * inside_right) * top[:, :, tile_cols:],
        )
        under = side_by_side(
            lower - (rate * inside_lower) * bottom[:, :, :tile_cols],
            corner - (rate * inside_lower * inside_right) * bottom[:, :, tile_cols:],
        )
        return jnp.concatenate([upper, under], axis=1)

    psi, piece = spread_call(slots, "pieces")(
        *spots, objects, right_one, lower, corner_one, probe, ordered, mats
    )
    back, left, middle, right = misfit_call(slots, "pieces")(
        *spots, live_here, objects, right_two, lower, corner_two, psi, ordered, mats
    )
    upper, under = slice(0, tile_rows), slice(tile_rows, 2 * tile_rows)
    two_from_left = shifted(right, "scan", 1)
    two_from_right = shifted(left, "scan", -1)
    top, bottom, gprobe = first_call(slots, 4 * SIDE + 64)(
        *spots[:2], live_here, back, piece, probe, ordered, mats
    )
    one_from_above = shifted(bottom, "band", 1)
    one_from_below = shifted(top, "band", -1)
    share, two_from_left, two_from_right = tied(gprobe, two_from_left, two_from_right)
    share = scatter_sum(share, CORE)
    share = scatter_sum(share, X)
    share, one_from_above, one_from_below = tied(share, one_from_above, one_from_below)
    share = ring_sum(share, Y)
    share = ring_sum(share, Z)
    share = gather(share, CORE)
    one_left = jnp.concatenate(
        [
            top[:, :, :width] + one_from_above[:, :, :width],
            bottom[:, :, :width] + one_from_below[:, :, :width],
        ],
        axis=1,
    )
    one_right = jnp.concatenate(
        [
            top[:, :, tile_cols:] + one_from_above[:, :, tile_cols:],
            bottom[:, :, tile_cols:] + one_from_below[:, :, tile_cols:],
        ],
        axis=1,
    )
    share, one_left, one_right = tied(share, one_left, one_right)
    share = gather(share, X)
    one_from_left = shifted(after(one_right, share), "scan", 1)
    one_from_right = shifted(after(one_left, share), "scan", -1)
    both = in_order(share)
    total = both[-1, 0]
    left, middle, right, both = tied(left, middle, right, both)
    two_ends = [
        side_by_side(
            left[:, part] + two_from_left[:, part],
            middle[:, part],
            right[:, part] + two_from_right[:, part],
        )
        for part in (upper, under)
    ]
    two_from_above = shifted(two_ends[1], "band", 1)
    two_from_below = shifted(two_ends[0], "band", -1)
    probe = moved_probe(probe, both[: 4 * width], total)
    top, bottom, probe = tied(top, bottom, probe)
    base_one = base_of(
        own_one, right_one, lower_one, corner_one, top + one_from_above, bottom + one_from_below
    )
    base_two = base_of(own_two, right_two, lower_two, corner_two, *two_ends)

    psi, piece, own_one = spread_call(slots, "sides")(
        *spots, base_one, one_from_left, one_from_right, probe, ordered, mats
    )
    back, left, middle, right, own_two = misfit_call(slots, "ends")(
        *spots, live_here, base_two, two_from_above, two_from_below, psi, ordered, mats
    )
    two_from_left = shifted(right, "scan", 1)
    top, bottom, gprobe = first_call(slots, 4 * SIDE)(
        *spots[:2], live_here, back, piece, probe, ordered, mats
    )
    one_from_above = shifted(bottom, "band", 1)
    share, two_from_left = tied(gprobe, two_from_left)
    share = scatter_sum(share, CORE)
    share = scatter_sum(share, X)
    share = ring_sum(share, Y)
    share, one_from_above = tied(share, one_from_above)
    one_right = top[:, :, tile_cols:] + one_from_above[:, :, tile_cols:]
    one_from_left = shifted(one_right, "scan", 1)
    share = ring_sum(share, Z)
    two_bottom = side_by_side(left[:, under] + two_from_left[:, under], middle[:, under])
    two_from_above = shifted(after(two_bottom, share), "band", 1)
    share, one_from_left = tied(share, one_from_left)
    share = gather(share, CORE)
    share = gather(share, X)
    probe = moved_probe(probe, in_order(share), total)
    top = top + one_from_above
    two_top = side_by_side(left[:, upper] + two_from_left[:, upper], middle[:, upper])

    own_one = own_one - object_rate * side_by_side(
        top[:, :, :width] + one_from_left, top[:, :, width:tile_cols]
    )
    own_two = own_two - object_rate * (two_top + two_from_above)
    return (jnp.concatenate([own_one, own_two]), probe)


def solution(mesh):
    return jax.shard_map(
        local,
        mesh=mesh,
        in_specs=(
            P(None, "band", "scan"),
            P(),
            P(),
            P("band", "scan", None, None, None),
            P("band", "scan"),
            P("band", "scan"),
            P("band", "scan"),
        ),
        out_specs=(P(None, "band", "scan"), P()),
        check_vma=False,
    )
```

```python
import functools
import math

import jax
import jax.numpy as jnp
import ml_dtypes
import numpy as np
from jax import lax
from jax.experimental import pallas as pl
from jax.experimental.pallas import tpu as pltpu
from jax.sharding import PartitionSpec as P

ITERS = 2
SIDE = 256
HALF = SIDE // 2
TALL = 264
WIDE = 384

object_rate = 0.1
probe_rate = 2.0
power_eps = 1e-06

f32 = jnp.float32
bf16 = jnp.bfloat16


def halves(matrix):
    high = matrix.astype(ml_dtypes.bfloat16)
    low = (matrix - high.astype(np.float64)).astype(ml_dtypes.bfloat16)
    return [high, low]


def tables():
    point = np.arange(HALF)[None, :]
    result = []
    for parity in (0, 1):
        frequency = 2 * np.arange(HALF)[:, None] + parity
        angle = -2.0 * np.pi / SIDE * (frequency * point % SIDE)
        real = np.cos(angle) / math.sqrt(SIDE)
        imag = np.sin(angle) / math.sqrt(SIDE)
        matrix = np.block([[real, -imag], [imag, real]])
        result += halves(matrix) + halves(matrix.T)
    return np.stack(result)


E_HI, E_LO, ET_HI, ET_LO, O_HI, O_LO, OT_HI, OT_LO = range(8)


def dot(a, b):
    return jnp.dot(a, b, preferred_element_type=f32)


def split(x):
    high = x.astype(bf16)
    low = (x - high.astype(f32)).astype(bf16)
    return high, low


def mul_left(m, hi, x):
    high, low = split(x)
    return dot(m[hi], high) + dot(m[hi], low) + dot(m[hi + 1], high)


def mul_right(x, m, hi):
    high, low = split(x)
    return dot(high, m[hi]) + dot(low, m[hi]) + dot(high, m[hi + 1])


def rows(*parts):
    return jnp.concatenate(parts, axis=0)


def cols(*parts):
    return jnp.concatenate(parts, axis=1)


def forward(re, im, m):
    even = mul_left(m, E_HI, rows(re[:HALF] + re[HALF:], im[:HALF] + im[HALF:]))
    odd = mul_left(m, O_HI, rows(re[:HALF] - re[HALF:], im[:HALF] - im[HALF:]))
    re = rows(even[:HALF], odd[:HALF])
    im = rows(even[HALF:], odd[HALF:])
    u = mul_right(cols(re[:, :HALF] + re[:, HALF:], im[:, :HALF] + im[:, HALF:]), m, ET_HI)
    v = mul_right(cols(re[:, :HALF] - re[:, HALF:], im[:, :HALF] - im[:, HALF:]), m, OT_HI)
    return u, v


def backward(u, v, m):
    a = mul_right(u, m, E_HI)
    b = mul_right(v, m, O_HI)
    re = cols(a[:, :HALF] + b[:, :HALF], a[:, :HALF] - b[:, :HALF])
    im = cols(a[:, HALF:] + b[:, HALF:], a[:, HALF:] - b[:, HALF:])
    a = mul_left(m, ET_HI, rows(re[:HALF], im[:HALF]))
    b = mul_left(m, OT_HI, rows(re[HALF:], im[HALF:]))
    re = rows(a[:HALF] + b[:HALF], a[:HALF] - b[:HALF])
    im = rows(a[HALF:] + b[HALF:], a[HALF:] - b[HALF:])
    return re, im


def by_kernel(u, h, place, sign):
    re, im = u[:, :HALF], u[:, HALF:]
    hr = h[0, :, place * HALF : (place + 1) * HALF]
    hi = h[1, :, place * HALF : (place + 1) * HALF]
    if sign > 0:
        return cols(hr * re - hi * im, hr * im + hi * re)
    return cols(hr * re + hi * im, hr * im - hi * re)


def window(ext, plane, spot):
    row0, row_rest, col0, col_rest = spot
    slab = ext[plane, pl.ds(row0, TALL), pl.ds(col0, WIDE)]
    slab = pltpu.roll(slab, lax.rem(WIDE - col_rest, WIDE), 1)[:, :SIDE]
    return pltpu.roll(slab, lax.rem(TALL - row_rest, TALL), 0)[:SIDE]


def place(row_ref, col_ref, slot):
    row = row_ref[slot]
    col = col_ref[slot]
    row_rest = lax.rem(row, 8)
    col_rest = lax.rem(col, 128)
    row0 = pl.multiple_of(row - row_rest, 8)
    col0 = pl.multiple_of(col - col_rest, 128)
    return row0, row_rest, col0, col_rest


def join_pieces(ext, scale, own, right, lower, corner):
    tile_rows, tile_cols = own.shape[1:]
    ext[:, :tile_rows, :tile_cols] = own[...]
    ext[:, :tile_rows, tile_cols:] = right[...]
    ext[:, tile_rows:, :tile_cols] = lower[...]
    ext[:, tile_rows:, tile_cols:] = corner[...]


def join_sides(ext, scale, base, from_left, from_right):
    inside_right, inside_lower = scale[0], scale[1]
    for rows_at, factor in ((0, object_rate), (SIDE, object_rate * inside_lower)):
        at = pl.ds(rows_at, SIDE)
        ext[:, at, :SIDE] = base[:, at, :SIDE] - factor * from_left[:, at]
        ext[:, at, SIDE : 2 * SIDE] = base[:, at, SIDE : 2 * SIDE]
        ext[:, at, 2 * SIDE :] = base[:, at, 2 * SIDE :] - factor * inside_right * from_right[:, at]


def join_ends(ext, scale, base, from_above, from_below):
    inside_right, inside_lower = scale[0], scale[1]
    for rows_at, come, factor in (
        (0, from_above, object_rate),
        (SIDE, from_below, object_rate * inside_lower),
    ):
        at = pl.ds(rows_at, SIDE)
        ext[:, at, : 2 * SIDE] = base[:, at, : 2 * SIDE] - factor * come[:, :, : 2 * SIDE]
        ext[:, at, 2 * SIDE :] = (
            base[:, at, 2 * SIDE :] - factor * inside_right * come[:, :, 2 * SIDE :]
        )


def spread_kernel(join, count, row_ref, col_ref, scale, *refs):
    slot = pl.program_id(0)
    parts, (probe, h, m, psi, piece, *rest) = refs[:count], refs[count:]
    own, ext = rest if len(rest) == 2 else (None, rest[0])

    @pl.when(slot == 0)
    def _():
        join(ext, scale, *parts)
        if own is not None:
            own[...] = ext[:, : own.shape[1], : own.shape[2]]

    for k in range(PER):
        spot = place(row_ref, col_ref, slot * PER + k)
        ar = window(ext, 0, spot)
        ai = window(ext, 1, spot)
        piece[k, 0] = ar
        piece[k, 1] = ai
        pr, pi = probe[0], probe[1]
        u, v = forward(pr * ar - pi * ai, pr * ai + pi * ar, m)
        re, im = backward(by_kernel(u, h, 0, 1), by_kernel(v, h, 1, 1), m)
        psi[k, 0] = re
        psi[k, 1] = im


def add_window(accum, plane, grad, spot):
    row0, row_rest, col0, col_rest = spot
    tall = rows(grad, jnp.zeros((TALL - SIDE, SIDE), f32))
    tall = pltpu.roll(tall, row_rest, 0)
    wide = cols(tall, jnp.zeros((TALL, WIDE - SIDE), f32))
    wide = pltpu.roll(wide, col_rest, 1)
    accum[plane, pl.ds(row0, TALL), pl.ds(col0, WIDE)] += wide


def misfit_kernel(join, count, row_ref, col_ref, scale, live_ref, *refs):
    slot = pl.program_id(0)
    parts, (psi, pattern, m, back, left, mid, right, *rest) = refs[:count], refs[count:]
    own, ext, accum = rest if len(rest) == 3 else (None, *rest)

    @pl.when(slot == 0)
    def _():
        join(ext, scale, *parts)
        if own is not None:
            own[...] = ext[:, : own.shape[1], : own.shape[2]]
        accum[...] = jnp.zeros_like(accum)

    for k in range(PER):
        spot = place(row_ref, col_ref, slot * PER + k)
        ar = window(ext, 0, spot)
        ai = window(ext, 1, spot)
        sr, si = psi[k, 0], psi[k, 1]
        u, v = forward(sr * ar - si * ai, sr * ai + si * ar, m)
        live = (slot * PER + k < live_ref[0]).astype(f32)

        def weigh(part, measured):
            re, im = part[:, :HALF], part[:, HALF:]
            weight = (re * re + im * im - measured) * live
            return cols(weight * re, weight * im)

        u = weigh(u, pattern[k, :, :HALF])
        v = weigh(v, pattern[k, :, HALF:])
        re, im = backward(u, v, m)
        back[k, 0] = ar * re + ai * im
        back[k, 1] = ar * im - ai * re
        add_window(accum, 0, sr * re + si * im, spot)
        add_window(accum, 1, sr * im - si * re, spot)

    @pl.when(slot == pl.num_programs(0) - 1)
    def _():
        left[...] = accum[:, :, :SIDE]
        mid[...] = accum[:, :, SIDE : 2 * SIDE]
        right[...] = accum[:, :, 2 * SIDE :]


def first_kernel(
    row_ref, col_ref, live_ref, back, piece, probe, h, m, top, bottom, gprobe, accum
):
    slot = pl.program_id(0)

    @pl.when(slot == 0)
    def _():
        accum[...] = jnp.zeros_like(accum)
        gprobe[: 4 * SIDE] = jnp.zeros((4 * SIDE, HALF), f32)
        if gprobe.shape[0] > 4 * SIDE:
            live = jnp.minimum(live_ref[0], PER * pl.num_programs(0)).astype(f32)
            gprobe[4 * SIDE :] = jnp.full((gprobe.shape[0] - 4 * SIDE, HALF), live)

    for k in range(PER):
        spot = place(row_ref, col_ref, slot * PER + k)
        u, v = forward(back[k, 0], back[k, 1], m)
        re, im = backward(by_kernel(u, h, 0, -1), by_kernel(v, h, 1, -1), m)
        ar, ai = piece[k, 0], piece[k, 1]
        for at, value in enumerate((ar * re + ai * im, ar * im - ai * re)):
            for side in (0, 1):
                part = value[:, side * HALF : (side + 1) * HALF]
                gprobe[(2 * at + side) * SIDE : (2 * at + side + 1) * SIDE] += part
        pr, pi = probe[0], probe[1]
        add_window(accum, 0, pr * re + pi * im, spot)
        add_window(accum, 1, pr * im - pi * re, spot)

    @pl.when(slot == pl.num_programs(0) - 1)
    def _():
        top[...] = accum[:, :SIDE]
        bottom[...] = accum[:, SIDE:]


def picked(value, move):
    total = None
    for _ in range(3):
        part = value.astype(bf16)
        value = value - part.astype(f32)
        moved = move(part)
        total = moved if total is None else total + moved
    return total


def order_kernel(x, swap, out):
    value = picked(x[0], lambda part: dot(part, swap[0]))
    out[0] = picked(value, lambda part: dot(swap[1], part))


SMEM = pl.BlockSpec(memory_space=pltpu.SMEM)


def whole(shape):
    return pl.BlockSpec(shape, lambda i: (0,) * len(shape))


PER = 4


def per_slot(shape):
    return pl.BlockSpec((PER,) + shape, lambda i: (i,) + (0,) * len(shape))


def call(kernel, name, slots, in_specs, out_specs, out_shape, scratch, flops, size):
    return pl.pallas_call(
        kernel,
        name=name,
        grid=(slots // PER,),
        in_specs=in_specs,
        out_specs=out_specs,
        out_shape=out_shape,
        scratch_shapes=scratch,
        compiler_params=pltpu.CompilerParams(vmem_limit_bytes=32 * 1024 * 1024),
        cost_estimate=pl.CostEstimate(flops=flops, bytes_accessed=size, transcendentals=0),
    )


def shape(*dims):
    return jax.ShapeDtypeStruct(dims, f32)


FIELD = (2, SIDE, SIDE)
MATS = (8, SIDE, SIDE)
EXT = (2, 2 * SIDE, 3 * SIDE)
OWN = (2, SIDE, 2 * SIDE)
SIDES = (2, 2 * SIDE, SIDE)
ENDS = (2, SIDE, 3 * SIDE)
JOINS = {
    "pieces": (join_pieces, [OWN, FIELD, OWN, FIELD]),
    "sides": (join_sides, [EXT, SIDES, SIDES]),
    "ends": (join_ends, [EXT, ENDS, ENDS]),
}
TWO_TRANSFORMS = 24 * 2 * SIDE**3


def specs(shapes):
    return [whole(dims) for dims in shapes]


def two_planes(dims, which):
    return pl.BlockSpec(dims, lambda i: (which, 0, 0))


def part_specs(how, parts, which):
    if how != "pieces":
        return specs(parts)
    return [
        two_planes(parts[0], which),
        whole(parts[1]),
        two_planes(parts[2], 1 - which),
        whole(parts[3]),
    ]


def shapes_of(shapes):
    return [shape(*dims) for dims in shapes]


KERNEL = pl.BlockSpec(FIELD, lambda i: (2, 0, 0))


def spread_call(slots, how):
    join, parts = JOINS[how]
    extra = [OWN] if how != "pieces" else []
    return call(
        functools.partial(spread_kernel, join, len(parts)), "spread", slots,
        [SMEM, SMEM, SMEM, *part_specs(how, parts, 0), whole(FIELD), KERNEL, whole(MATS)],
        [per_slot(FIELD), per_slot(FIELD), *specs(extra)],
        [shape(slots, *FIELD), shape(slots, *FIELD), *shapes_of(extra)],
        [pltpu.VMEM(EXT, f32)],
        slots * TWO_TRANSFORMS, 9 << 20,
    )


def misfit_call(slots, how):
    join, parts = JOINS[how]
    extra = [OWN] if how != "pieces" else []
    return call(
        functools.partial(misfit_kernel, join, len(parts)), "misfit", slots,
        [SMEM, SMEM, SMEM, SMEM, *part_specs(how, parts, 1), per_slot(FIELD), per_slot((SIDE, SIDE)), whole(MATS)],
        [per_slot(FIELD), *specs([SIDES] * 3 + extra)],
        [shape(slots, *FIELD), *shapes_of([SIDES] * 3 + extra)],
        [pltpu.VMEM(EXT, f32), pltpu.VMEM(EXT, f32)],
        slots * TWO_TRANSFORMS, 12 << 20,
    )


def first_call(slots, sum_rows):
    return call(
        first_kernel, "first", slots,
        [SMEM, SMEM, SMEM, per_slot(FIELD), per_slot(FIELD), whole(FIELD), KERNEL, whole(MATS)],
        specs([ENDS, ENDS, (sum_rows, HALF)]),
        shapes_of([ENDS, ENDS, (sum_rows, HALF)]),
        [pltpu.VMEM(EXT, f32)],
        slots * TWO_TRANSFORMS, 9 << 20,
    )


def order_call(count):
    return call(
        order_kernel, "order", count * PER,
        [pl.BlockSpec((1, SIDE, SIDE), lambda i: (i, 0, 0)), whole((2, SIDE, SIDE))],
        pl.BlockSpec((1, SIDE, SIDE), lambda i: (i, 0, 0)),
        shape(count, SIDE, SIDE),
        [],
        count * 12 * SIDE**3, 4 << 20,
    )


def shifted(block, axis, distance):
    devices = range(lax.axis_size(axis))
    route = [(i - distance, i) for i in devices if i - distance in devices]
    return lax.ppermute(block, axis, route)


def partners(block, axis, stride, count, hop):
    route = []
    for i in range(lax.axis_size(axis)):
        digit = i // stride % count
        j = i + ((digit - hop) % count - digit) * stride
        route.append((i, j))
    return lax.ppermute(block, axis, route)


CORE, Z, X, Y = ("band", 1, 2), ("band", 2, 4), ("scan", 1, 4), ("scan", 4, 4)


def scatter_sum(x, ring):
    axis, stride, count = ring
    digit = lax.axis_index(axis) // stride % count
    parts = x.reshape(count, x.shape[0] // count, *x.shape[1:])
    total = lax.dynamic_index_in_dim(parts, digit, 0, False)
    for hop in range(1, count):
        sent = lax.dynamic_index_in_dim(parts, (digit - hop) % count, 0, False)
        total = total + partners(sent, axis, stride, count, hop)
    return total


def gather(x, ring):
    axis, stride, count = ring
    digit = lax.axis_index(axis) // stride % count
    result = jnp.zeros((count, *x.shape), f32)
    result = lax.dynamic_update_index_in_dim(result, x, digit, 0)
    for hop in range(1, count):
        part = partners(x, axis, stride, count, hop)
        result = lax.dynamic_update_index_in_dim(result, part, (digit + hop) % count, 0)
    return result.reshape(count * x.shape[0], *x.shape[1:])


def ring_sum(x, ring):
    axis, stride, count = ring
    one, two, three = (partners(x, axis, stride, count, hop) for hop in (1, 2, 3))
    return (x + two) + (one + three)


def in_order(x):
    parts = x.reshape(X[2], CORE[2], -1, x.shape[1])
    return jnp.swapaxes(parts, 0, 1).reshape(x.shape)


def after(value, *others):
    return lax.optimization_barrier((value, *others))[0]


def tied(*values):
    return lax.optimization_barrier(values)


def side_by_side(*parts):
    return jnp.concatenate(parts, axis=2)


def local(objects, probe_field, propagator_phase, patterns, offset_row, offset_column, live_counts):
    width = probe_field.shape[-1]
    tile_rows, tile_cols = objects.shape[1:]
    slots = patterns.shape[2]
    inside_lower = (lax.axis_index("band") < lax.axis_size("band") - 1).astype(f32)
    inside_right = (lax.axis_index("scan") < lax.axis_size("scan") - 1).astype(f32)
    scale = jnp.stack([inside_right, inside_lower])
    mats = jnp.asarray(tables())
    index = np.arange(SIDE)
    order = np.concatenate([np.arange(0, SIDE, 2), np.arange(1, SIDE, 2)])
    swap = (index[:, None] == order[None, :]).astype(ml_dtypes.bfloat16)
    swap = jnp.asarray(np.stack([swap, swap.T]))

    spots = (offset_row[0], offset_column[0], scale)
    live_here = live_counts[0]

    own_one, own_two = objects[:2], objects[2:]
    lower = shifted(jnp.concatenate([own_two, own_one]), "band", -1)
    right_one = shifted(own_one[:, :, :width], "scan", -1)
    right_two = shifted(own_two[:, :, :width], "scan", -1)
    lower_two, lower_one = lower[:2], lower[2:]
    images = jnp.concatenate(
        [patterns[0, 0], jnp.cos(propagator_phase)[None], jnp.sin(propagator_phase)[None]]
    )
    ordered = order_call(slots + 2)(images, swap)
    corner_one = shifted(after(right_one, ordered), "band", -1)
    corner_two = shifted(right_two, "band", -1)
    probe = probe_field

    def moved_probe(probe, summed, total):
        halves_of = summed.reshape(2, 2, width, width // 2)
        summed = side_by_side(halves_of[:, 0], halves_of[:, 1])
        moved = probe - probe_rate / total * summed
        power = jnp.sum(moved * moved)
        return moved * jnp.sqrt(width * width / (power + power_eps))

    def base_of(own, right, lower, corner, top, bottom):
        rate = object_rate
        upper = side_by_side(
            own - rate * top[:, :, :tile_cols],
            right - (rate * inside_right) * top[:, :, tile_cols:],
        )
        under = side_by_side(
            lower - (rate * inside_lower) * bottom[:, :, :tile_cols],
            corner - (rate * inside_lower * inside_right) * bottom[:, :, tile_cols:],
        )
        return jnp.concatenate([upper, under], axis=1)

    psi, piece = spread_call(slots, "pieces")(
        *spots, objects, right_one, lower, corner_one, probe, ordered, mats
    )
    back, left, middle, right = misfit_call(slots, "pieces")(
        *spots, live_here, objects, right_two, lower, corner_two, psi, ordered, mats
    )
    upper, under = slice(0, tile_rows), slice(tile_rows, 2 * tile_rows)
    two_from_left = shifted(right, "scan", 1)
    two_from_right = shifted(left, "scan", -1)
    top, bottom, gprobe = first_call(slots, 4 * SIDE + 64)(
        *spots[:2], live_here, back, piece, probe, ordered, mats
    )
    one_from_above = shifted(bottom, "band", 1)
    one_from_below = shifted(top, "band", -1)
    share, two_from_left, two_from_right = tied(gprobe, two_from_left, two_from_right)
    share = scatter_sum(share, CORE)
    share = scatter_sum(share, X)
    share, one_from_above, one_from_below = tied(share, one_from_above, one_from_below)
    share = ring_sum(share, Y)
    share = ring_sum(share, Z)
    share = gather(share, CORE)
    one_left = jnp.concatenate(
        [
            top[:, :, :width] + one_from_above[:, :, :width],
            bottom[:, :, :width] + one_from_below[:, :, :width],
        ],
        axis=1,
    )
    one_right = jnp.concatenate(
        [
            top[:, :, tile_cols:] + one_from_above[:, :, tile_cols:],
            bottom[:, :, tile_cols:] + one_from_below[:, :, tile_cols:],
        ],
        axis=1,
    )
    share, one_left, one_right = tied(share, one_left, one_right)
    share = gather(share, X)
    one_from_left = shifted(after(one_right, share), "scan", 1)
    one_from_right = shifted(after(one_left, share), "scan", -1)
    both = in_order(share)
    total = both[-1, 0]
    left, middle, right, both = tied(left, middle, right, both)
    two_ends = [
        side_by_side(
            left[:, part] + two_from_left[:, part],
            middle[:, part],
            right[:, part] + two_from_right[:, part],
        )
        for part in (upper, under)
    ]
    two_from_above = shifted(two_ends[1], "band", 1)
    two_from_below = shifted(two_ends[0], "band", -1)
    probe = moved_probe(probe, both[: 4 * width], total)
    top, bottom, probe = tied(top, bottom, probe)
    base_one = base_of(
        own_one, right_one, lower_one, corner_one, top + one_from_above, bottom + one_from_below
    )
    base_two = base_of(own_two, right_two, lower_two, corner_two, *two_ends)

    psi, piece, own_one = spread_call(slots, "sides")(
        *spots, base_one, one_from_left, one_from_right, probe, ordered, mats
    )
    back, left, middle, right, own_two = misfit_call(slots, "ends")(
        *spots, live_here, base_two, two_from_above, two_from_below, psi, ordered, mats
    )
    two_from_left = shifted(right, "scan", 1)
    top, bottom, gprobe = first_call(slots, 4 * SIDE)(
        *spots[:2], live_here, back, piece, probe, ordered, mats
    )
    one_from_above = shifted(bottom, "band", 1)
    share, two_from_left = tied(gprobe, two_from_left)
    share = scatter_sum(share, CORE)
    share = scatter_sum(share, X)
    two_bottom = side_by_side(left[:, under] + two_from_left[:, under], middle[:, under])
    two_from_above = shifted(two_bottom, "band", 1)
    share = ring_sum(share, Y)
    share, one_from_above = tied(share, one_from_above)
    share = gather(share, X)
    one_right = top[:, :, tile_cols:] + one_from_above[:, :, tile_cols:]
    one_from_left = shifted(after(one_right, share), "scan", 1)
    share, two_from_above = tied(share, two_from_above)
    share = ring_sum(share, Z)
    share, one_from_left = tied(share, one_from_left)
    probe = moved_probe(probe, gather(share, CORE), total)
    top = top + one_from_above
    two_top = side_by_side(left[:, upper] + two_from_left[:, upper], middle[:, upper])

    own_one = own_one - object_rate * side_by_side(
        top[:, :, :width] + one_from_left, top[:, :, width:tile_cols]
    )
    own_two = own_two - object_rate * (two_top + two_from_above)
    return (jnp.concatenate([own_one, own_two]), probe)


def solution(mesh):
    return jax.shard_map(
        local,
        mesh=mesh,
        in_specs=(
            P(None, "band", "scan"),
            P(),
            P(),
            P("band", "scan", None, None, None),
            P("band", "scan"),
            P("band", "scan"),
            P("band", "scan"),
        ),
        out_specs=(P(None, "band", "scan"), P()),
        check_vma=False,
    )
```

```python
import functools
import math

import jax
import jax.numpy as jnp
import ml_dtypes
import numpy as np
from jax import lax
from jax.experimental import pallas as pl
from jax.experimental.pallas import tpu as pltpu
from jax.sharding import PartitionSpec as P

ITERS = 2
SIDE = 256
HALF = SIDE // 2
TALL = 264
WIDE = 384

object_rate = 0.1
probe_rate = 2.0
power_eps = 1e-06

f32 = jnp.float32
bf16 = jnp.bfloat16


def halves(matrix):
    high = matrix.astype(ml_dtypes.bfloat16)
    low = (matrix - high.astype(np.float64)).astype(ml_dtypes.bfloat16)
    return [high, low]


def tables():
    point = np.arange(HALF)[None, :]
    result = []
    for parity in (0, 1):
        frequency = 2 * np.arange(HALF)[:, None] + parity
        angle = -2.0 * np.pi / SIDE * (frequency * point % SIDE)
        real = np.cos(angle) / math.sqrt(SIDE)
        imag = np.sin(angle) / math.sqrt(SIDE)
        matrix = np.block([[real, -imag], [imag, real]])
        result += halves(matrix) + halves(matrix.T)
    return np.stack(result)


E_HI, E_LO, ET_HI, ET_LO, O_HI, O_LO, OT_HI, OT_LO = range(8)


def dot(a, b):
    return jnp.dot(a, b, preferred_element_type=f32)


def split(x):
    high = x.astype(bf16)
    low = (x - high.astype(f32)).astype(bf16)
    return high, low


def mul_left(m, hi, x):
    high, low = split(x)
    return dot(m[hi], high) + dot(m[hi], low) + dot(m[hi + 1], high)


def mul_right(x, m, hi):
    high, low = split(x)
    return dot(high, m[hi]) + dot(low, m[hi]) + dot(high, m[hi + 1])


def rows(*parts):
    return jnp.concatenate(parts, axis=0)


def cols(*parts):
    return jnp.concatenate(parts, axis=1)


def forward(re, im, m):
    even = mul_left(m, E_HI, rows(re[:HALF] + re[HALF:], im[:HALF] + im[HALF:]))
    odd = mul_left(m, O_HI, rows(re[:HALF] - re[HALF:], im[:HALF] - im[HALF:]))
    re = rows(even[:HALF], odd[:HALF])
    im = rows(even[HALF:], odd[HALF:])
    u = mul_right(cols(re[:, :HALF] + re[:, HALF:], im[:, :HALF] + im[:, HALF:]), m, ET_HI)
    v = mul_right(cols(re[:, :HALF] - re[:, HALF:], im[:, :HALF] - im[:, HALF:]), m, OT_HI)
    return u, v


def backward(u, v, m):
    a = mul_right(u, m, E_HI)
    b = mul_right(v, m, O_HI)
    re = cols(a[:, :HALF] + b[:, :HALF], a[:, :HALF] - b[:, :HALF])
    im = cols(a[:, HALF:] + b[:, HALF:], a[:, HALF:] - b[:, HALF:])
    a = mul_left(m, ET_HI, rows(re[:HALF], im[:HALF]))
    b = mul_left(m, OT_HI, rows(re[HALF:], im[HALF:]))
    re = rows(a[:HALF] + b[:HALF], a[:HALF] - b[:HALF])
    im = rows(a[HALF:] + b[HALF:], a[HALF:] - b[HALF:])
    return re, im


def by_kernel(u, h, place, sign):
    re, im = u[:, :HALF], u[:, HALF:]
    hr = h[0, :, place * HALF : (place + 1) * HALF]
    hi = h[1, :, place * HALF : (place + 1) * HALF]
    if sign > 0:
        return cols(hr * re - hi * im, hr * im + hi * re)
    return cols(hr * re + hi * im, hr * im - hi * re)


def window(ext, plane, spot):
    row0, row_rest, col0, col_rest = spot
    slab = ext[plane, pl.ds(row0, TALL), pl.ds(col0, WIDE)]
    slab = pltpu.roll(slab, lax.rem(WIDE - col_rest, WIDE), 1)[:, :SIDE]
    return pltpu.roll(slab, lax.rem(TALL - row_rest, TALL), 0)[:SIDE]


def place(row_ref, col_ref, slot):
    row = row_ref[slot]
    col = col_ref[slot]
    row_rest = lax.rem(row, 8)
    col_rest = lax.rem(col, 128)
    row0 = pl.multiple_of(row - row_rest, 8)
    col0 = pl.multiple_of(col - col_rest, 128)
    return row0, row_rest, col0, col_rest


def join_pieces(ext, scale, own, right, lower, corner):
    tile_rows, tile_cols = own.shape[1:]
    ext[:, :tile_rows, :tile_cols] = own[...]
    ext[:, :tile_rows, tile_cols:] = right[...]
    ext[:, tile_rows:, :tile_cols] = lower[...]
    ext[:, tile_rows:, tile_cols:] = corner[...]


def join_sides(ext, scale, base, from_left, from_right):
    inside_right, inside_lower = scale[0], scale[1]
    for rows_at, factor in ((0, object_rate), (SIDE, object_rate * inside_lower)):
        at = pl.ds(rows_at, SIDE)
        ext[:, at, :SIDE] = base[:, at, :SIDE] - factor * from_left[:, at]
        ext[:, at, SIDE : 2 * SIDE] = base[:, at, SIDE : 2 * SIDE]
        ext[:, at, 2 * SIDE :] = base[:, at, 2 * SIDE :] - factor * inside_right * from_right[:, at]


def join_ends(ext, scale, base, from_above, from_below):
    inside_right, inside_lower = scale[0], scale[1]
    for rows_at, come, factor in (
        (0, from_above, object_rate),
        (SIDE, from_below, object_rate * inside_lower),
    ):
        at = pl.ds(rows_at, SIDE)
        ext[:, at, : 2 * SIDE] = base[:, at, : 2 * SIDE] - factor * come[:, :, : 2 * SIDE]
        ext[:, at, 2 * SIDE :] = (
            base[:, at, 2 * SIDE :] - factor * inside_right * come[:, :, 2 * SIDE :]
        )


def spread_kernel(join, count, row_ref, col_ref, scale, *refs):
    slot = pl.program_id(0)
    parts, (probe, h, m, psi, piece, *rest) = refs[:count], refs[count:]
    own, ext = rest if len(rest) == 2 else (None, rest[0])

    @pl.when(slot == 0)
    def _():
        join(ext, scale, *parts)
        if own is not None:
            own[...] = ext[:, : own.shape[1], : own.shape[2]]

    for k in range(PER):
        spot = place(row_ref, col_ref, slot * PER + k)
        ar = window(ext, 0, spot)
        ai = window(ext, 1, spot)
        piece[k, 0] = ar
        piece[k, 1] = ai
        pr, pi = probe[0], probe[1]
        u, v = forward(pr * ar - pi * ai, pr * ai + pi * ar, m)
        re, im = backward(by_kernel(u, h, 0, 1), by_kernel(v, h, 1, 1), m)
        psi[k, 0] = re
        psi[k, 1] = im


def add_window(accum, plane, grad, spot):
    row0, row_rest, col0, col_rest = spot
    tall = rows(grad, jnp.zeros((TALL - SIDE, SIDE), f32))
    tall = pltpu.roll(tall, row_rest, 0)
    wide = cols(tall, jnp.zeros((TALL, WIDE - SIDE), f32))
    wide = pltpu.roll(wide, col_rest, 1)
    accum[plane, pl.ds(row0, TALL), pl.ds(col0, WIDE)] += wide


def misfit_kernel(join, count, row_ref, col_ref, scale, live_ref, *refs):
    slot = pl.program_id(0)
    parts, (psi, pattern, m, back, left, mid, right, *rest) = refs[:count], refs[count:]
    own, ext, accum = rest if len(rest) == 3 else (None, *rest)

    @pl.when(slot == 0)
    def _():
        join(ext, scale, *parts)
        if own is not None:
            own[...] = ext[:, : own.shape[1], : own.shape[2]]
        accum[...] = jnp.zeros_like(accum)

    for k in range(PER):
        spot = place(row_ref, col_ref, slot * PER + k)
        ar = window(ext, 0, spot)
        ai = window(ext, 1, spot)
        sr, si = psi[k, 0], psi[k, 1]
        u, v = forward(sr * ar - si * ai, sr * ai + si * ar, m)
        live = (slot * PER + k < live_ref[0]).astype(f32)

        def weigh(part, measured):
            re, im = part[:, :HALF], part[:, HALF:]
            weight = (re * re + im * im - measured) * live
            return cols(weight * re, weight * im)

        u = weigh(u, pattern[k, :, :HALF])
        v = weigh(v, pattern[k, :, HALF:])
        re, im = backward(u, v, m)
        back[k, 0] = ar * re + ai * im
        back[k, 1] = ar * im - ai * re
        add_window(accum, 0, sr * re + si * im, spot)
        add_window(accum, 1, sr * im - si * re, spot)

    @pl.when(slot == pl.num_programs(0) - 1)
    def _():
        left[...] = accum[:, :, :SIDE]
        mid[...] = accum[:, :, SIDE : 2 * SIDE]
        right[...] = accum[:, :, 2 * SIDE :]


def first_kernel(
    row_ref, col_ref, live_ref, back, piece, probe, h, m, top, bottom, gprobe, accum
):
    slot = pl.program_id(0)

    @pl.when(slot == 0)
    def _():
        accum[...] = jnp.zeros_like(accum)
        gprobe[: 4 * SIDE] = jnp.zeros((4 * SIDE, HALF), f32)
        if gprobe.shape[0] > 4 * SIDE:
            live = jnp.minimum(live_ref[0], PER * pl.num_programs(0)).astype(f32)
            gprobe[4 * SIDE :] = jnp.full((gprobe.shape[0] - 4 * SIDE, HALF), live)

    for k in range(PER):
        spot = place(row_ref, col_ref, slot * PER + k)
        u, v = forward(back[k, 0], back[k, 1], m)
        re, im = backward(by_kernel(u, h, 0, -1), by_kernel(v, h, 1, -1), m)
        ar, ai = piece[k, 0], piece[k, 1]
        for at, value in enumerate((ar * re + ai * im, ar * im - ai * re)):
            for side in (0, 1):
                part = value[:, side * HALF : (side + 1) * HALF]
                gprobe[(2 * at + side) * SIDE : (2 * at + side + 1) * SIDE] += part
        pr, pi = probe[0], probe[1]
        add_window(accum, 0, pr * re + pi * im, spot)
        add_window(accum, 1, pr * im - pi * re, spot)

    @pl.when(slot == pl.num_programs(0) - 1)
    def _():
        top[...] = accum[:, :SIDE]
        bottom[...] = accum[:, SIDE:]


def picked(value, move):
    total = None
    for _ in range(3):
        part = value.astype(bf16)
        value = value - part.astype(f32)
        moved = move(part)
        total = moved if total is None else total + moved
    return total


def order_kernel(x, swap, out):
    value = picked(x[0], lambda part: dot(part, swap[0]))
    out[0] = picked(value, lambda part: dot(swap[1], part))


SMEM = pl.BlockSpec(memory_space=pltpu.SMEM)


def whole(shape):
    return pl.BlockSpec(shape, lambda i: (0,) * len(shape))


PER = 1


def per_slot(shape):
    return pl.BlockSpec((PER,) + shape, lambda i: (i,) + (0,) * len(shape))


def call(kernel, name, slots, in_specs, out_specs, out_shape, scratch, flops, size):
    return pl.pallas_call(
        kernel,
        name=name,
        grid=(slots // PER,),
        in_specs=in_specs,
        out_specs=out_specs,
        out_shape=out_shape,
        scratch_shapes=scratch,
        compiler_params=pltpu.CompilerParams(vmem_limit_bytes=32 * 1024 * 1024),
        cost_estimate=pl.CostEstimate(flops=flops, bytes_accessed=size, transcendentals=0),
    )


def shape(*dims):
    return jax.ShapeDtypeStruct(dims, f32)


FIELD = (2, SIDE, SIDE)
MATS = (8, SIDE, SIDE)
EXT = (2, 2 * SIDE, 3 * SIDE)
OWN = (2, SIDE, 2 * SIDE)
SIDES = (2, 2 * SIDE, SIDE)
ENDS = (2, SIDE, 3 * SIDE)
JOINS = {
    "pieces": (join_pieces, [OWN, FIELD, OWN, FIELD]),
    "sides": (join_sides, [EXT, SIDES, SIDES]),
    "ends": (join_ends, [EXT, ENDS, ENDS]),
}
TWO_TRANSFORMS = 24 * 2 * SIDE**3


def specs(shapes):
    return [whole(dims) for dims in shapes]


def two_planes(dims, which):
    return pl.BlockSpec(dims, lambda i: (which, 0, 0))


def part_specs(how, parts, which):
    if how != "pieces":
        return specs(parts)
    return [
        two_planes(parts[0], which),
        whole(parts[1]),
        two_planes(parts[2], 1 - which),
        whole(parts[3]),
    ]


def shapes_of(shapes):
    return [shape(*dims) for dims in shapes]


KERNEL = pl.BlockSpec(FIELD, lambda i: (2, 0, 0))


def spread_call(slots, how):
    join, parts = JOINS[how]
    extra = [OWN] if how != "pieces" else []
    return call(
        functools.partial(spread_kernel, join, len(parts)), "spread", slots,
        [SMEM, SMEM, SMEM, *part_specs(how, parts, 0), whole(FIELD), KERNEL, whole(MATS)],
        [per_slot(FIELD), per_slot(FIELD), *specs(extra)],
        [shape(slots, *FIELD), shape(slots, *FIELD), *shapes_of(extra)],
        [pltpu.VMEM(EXT, f32)],
        slots * TWO_TRANSFORMS, 9 << 20,
    )


def misfit_call(slots, how):
    join, parts = JOINS[how]
    extra = [OWN] if how != "pieces" else []
    return call(
        functools.partial(misfit_kernel, join, len(parts)), "misfit", slots,
        [SMEM, SMEM, SMEM, SMEM, *part_specs(how, parts, 1), per_slot(FIELD), per_slot((SIDE, SIDE)), whole(MATS)],
        [per_slot(FIELD), *specs([SIDES] * 3 + extra)],
        [shape(slots, *FIELD), *shapes_of([SIDES] * 3 + extra)],
        [pltpu.VMEM(EXT, f32), pltpu.VMEM(EXT, f32)],
        slots * TWO_TRANSFORMS, 12 << 20,
    )


def first_call(slots, sum_rows):
    return call(
        first_kernel, "first", slots,
        [SMEM, SMEM, SMEM, per_slot(FIELD), per_slot(FIELD), whole(FIELD), KERNEL, whole(MATS)],
        specs([ENDS, ENDS, (sum_rows, HALF)]),
        shapes_of([ENDS, ENDS, (sum_rows, HALF)]),
        [pltpu.VMEM(EXT, f32)],
        slots * TWO_TRANSFORMS, 9 << 20,
    )


def order_call(count):
    return call(
        order_kernel, "order", count * PER,
        [pl.BlockSpec((1, SIDE, SIDE), lambda i: (i, 0, 0)), whole((2, SIDE, SIDE))],
        pl.BlockSpec((1, SIDE, SIDE), lambda i: (i, 0, 0)),
        shape(count, SIDE, SIDE),
        [],
        count * 12 * SIDE**3, 4 << 20,
    )


def shifted(block, axis, distance):
    devices = range(lax.axis_size(axis))
    route = [(i - distance, i) for i in devices if i - distance in devices]
    return lax.ppermute(block, axis, route)


def partners(block, axis, stride, count, hop):
    route = []
    for i in range(lax.axis_size(axis)):
        digit = i // stride % count
        j = i + ((digit - hop) % count - digit) * stride
        route.append((i, j))
    return lax.ppermute(block, axis, route)


CORE, Z, X, Y = ("band", 1, 2), ("band", 2, 4), ("scan", 1, 4), ("scan", 4, 4)


def scatter_sum(x, ring):
    axis, stride, count = ring
    digit = lax.axis_index(axis) // stride % count
    parts = x.reshape(count, x.shape[0] // count, *x.shape[1:])
    total = lax.dynamic_index_in_dim(parts, digit, 0, False)
    for hop in range(1, count):
        sent = lax.dynamic_index_in_dim(parts, (digit - hop) % count, 0, False)
        total = total + partners(sent, axis, stride, count, hop)
    return total


def gather(x, ring):
    axis, stride, count = ring
    digit = lax.axis_index(axis) // stride % count
    result = jnp.zeros((count, *x.shape), f32)
    result = lax.dynamic_update_index_in_dim(result, x, digit, 0)
    for hop in range(1, count):
        part = partners(x, axis, stride, count, hop)
        result = lax.dynamic_update_index_in_dim(result, part, (digit + hop) % count, 0)
    return result.reshape(count * x.shape[0], *x.shape[1:])


def ring_sum(x, ring):
    axis, stride, count = ring
    one, two, three = (partners(x, axis, stride, count, hop) for hop in (1, 2, 3))
    return (x + two) + (one + three)


def in_order(x):
    parts = x.reshape(X[2], CORE[2], -1, x.shape[1])
    return jnp.swapaxes(parts, 0, 1).reshape(x.shape)


def after(value, *others):
    return lax.optimization_barrier((value, *others))[0]


def tied(*values):
    return lax.optimization_barrier(values)


def side_by_side(*parts):
    return jnp.concatenate(parts, axis=2)


def local(objects, probe_field, propagator_phase, patterns, offset_row, offset_column, live_counts):
    width = probe_field.shape[-1]
    tile_rows, tile_cols = objects.shape[1:]
    slots = patterns.shape[2]
    inside_lower = (lax.axis_index("band") < lax.axis_size("band") - 1).astype(f32)
    inside_right = (lax.axis_index("scan") < lax.axis_size("scan") - 1).astype(f32)
    scale = jnp.stack([inside_right, inside_lower])
    mats = jnp.asarray(tables())
    index = np.arange(SIDE)
    order = np.concatenate([np.arange(0, SIDE, 2), np.arange(1, SIDE, 2)])
    swap = (index[:, None] == order[None, :]).astype(ml_dtypes.bfloat16)
    swap = jnp.asarray(np.stack([swap, swap.T]))

    spots = (offset_row[0], offset_column[0], scale)
    live_here = live_counts[0]

    own_one, own_two = objects[:2], objects[2:]
    lower = shifted(jnp.concatenate([own_two, own_one]), "band", -1)
    right_one = shifted(own_one[:, :, :width], "scan", -1)
    right_two = shifted(own_two[:, :, :width], "scan", -1)
    lower_two, lower_one = lower[:2], lower[2:]
    images = jnp.concatenate(
        [patterns[0, 0], jnp.cos(propagator_phase)[None], jnp.sin(propagator_phase)[None]]
    )
    ordered = order_call(slots + 2)(images, swap)
    corner_one = shifted(after(right_one, ordered), "band", -1)
    corner_two = shifted(right_two, "band", -1)
    probe = probe_field

    def moved_probe(probe, summed, total):
        halves_of = summed.reshape(2, 2, width, width // 2)
        summed = side_by_side(halves_of[:, 0], halves_of[:, 1])
        moved = probe - probe_rate / total * summed
        power = jnp.sum(moved * moved)
        return moved * jnp.sqrt(width * width / (power + power_eps))

    def base_of(own, right, lower, corner, top, bottom):
        rate = object_rate
        upper = side_by_side(
            own - rate * top[:, :, :tile_cols],
            right - (rate * inside_right) * top[:, :, tile_cols:],
        )
        under = side_by_side(
            lower - (rate * inside_lower) * bottom[:, :, :tile_cols],
            corner - (rate * inside_lower * inside_right) * bottom[:, :, tile_cols:],
        )
        return jnp.concatenate([upper, under], axis=1)

    psi, piece = spread_call(slots, "pieces")(
        *spots, objects, right_one, lower, corner_one, probe, ordered, mats
    )
    back, left, middle, right = misfit_call(slots, "pieces")(
        *spots, live_here, objects, right_two, lower, corner_two, psi, ordered, mats
    )
    upper, under = slice(0, tile_rows), slice(tile_rows, 2 * tile_rows)
    two_from_left = shifted(right, "scan", 1)
    two_from_right = shifted(left, "scan", -1)
    top, bottom, gprobe = first_call(slots, 4 * SIDE + 64)(
        *spots[:2], live_here, back, piece, probe, ordered, mats
    )
    one_from_above = shifted(bottom, "band", 1)
    one_from_below = shifted(top, "band", -1)
    share, two_from_left, two_from_right = tied(gprobe, two_from_left, two_from_right)
    share = scatter_sum(share, CORE)
    share = scatter_sum(share, X)
    share, one_from_above, one_from_below = tied(share, one_from_above, one_from_below)
    share = ring_sum(share, Y)
    share = ring_sum(share, Z)
    share = gather(share, CORE)
    one_left = jnp.concatenate(
        [
            top[:, :, :width] + one_from_above[:, :, :width],
            bottom[:, :, :width] + one_from_below[:, :, :width],
        ],
        axis=1,
    )
    one_right = jnp.concatenate(
        [
            top[:, :, tile_cols:] + one_from_above[:, :, tile_cols:],
            bottom[:, :, tile_cols:] + one_from_below[:, :, tile_cols:],
        ],
        axis=1,
    )
    share, one_left, one_right = tied(share, one_left, one_right)
    share = gather(share, X)
    one_from_left = shifted(after(one_right, share), "scan", 1)
    one_from_right = shifted(after(one_left, share), "scan", -1)
    both = in_order(share)
    total = both[-1, 0]
    left, middle, right, both = tied(left, middle, right, both)
    two_ends = [
        side_by_side(
            left[:, part] + two_from_left[:, part],
            middle[:, part],
            right[:, part] + two_from_right[:, part],
        )
        for part in (upper, under)
    ]
    two_from_above = shifted(two_ends[1], "band", 1)
    two_from_below = shifted(two_ends[0], "band", -1)
    probe = moved_probe(probe, both[: 4 * width], total)
    top, bottom, probe = tied(top, bottom, probe)
    base_one = base_of(
        own_one, right_one, lower_one, corner_one, top + one_from_above, bottom + one_from_below
    )
    base_two = base_of(own_two, right_two, lower_two, corner_two, *two_ends)

    psi, piece, own_one = spread_call(slots, "sides")(
        *spots, base_one, one_from_left, one_from_right, probe, ordered, mats
    )
    back, left, middle, right, own_two = misfit_call(slots, "ends")(
        *spots, live_here, base_two, two_from_above, two_from_below, psi, ordered, mats
    )
    two_from_left = shifted(right, "scan", 1)
    top, bottom, gprobe = first_call(slots, 4 * SIDE)(
        *spots[:2], live_here, back, piece, probe, ordered, mats
    )
    one_from_above = shifted(bottom, "band", 1)
    share, two_from_left = tied(gprobe, two_from_left)
    share = scatter_sum(share, CORE)
    share = scatter_sum(share, X)
    two_bottom = side_by_side(left[:, under] + two_from_left[:, under], middle[:, under])
    two_from_above = shifted(two_bottom, "band", 1)
    share = ring_sum(share, Y)
    share, one_from_above = tied(share, one_from_above)
    share = gather(share, X)
    one_right = top[:, :, tile_cols:] + one_from_above[:, :, tile_cols:]
    one_from_left = shifted(after(one_right, share), "scan", 1)
    share, two_from_above = tied(share, two_from_above)
    share = ring_sum(share, Z)
    share, one_from_left = tied(share, one_from_left)
    probe = moved_probe(probe, gather(share, CORE), total)
    top = top + one_from_above
    two_top = side_by_side(left[:, upper] + two_from_left[:, upper], middle[:, upper])

    own_one = own_one - object_rate * side_by_side(
        top[:, :, :width] + one_from_left, top[:, :, width:tile_cols]
    )
    own_two = own_two - object_rate * (two_top + two_from_above)
    return (jnp.concatenate([own_one, own_two]), probe)


def solution(mesh):
    return jax.shard_map(
        local,
        mesh=mesh,
        in_specs=(
            P(None, "band", "scan"),
            P(),
            P(),
            P("band", "scan", None, None, None),
            P("band", "scan"),
            P("band", "scan"),
            P("band", "scan"),
        ),
        out_specs=(P(None, "band", "scan"), P()),
        check_vma=False,
    )
```

```python
import functools
import math

import jax
import jax.numpy as jnp
import ml_dtypes
import numpy as np
from jax import lax
from jax.experimental import pallas as pl
from jax.experimental.pallas import tpu as pltpu
from jax.sharding import PartitionSpec as P

ITERS = 2
SIDE = 256
HALF = SIDE // 2
TALL = 264
WIDE = 384

object_rate = 0.1
probe_rate = 2.0
power_eps = 1e-06

f32 = jnp.float32
bf16 = jnp.bfloat16


def halves(matrix):
    high = matrix.astype(ml_dtypes.bfloat16)
    low = (matrix - high.astype(np.float64)).astype(ml_dtypes.bfloat16)
    return [high, low]


def tables():
    point = np.arange(HALF)[None, :]
    result = []
    for parity in (0, 1):
        frequency = 2 * np.arange(HALF)[:, None] + parity
        angle = -2.0 * np.pi / SIDE * (frequency * point % SIDE)
        real = np.cos(angle) / math.sqrt(SIDE)
        imag = np.sin(angle) / math.sqrt(SIDE)
        matrix = np.block([[real, -imag], [imag, real]])
        result += halves(matrix) + halves(matrix.T)
    return np.stack(result)


E_HI, E_LO, ET_HI, ET_LO, O_HI, O_LO, OT_HI, OT_LO = range(8)


def dot(a, b):
    return jnp.dot(a, b, preferred_element_type=f32)


def split(x):
    high = x.astype(bf16)
    low = (x - high.astype(f32)).astype(bf16)
    return high, low


def mul_left(m, hi, x):
    high, low = split(x)
    return dot(m[hi], high) + dot(m[hi], low) + dot(m[hi + 1], high)


def mul_right(x, m, hi):
    high, low = split(x)
    return dot(high, m[hi]) + dot(low, m[hi]) + dot(high, m[hi + 1])


def rows(*parts):
    return jnp.concatenate(parts, axis=0)


def cols(*parts):
    return jnp.concatenate(parts, axis=1)


def forward(re, im, m):
    even = mul_left(m, E_HI, rows(re[:HALF] + re[HALF:], im[:HALF] + im[HALF:]))
    odd = mul_left(m, O_HI, rows(re[:HALF] - re[HALF:], im[:HALF] - im[HALF:]))
    re = rows(even[:HALF], odd[:HALF])
    im = rows(even[HALF:], odd[HALF:])
    u = mul_right(cols(re[:, :HALF] + re[:, HALF:], im[:, :HALF] + im[:, HALF:]), m, ET_HI)
    v = mul_right(cols(re[:, :HALF] - re[:, HALF:], im[:, :HALF] - im[:, HALF:]), m, OT_HI)
    return u, v


def backward(u, v, m):
    a = mul_right(u, m, E_HI)
    b = mul_right(v, m, O_HI)
    re = cols(a[:, :HALF] + b[:, :HALF], a[:, :HALF] - b[:, :HALF])
    im = cols(a[:, HALF:] + b[:, HALF:], a[:, HALF:] - b[:, HALF:])
    a = mul_left(m, ET_HI, rows(re[:HALF], im[:HALF]))
    b = mul_left(m, OT_HI, rows(re[HALF:], im[HALF:]))
    re = rows(a[:HALF] + b[:HALF], a[:HALF] - b[:HALF])
    im = rows(a[HALF:] + b[HALF:], a[HALF:] - b[HALF:])
    return re, im


def by_kernel(u, h, place, sign):
    re, im = u[:, :HALF], u[:, HALF:]
    hr = h[0, :, place * HALF : (place + 1) * HALF]
    hi = h[1, :, place * HALF : (place + 1) * HALF]
    if sign > 0:
        return cols(hr * re - hi * im, hr * im + hi * re)
    return cols(hr * re + hi * im, hr * im - hi * re)


def window(ext, plane, spot):
    row0, row_rest, col0, col_rest = spot
    slab = ext[plane, pl.ds(row0, TALL), pl.ds(col0, WIDE)]
    slab = pltpu.roll(slab, lax.rem(WIDE - col_rest, WIDE), 1)[:, :SIDE]
    return pltpu.roll(slab, lax.rem(TALL - row_rest, TALL), 0)[:SIDE]


def place(row_ref, col_ref, slot):
    row = row_ref[slot]
    col = col_ref[slot]
    row_rest = lax.rem(row, 8)
    col_rest = lax.rem(col, 128)
    row0 = pl.multiple_of(row - row_rest, 8)
    col0 = pl.multiple_of(col - col_rest, 128)
    return row0, row_rest, col0, col_rest


def join_pieces(ext, scale, own, right, lower, corner):
    tile_rows, tile_cols = own.shape[1:]
    ext[:, :tile_rows, :tile_cols] = own[...]
    ext[:, :tile_rows, tile_cols:] = right[...]
    ext[:, tile_rows:, :tile_cols] = lower[...]
    ext[:, tile_rows:, tile_cols:] = corner[...]


def join_sides(ext, scale, base, from_left, from_right):
    inside_right, inside_lower = scale[0], scale[1]
    for rows_at, factor in ((0, object_rate), (SIDE, object_rate * inside_lower)):
        at = pl.ds(rows_at, SIDE)
        ext[:, at, :SIDE] = base[:, at, :SIDE] - factor * from_left[:, at]
        ext[:, at, SIDE : 2 * SIDE] = base[:, at, SIDE : 2 * SIDE]
        ext[:, at, 2 * SIDE :] = base[:, at, 2 * SIDE :] - factor * inside_right * from_right[:, at]


def join_ends(ext, scale, base, from_above, from_below):
    inside_right, inside_lower = scale[0], scale[1]
    for rows_at, come, factor in (
        (0, from_above, object_rate),
        (SIDE, from_below, object_rate * inside_lower),
    ):
        at = pl.ds(rows_at, SIDE)
        ext[:, at, : 2 * SIDE] = base[:, at, : 2 * SIDE] - factor * come[:, :, : 2 * SIDE]
        ext[:, at, 2 * SIDE :] = (
            base[:, at, 2 * SIDE :] - factor * inside_right * come[:, :, 2 * SIDE :]
        )


def spread_kernel(join, count, row_ref, col_ref, scale, *refs):
    slot = pl.program_id(0)
    parts, (probe, h, m, psi, piece, *rest) = refs[:count], refs[count:]
    own, ext = rest if len(rest) == 2 else (None, rest[0])

    @pl.when(slot == 0)
    def _():
        join(ext, scale, *parts)
        if own is not None:
            own[...] = ext[:, : own.shape[1], : own.shape[2]]

    per = psi.shape[0]
    for k in range(per):
        spot = place(row_ref, col_ref, slot * per + k)
        ar = window(ext, 0, spot)
        ai = window(ext, 1, spot)
        piece[k, 0] = ar
        piece[k, 1] = ai
        pr, pi = probe[0], probe[1]
        u, v = forward(pr * ar - pi * ai, pr * ai + pi * ar, m)
        re, im = backward(by_kernel(u, h, 0, 1), by_kernel(v, h, 1, 1), m)
        psi[k, 0] = re
        psi[k, 1] = im


def add_window(accum, plane, grad, spot):
    row0, row_rest, col0, col_rest = spot
    tall = rows(grad, jnp.zeros((TALL - SIDE, SIDE), f32))
    tall = pltpu.roll(tall, row_rest, 0)
    wide = cols(tall, jnp.zeros((TALL, WIDE - SIDE), f32))
    wide = pltpu.roll(wide, col_rest, 1)
    accum[plane, pl.ds(row0, TALL), pl.ds(col0, WIDE)] += wide


def misfit_kernel(join, count, row_ref, col_ref, scale, live_ref, *refs):
    slot = pl.program_id(0)
    parts, (psi, pattern, m, back, left, mid, right, *rest) = refs[:count], refs[count:]
    own, ext, accum = rest if len(rest) == 3 else (None, *rest)

    @pl.when(slot == 0)
    def _():
        join(ext, scale, *parts)
        if own is not None:
            own[...] = ext[:, : own.shape[1], : own.shape[2]]
        accum[...] = jnp.zeros_like(accum)

    per = psi.shape[0]
    for k in range(per):
        spot = place(row_ref, col_ref, slot * per + k)
        ar = window(ext, 0, spot)
        ai = window(ext, 1, spot)
        sr, si = psi[k, 0], psi[k, 1]
        u, v = forward(sr * ar - si * ai, sr * ai + si * ar, m)
        live = (slot * per + k < live_ref[0]).astype(f32)

        def weigh(part, measured):
            re, im = part[:, :HALF], part[:, HALF:]
            weight = (re * re + im * im - measured) * live
            return cols(weight * re, weight * im)

        u = weigh(u, pattern[k, :, :HALF])
        v = weigh(v, pattern[k, :, HALF:])
        re, im = backward(u, v, m)
        back[k, 0] = ar * re + ai * im
        back[k, 1] = ar * im - ai * re
        add_window(accum, 0, sr * re + si * im, spot)
        add_window(accum, 1, sr * im - si * re, spot)

    @pl.when(slot == pl.num_programs(0) - 1)
    def _():
        left[...] = accum[:, :, :SIDE]
        mid[...] = accum[:, :, SIDE : 2 * SIDE]
        right[...] = accum[:, :, 2 * SIDE :]


def first_kernel(
    row_ref, col_ref, live_ref, back, piece, probe, h, m, top, bottom, gprobe, accum
):
    slot = pl.program_id(0)
    per = back.shape[0]

    @pl.when(slot == 0)
    def _():
        accum[...] = jnp.zeros_like(accum)
        gprobe[: 4 * SIDE] = jnp.zeros((4 * SIDE, HALF), f32)
        if gprobe.shape[0] > 4 * SIDE:
            live = jnp.minimum(live_ref[0], per * pl.num_programs(0)).astype(f32)
            gprobe[4 * SIDE :] = jnp.full((gprobe.shape[0] - 4 * SIDE, HALF), live)

    for k in range(per):
        spot = place(row_ref, col_ref, slot * per + k)
        u, v = forward(back[k, 0], back[k, 1], m)
        re, im = backward(by_kernel(u, h, 0, -1), by_kernel(v, h, 1, -1), m)
        ar, ai = piece[k, 0], piece[k, 1]
        for at, value in enumerate((ar * re + ai * im, ar * im - ai * re)):
            for side in (0, 1):
                part = value[:, side * HALF : (side + 1) * HALF]
                gprobe[(2 * at + side) * SIDE : (2 * at + side + 1) * SIDE] += part
        pr, pi = probe[0], probe[1]
        add_window(accum, 0, pr * re + pi * im, spot)
        add_window(accum, 1, pr * im - pi * re, spot)

    @pl.when(slot == pl.num_programs(0) - 1)
    def _():
        top[...] = accum[:, :SIDE]
        bottom[...] = accum[:, SIDE:]


def picked(value, move):
    total = None
    for _ in range(3):
        part = value.astype(bf16)
        value = value - part.astype(f32)
        moved = move(part)
        total = moved if total is None else total + moved
    return total


def order_kernel(x, swap, out):
    value = picked(x[0], lambda part: dot(part, swap[0]))
    out[0] = picked(value, lambda part: dot(swap[1], part))


SMEM = pl.BlockSpec(memory_space=pltpu.SMEM)


def whole(shape):
    return pl.BlockSpec(shape, lambda i: (0,) * len(shape))


def per_slot(shape, per=1):
    return pl.BlockSpec((per,) + shape, lambda i: (i,) + (0,) * len(shape))


def call(kernel, name, slots, in_specs, out_specs, out_shape, scratch, flops, size, per=1):
    return pl.pallas_call(
        kernel,
        name=name,
        grid=(slots // per,),
        in_specs=in_specs,
        out_specs=out_specs,
        out_shape=out_shape,
        scratch_shapes=scratch,
        compiler_params=pltpu.CompilerParams(vmem_limit_bytes=32 * 1024 * 1024),
        cost_estimate=pl.CostEstimate(flops=flops, bytes_accessed=size, transcendentals=0),
    )


def shape(*dims):
    return jax.ShapeDtypeStruct(dims, f32)


FIELD = (2, SIDE, SIDE)
MATS = (8, SIDE, SIDE)
EXT = (2, 2 * SIDE, 3 * SIDE)
OWN = (2, SIDE, 2 * SIDE)
SIDES = (2, 2 * SIDE, SIDE)
ENDS = (2, SIDE, 3 * SIDE)
JOINS = {
    "pieces": (join_pieces, [OWN, FIELD, OWN, FIELD]),
    "sides": (join_sides, [EXT, SIDES, SIDES]),
    "ends": (join_ends, [EXT, ENDS, ENDS]),
}
TWO_TRANSFORMS = 24 * 2 * SIDE**3


def specs(shapes):
    return [whole(dims) for dims in shapes]


def two_planes(dims, which):
    return pl.BlockSpec(dims, lambda i: (which, 0, 0))


def part_specs(how, parts, which):
    if how != "pieces":
        return specs(parts)
    return [
        two_planes(parts[0], which),
        whole(parts[1]),
        two_planes(parts[2], 1 - which),
        whole(parts[3]),
    ]


def shapes_of(shapes):
    return [shape(*dims) for dims in shapes]


KERNEL = pl.BlockSpec(FIELD, lambda i: (2, 0, 0))


SPREAD_STEP = {"pieces": 1, "sides": 2}
MISFIT_STEP = {"pieces": 2, "ends": 2}


def spread_call(slots, how):
    join, parts = JOINS[how]
    extra = [OWN] if how != "pieces" else []
    per = SPREAD_STEP[how]
    return call(
        functools.partial(spread_kernel, join, len(parts)), "spread", slots,
        [SMEM, SMEM, SMEM, *part_specs(how, parts, 0), whole(FIELD), KERNEL, whole(MATS)],
        [per_slot(FIELD, per), per_slot(FIELD, per), *specs(extra)],
        [shape(slots, *FIELD), shape(slots, *FIELD), *shapes_of(extra)],
        [pltpu.VMEM(EXT, f32)],
        slots * TWO_TRANSFORMS, 9 << 20, per,
    )


def misfit_call(slots, how):
    join, parts = JOINS[how]
    extra = [OWN] if how != "pieces" else []
    per = MISFIT_STEP[how]
    return call(
        functools.partial(misfit_kernel, join, len(parts)), "misfit", slots,
        [SMEM, SMEM, SMEM, SMEM, *part_specs(how, parts, 1), per_slot(FIELD, per), per_slot((SIDE, SIDE), per), whole(MATS)],
        [per_slot(FIELD, per), *specs([SIDES] * 3 + extra)],
        [shape(slots, *FIELD), *shapes_of([SIDES] * 3 + extra)],
        [pltpu.VMEM(EXT, f32), pltpu.VMEM(EXT, f32)],
        slots * TWO_TRANSFORMS, 12 << 20, per,
    )


def first_call(slots, sum_rows):
    return call(
        first_kernel, "first", slots,
        [SMEM, SMEM, SMEM, per_slot(FIELD), per_slot(FIELD), whole(FIELD), KERNEL, whole(MATS)],
        specs([ENDS, ENDS, (sum_rows, HALF)]),
        shapes_of([ENDS, ENDS, (sum_rows, HALF)]),
        [pltpu.VMEM(EXT, f32)],
        slots * TWO_TRANSFORMS, 9 << 20,
    )


def order_call(count):
    return call(
        order_kernel, "order", count,
        [pl.BlockSpec((1, SIDE, SIDE), lambda i: (i, 0, 0)), whole((2, SIDE, SIDE))],
        pl.BlockSpec((1, SIDE, SIDE), lambda i: (i, 0, 0)),
        shape(count, SIDE, SIDE),
        [],
        count * 12 * SIDE**3, 4 << 20,
    )


def shifted(block, axis, distance):
    devices = range(lax.axis_size(axis))
    route = [(i - distance, i) for i in devices if i - distance in devices]
    return lax.ppermute(block, axis, route)


def partners(block, axis, stride, count, hop):
    route = []
    for i in range(lax.axis_size(axis)):
        digit = i // stride % count
        j = i + ((digit - hop) % count - digit) * stride
        route.append((i, j))
    return lax.ppermute(block, axis, route)


CORE, Z, X, Y = ("band", 1, 2), ("band", 2, 4), ("scan", 1, 4), ("scan", 4, 4)


def scatter_sum(x, ring):
    axis, stride, count = ring
    digit = lax.axis_index(axis) // stride % count
    parts = x.reshape(count, x.shape[0] // count, *x.shape[1:])
    total = lax.dynamic_index_in_dim(parts, digit, 0, False)
    for hop in range(1, count):
        sent = lax.dynamic_index_in_dim(parts, (digit - hop) % count, 0, False)
        total = total + partners(sent, axis, stride, count, hop)
    return total


def gather(x, ring):
    axis, stride, count = ring
    digit = lax.axis_index(axis) // stride % count
    result = jnp.zeros((count, *x.shape), f32)
    result = lax.dynamic_update_index_in_dim(result, x, digit, 0)
    for hop in range(1, count):
        part = partners(x, axis, stride, count, hop)
        result = lax.dynamic_update_index_in_dim(result, part, (digit + hop) % count, 0)
    return result.reshape(count * x.shape[0], *x.shape[1:])


def ring_sum(x, ring):
    axis, stride, count = ring
    one, two, three = (partners(x, axis, stride, count, hop) for hop in (1, 2, 3))
    return (x + two) + (one + three)


def in_order(x):
    parts = x.reshape(X[2], CORE[2], -1, x.shape[1])
    return jnp.swapaxes(parts, 0, 1).reshape(x.shape)


def after(value, *others):
    return lax.optimization_barrier((value, *others))[0]


def tied(*values):
    return lax.optimization_barrier(values)


def side_by_side(*parts):
    return jnp.concatenate(parts, axis=2)


def local(objects, probe_field, propagator_phase, patterns, offset_row, offset_column, live_counts):
    width = probe_field.shape[-1]
    tile_rows, tile_cols = objects.shape[1:]
    slots = patterns.shape[2]
    inside_lower = (lax.axis_index("band") < lax.axis_size("band") - 1).astype(f32)
    inside_right = (lax.axis_index("scan") < lax.axis_size("scan") - 1).astype(f32)
    scale = jnp.stack([inside_right, inside_lower])
    mats = jnp.asarray(tables())
    index = np.arange(SIDE)
    order = np.concatenate([np.arange(0, SIDE, 2), np.arange(1, SIDE, 2)])
    swap = (index[:, None] == order[None, :]).astype(ml_dtypes.bfloat16)
    swap = jnp.asarray(np.stack([swap, swap.T]))

    spots = (offset_row[0], offset_column[0], scale)
    live_here = live_counts[0]

    own_one, own_two = objects[:2], objects[2:]
    lower = shifted(jnp.concatenate([own_two, own_one]), "band", -1)
    right_one = shifted(own_one[:, :, :width], "scan", -1)
    right_two = shifted(own_two[:, :, :width], "scan", -1)
    lower_two, lower_one = lower[:2], lower[2:]
    images = jnp.concatenate(
        [patterns[0, 0], jnp.cos(propagator_phase)[None], jnp.sin(propagator_phase)[None]]
    )
    ordered = order_call(slots + 2)(images, swap)
    corner_one = shifted(after(right_one, ordered), "band", -1)
    corner_two = shifted(right_two, "band", -1)
    probe = probe_field

    def moved_probe(probe, summed, total):
        halves_of = summed.reshape(2, 2, width, width // 2)
        summed = side_by_side(halves_of[:, 0], halves_of[:, 1])
        moved = probe - probe_rate / total * summed
        power = jnp.sum(moved * moved)
        return moved * jnp.sqrt(width * width / (power + power_eps))

    def base_of(own, right, lower, corner, top, bottom):
        rate = object_rate
        upper = side_by_side(
            own - rate * top[:, :, :tile_cols],
            right - (rate * inside_right) * top[:, :, tile_cols:],
        )
        under = side_by_side(
            lower - (rate * inside_lower) * bottom[:, :, :tile_cols],
            corner - (rate * inside_lower * inside_right) * bottom[:, :, tile_cols:],
        )
        return jnp.concatenate([upper, under], axis=1)

    psi, piece = spread_call(slots, "pieces")(
        *spots, objects, right_one, lower, corner_one, probe, ordered, mats
    )
    back, left, middle, right = misfit_call(slots, "pieces")(
        *spots, live_here, objects, right_two, lower, corner_two, psi, ordered, mats
    )
    upper, under = slice(0, tile_rows), slice(tile_rows, 2 * tile_rows)
    two_from_left = shifted(right, "scan", 1)
    two_from_right = shifted(left, "scan", -1)
    top, bottom, gprobe = first_call(slots, 4 * SIDE + 64)(
        *spots[:2], live_here, back, piece, probe, ordered, mats
    )
    one_from_above = shifted(bottom, "band", 1)
    one_from_below = shifted(top, "band", -1)
    share, two_from_left, two_from_right = tied(gprobe, two_from_left, two_from_right)
    share = scatter_sum(share, CORE)
    share = scatter_sum(share, X)
    share, one_from_above, one_from_below = tied(share, one_from_above, one_from_below)
    share = ring_sum(share, Y)
    share = ring_sum(share, Z)
    share = gather(share, CORE)
    one_left = jnp.concatenate(
        [
            top[:, :, :width] + one_from_above[:, :, :width],
            bottom[:, :, :width] + one_from_below[:, :, :width],
        ],
        axis=1,
    )
    one_right = jnp.concatenate(
        [
            top[:, :, tile_cols:] + one_from_above[:, :, tile_cols:],
            bottom[:, :, tile_cols:] + one_from_below[:, :, tile_cols:],
        ],
        axis=1,
    )
    share, one_left, one_right = tied(share, one_left, one_right)
    share = gather(share, X)
    one_from_left = shifted(after(one_right, share), "scan", 1)
    one_from_right = shifted(after(one_left, share), "scan", -1)
    both = in_order(share)
    total = both[-1, 0]
    left, middle, right, both = tied(left, middle, right, both)
    two_ends = [
        side_by_side(
            left[:, part] + two_from_left[:, part],
            middle[:, part],
            right[:, part] + two_from_right[:, part],
        )
        for part in (upper, under)
    ]
    two_from_above = shifted(two_ends[1], "band", 1)
    two_from_below = shifted(two_ends[0], "band", -1)
    probe = moved_probe(probe, both[: 4 * width], total)
    top, bottom, probe = tied(top, bottom, probe)
    base_one = base_of(
        own_one, right_one, lower_one, corner_one, top + one_from_above, bottom + one_from_below
    )
    base_two = base_of(own_two, right_two, lower_two, corner_two, *two_ends)

    psi, piece, own_one = spread_call(slots, "sides")(
        *spots, base_one, one_from_left, one_from_right, probe, ordered, mats
    )
    back, left, middle, right, own_two = misfit_call(slots, "ends")(
        *spots, live_here, base_two, two_from_above, two_from_below, psi, ordered, mats
    )
    two_from_left = shifted(right, "scan", 1)
    top, bottom, gprobe = first_call(slots, 4 * SIDE)(
        *spots[:2], live_here, back, piece, probe, ordered, mats
    )
    one_from_above = shifted(bottom, "band", 1)
    share, two_from_left = tied(gprobe, two_from_left)
    share = scatter_sum(share, CORE)
    share = scatter_sum(share, X)
    two_bottom = side_by_side(left[:, under] + two_from_left[:, under], middle[:, under])
    two_from_above = shifted(two_bottom, "band", 1)
    share = ring_sum(share, Y)
    share, one_from_above = tied(share, one_from_above)
    share = gather(share, X)
    one_right = top[:, :, tile_cols:] + one_from_above[:, :, tile_cols:]
    one_from_left = shifted(after(one_right, share), "scan", 1)
    share, two_from_above = tied(share, two_from_above)
    share = ring_sum(share, Z)
    share, one_from_left = tied(share, one_from_left)
    probe = moved_probe(probe, gather(share, CORE), total)
    top = top + one_from_above
    two_top = side_by_side(left[:, upper] + two_from_left[:, upper], middle[:, upper])

    own_one = own_one - object_rate * side_by_side(
        top[:, :, :width] + one_from_left, top[:, :, width:tile_cols]
    )
    own_two = own_two - object_rate * (two_top + two_from_above)
    return (jnp.concatenate([own_one, own_two]), probe)


def solution(mesh):
    return jax.shard_map(
        local,
        mesh=mesh,
        in_specs=(
            P(None, "band", "scan"),
            P(),
            P(),
            P("band", "scan", None, None, None),
            P("band", "scan"),
            P("band", "scan"),
            P("band", "scan"),
        ),
        out_specs=(P(None, "band", "scan"), P()),
        check_vma=False,
    )
```

```python
import functools
import math

import jax
import jax.numpy as jnp
import ml_dtypes
import numpy as np
from jax import lax
from jax.experimental import pallas as pl
from jax.experimental.pallas import tpu as pltpu
from jax.sharding import PartitionSpec as P

ITERS = 2
SIDE = 256
HALF = SIDE // 2
TALL = 264
WIDE = 384

object_rate = 0.1
probe_rate = 2.0
power_eps = 1e-06

f32 = jnp.float32
bf16 = jnp.bfloat16


def halves(matrix):
    high = matrix.astype(ml_dtypes.bfloat16)
    low = (matrix - high.astype(np.float64)).astype(ml_dtypes.bfloat16)
    return [high, low]


def tables():
    point = np.arange(HALF)[None, :]
    result = []
    for parity in (0, 1):
        frequency = 2 * np.arange(HALF)[:, None] + parity
        angle = -2.0 * np.pi / SIDE * (frequency * point % SIDE)
        real = np.cos(angle) / math.sqrt(SIDE)
        imag = np.sin(angle) / math.sqrt(SIDE)
        matrix = np.block([[real, -imag], [imag, real]])
        result += halves(matrix) + halves(matrix.T)
    return np.stack(result)


E_HI, E_LO, ET_HI, ET_LO, O_HI, O_LO, OT_HI, OT_LO = range(8)


def dot(a, b):
    return jnp.dot(a, b, preferred_element_type=f32)


def split(x):
    high = x.astype(bf16)
    low = (x - high.astype(f32)).astype(bf16)
    return high, low


def mul_left(m, hi, x):
    high, low = split(x)
    return dot(m[hi], high) + dot(m[hi], low) + dot(m[hi + 1], high)


def mul_right(x, m, hi):
    high, low = split(x)
    return dot(high, m[hi]) + dot(low, m[hi]) + dot(high, m[hi + 1])


def rows(*parts):
    return jnp.concatenate(parts, axis=0)


def cols(*parts):
    return jnp.concatenate(parts, axis=1)


def forward(re, im, m):
    even = mul_left(m, E_HI, rows(re[:HALF] + re[HALF:], im[:HALF] + im[HALF:]))
    odd = mul_left(m, O_HI, rows(re[:HALF] - re[HALF:], im[:HALF] - im[HALF:]))
    re = rows(even[:HALF], odd[:HALF])
    im = rows(even[HALF:], odd[HALF:])
    u = mul_right(cols(re[:, :HALF] + re[:, HALF:], im[:, :HALF] + im[:, HALF:]), m, ET_HI)
    v = mul_right(cols(re[:, :HALF] - re[:, HALF:], im[:, :HALF] - im[:, HALF:]), m, OT_HI)
    return u, v


def backward(u, v, m):
    a = mul_right(u, m, E_HI)
    b = mul_right(v, m, O_HI)
    re = cols(a[:, :HALF] + b[:, :HALF], a[:, :HALF] - b[:, :HALF])
    im = cols(a[:, HALF:] + b[:, HALF:], a[:, HALF:] - b[:, HALF:])
    a = mul_left(m, ET_HI, rows(re[:HALF], im[:HALF]))
    b = mul_left(m, OT_HI, rows(re[HALF:], im[HALF:]))
    re = rows(a[:HALF] + b[:HALF], a[:HALF] - b[:HALF])
    im = rows(a[HALF:] + b[HALF:], a[HALF:] - b[HALF:])
    return re, im


def by_kernel(u, h, place, sign):
    re, im = u[:, :HALF], u[:, HALF:]
    hr = h[0, :, place * HALF : (place + 1) * HALF]
    hi = h[1, :, place * HALF : (place + 1) * HALF]
    if sign > 0:
        return cols(hr * re - hi * im, hr * im + hi * re)
    return cols(hr * re + hi * im, hr * im - hi * re)


def window(ext, plane, spot):
    row0, row_rest, col0, col_rest = spot
    slab = ext[plane, pl.ds(row0, TALL), pl.ds(col0, WIDE)]
    slab = pltpu.roll(slab, lax.rem(WIDE - col_rest, WIDE), 1)[:, :SIDE]
    return pltpu.roll(slab, lax.rem(TALL - row_rest, TALL), 0)[:SIDE]


def place(row_ref, col_ref, slot):
    row = row_ref[slot]
    col = col_ref[slot]
    row_rest = lax.rem(row, 8)
    col_rest = lax.rem(col, 128)
    row0 = pl.multiple_of(row - row_rest, 8)
    col0 = pl.multiple_of(col - col_rest, 128)
    return row0, row_rest, col0, col_rest


def join_pieces(ext, scale, own, right, lower, corner):
    tile_rows, tile_cols = own.shape[1:]
    ext[:, :tile_rows, :tile_cols] = own[...]
    ext[:, :tile_rows, tile_cols:] = right[...]
    ext[:, tile_rows:, :tile_cols] = lower[...]
    ext[:, tile_rows:, tile_cols:] = corner[...]


def join_sides(ext, scale, base, from_left, from_right):
    inside_right, inside_lower = scale[0], scale[1]
    for rows_at, factor in ((0, object_rate), (SIDE, object_rate * inside_lower)):
        at = pl.ds(rows_at, SIDE)
        ext[:, at, :SIDE] = base[:, at, :SIDE] - factor * from_left[:, at]
        ext[:, at, SIDE : 2 * SIDE] = base[:, at, SIDE : 2 * SIDE]
        ext[:, at, 2 * SIDE :] = base[:, at, 2 * SIDE :] - factor * inside_right * from_right[:, at]


def join_ends(ext, scale, base, from_above, from_below):
    inside_right, inside_lower = scale[0], scale[1]
    for rows_at, come, factor in (
        (0, from_above, object_rate),
        (SIDE, from_below, object_rate * inside_lower),
    ):
        at = pl.ds(rows_at, SIDE)
        ext[:, at, : 2 * SIDE] = base[:, at, : 2 * SIDE] - factor * come[:, :, : 2 * SIDE]
        ext[:, at, 2 * SIDE :] = (
            base[:, at, 2 * SIDE :] - factor * inside_right * come[:, :, 2 * SIDE :]
        )


def spread_kernel(join, count, row_ref, col_ref, scale, *refs):
    slot = pl.program_id(0)
    parts, (probe, h, m, psi, piece, *rest) = refs[:count], refs[count:]
    own, ext = rest if len(rest) == 2 else (None, rest[0])

    @pl.when(slot == 0)
    def _():
        join(ext, scale, *parts)
        if own is not None:
            own[...] = ext[:, : own.shape[1], : own.shape[2]]

    per = psi.shape[0]
    for k in range(per):
        spot = place(row_ref, col_ref, slot * per + k)
        ar = window(ext, 0, spot)
        ai = window(ext, 1, spot)
        piece[k, 0] = ar
        piece[k, 1] = ai
        pr, pi = probe[0], probe[1]
        u, v = forward(pr * ar - pi * ai, pr * ai + pi * ar, m)
        re, im = backward(by_kernel(u, h, 0, 1), by_kernel(v, h, 1, 1), m)
        psi[k, 0] = re
        psi[k, 1] = im


def add_window(accum, plane, grad, spot):
    row0, row_rest, col0, col_rest = spot
    tall = rows(grad, jnp.zeros((TALL - SIDE, SIDE), f32))
    tall = pltpu.roll(tall, row_rest, 0)
    wide = cols(tall, jnp.zeros((TALL, WIDE - SIDE), f32))
    wide = pltpu.roll(wide, col_rest, 1)
    accum[plane, pl.ds(row0, TALL), pl.ds(col0, WIDE)] += wide


def misfit_kernel(join, count, row_ref, col_ref, scale, live_ref, *refs):
    slot = pl.program_id(0)
    parts, (psi, pattern, m, back, left, mid, right, *rest) = refs[:count], refs[count:]
    own, ext, accum = rest if len(rest) == 3 else (None, *rest)

    @pl.when(slot == 0)
    def _():
        join(ext, scale, *parts)
        if own is not None:
            own[...] = ext[:, : own.shape[1], : own.shape[2]]
        accum[...] = jnp.zeros_like(accum)

    per = psi.shape[0]
    for k in range(per):
        spot = place(row_ref, col_ref, slot * per + k)
        ar = window(ext, 0, spot)
        ai = window(ext, 1, spot)
        sr, si = psi[k, 0], psi[k, 1]
        u, v = forward(sr * ar - si * ai, sr * ai + si * ar, m)
        live = (slot * per + k < live_ref[0]).astype(f32)

        def weigh(part, measured):
            re, im = part[:, :HALF], part[:, HALF:]
            weight = (re * re + im * im - measured) * live
            return cols(weight * re, weight * im)

        u = weigh(u, pattern[k, :, :HALF])
        v = weigh(v, pattern[k, :, HALF:])
        re, im = backward(u, v, m)
        back[k, 0] = ar * re + ai * im
        back[k, 1] = ar * im - ai * re
        add_window(accum, 0, sr * re + si * im, spot)
        add_window(accum, 1, sr * im - si * re, spot)

    @pl.when(slot == pl.num_programs(0) - 1)
    def _():
        left[...] = accum[:, :, :SIDE]
        mid[...] = accum[:, :, SIDE : 2 * SIDE]
        right[...] = accum[:, :, 2 * SIDE :]


def first_kernel(
    row_ref, col_ref, live_ref, back, piece, probe, h, m, top, bottom, gprobe, accum
):
    slot = pl.program_id(0)
    per = back.shape[0]

    @pl.when(slot == 0)
    def _():
        accum[...] = jnp.zeros_like(accum)
        gprobe[: 4 * SIDE] = jnp.zeros((4 * SIDE, HALF), f32)
        if gprobe.shape[0] > 4 * SIDE:
            live = jnp.minimum(live_ref[0], per * pl.num_programs(0)).astype(f32)
            gprobe[4 * SIDE :] = jnp.full((gprobe.shape[0] - 4 * SIDE, HALF), live)

    for k in range(per):
        spot = place(row_ref, col_ref, slot * per + k)
        u, v = forward(back[k, 0], back[k, 1], m)
        re, im = backward(by_kernel(u, h, 0, -1), by_kernel(v, h, 1, -1), m)
        ar, ai = piece[k, 0], piece[k, 1]
        for at, value in enumerate((ar * re + ai * im, ar * im - ai * re)):
            for side in (0, 1):
                part = value[:, side * HALF : (side + 1) * HALF]
                gprobe[(2 * at + side) * SIDE : (2 * at + side + 1) * SIDE] += part
        pr, pi = probe[0], probe[1]
        add_window(accum, 0, pr * re + pi * im, spot)
        add_window(accum, 1, pr * im - pi * re, spot)

    @pl.when(slot == pl.num_programs(0) - 1)
    def _():
        top[...] = accum[:, :SIDE]
        bottom[...] = accum[:, SIDE:]


def picked(value, move):
    total = None
    for _ in range(3):
        part = value.astype(bf16)
        value = value - part.astype(f32)
        moved = move(part)
        total = moved if total is None else total + moved
    return total


def order_kernel(x, swap, out):
    value = picked(x[0], lambda part: dot(part, swap[0]))
    out[0] = picked(value, lambda part: dot(swap[1], part))


SMEM = pl.BlockSpec(memory_space=pltpu.SMEM)


def whole(shape):
    return pl.BlockSpec(shape, lambda i: (0,) * len(shape))


def per_slot(shape, per=1):
    return pl.BlockSpec((per,) + shape, lambda i: (i,) + (0,) * len(shape))


def call(kernel, name, slots, in_specs, out_specs, out_shape, scratch, flops, size, per=1):
    return pl.pallas_call(
        kernel,
        name=name,
        grid=(slots // per,),
        in_specs=in_specs,
        out_specs=out_specs,
        out_shape=out_shape,
        scratch_shapes=scratch,
        compiler_params=pltpu.CompilerParams(vmem_limit_bytes=32 * 1024 * 1024),
        cost_estimate=pl.CostEstimate(flops=flops, bytes_accessed=size, transcendentals=0),
    )


def shape(*dims):
    return jax.ShapeDtypeStruct(dims, f32)


FIELD = (2, SIDE, SIDE)
MATS = (8, SIDE, SIDE)
EXT = (2, 2 * SIDE, 3 * SIDE)
OWN = (2, SIDE, 2 * SIDE)
SIDES = (2, 2 * SIDE, SIDE)
ENDS = (2, SIDE, 3 * SIDE)
JOINS = {
    "pieces": (join_pieces, [OWN, FIELD, OWN, FIELD]),
    "sides": (join_sides, [EXT, SIDES, SIDES]),
    "ends": (join_ends, [EXT, ENDS, ENDS]),
}
TWO_TRANSFORMS = 24 * 2 * SIDE**3


def specs(shapes):
    return [whole(dims) for dims in shapes]


def two_planes(dims, which):
    return pl.BlockSpec(dims, lambda i: (which, 0, 0))


def part_specs(how, parts, which):
    if how != "pieces":
        return specs(parts)
    return [
        two_planes(parts[0], which),
        whole(parts[1]),
        two_planes(parts[2], which),
        whole(parts[3]),
    ]


def shapes_of(shapes):
    return [shape(*dims) for dims in shapes]


KERNEL = pl.BlockSpec(FIELD, lambda i: (2, 0, 0))


SPREAD_STEP = {"pieces": 1, "sides": 2}
MISFIT_STEP = {"pieces": 2, "ends": 2}


def spread_call(slots, how):
    join, parts = JOINS[how]
    extra = [OWN] if how != "pieces" else []
    per = SPREAD_STEP[how]
    return call(
        functools.partial(spread_kernel, join, len(parts)), "spread", slots,
        [SMEM, SMEM, SMEM, *part_specs(how, parts, 0), whole(FIELD), KERNEL, whole(MATS)],
        [per_slot(FIELD, per), per_slot(FIELD, per), *specs(extra)],
        [shape(slots, *FIELD), shape(slots, *FIELD), *shapes_of(extra)],
        [pltpu.VMEM(EXT, f32)],
        slots * TWO_TRANSFORMS, 9 << 20, per,
    )


def misfit_call(slots, how):
    join, parts = JOINS[how]
    extra = [OWN] if how != "pieces" else []
    per = MISFIT_STEP[how]
    return call(
        functools.partial(misfit_kernel, join, len(parts)), "misfit", slots,
        [SMEM, SMEM, SMEM, SMEM, *part_specs(how, parts, 1), per_slot(FIELD, per), per_slot((SIDE, SIDE), per), whole(MATS)],
        [per_slot(FIELD, per), *specs([SIDES] * 3 + extra)],
        [shape(slots, *FIELD), *shapes_of([SIDES] * 3 + extra)],
        [pltpu.VMEM(EXT, f32), pltpu.VMEM(EXT, f32)],
        slots * TWO_TRANSFORMS, 12 << 20, per,
    )


def first_call(slots, sum_rows):
    return call(
        first_kernel, "first", slots,
        [SMEM, SMEM, SMEM, per_slot(FIELD), per_slot(FIELD), whole(FIELD), KERNEL, whole(MATS)],
        specs([ENDS, ENDS, (sum_rows, HALF)]),
        shapes_of([ENDS, ENDS, (sum_rows, HALF)]),
        [pltpu.VMEM(EXT, f32)],
        slots * TWO_TRANSFORMS, 9 << 20,
    )


def order_call(count):
    return call(
        order_kernel, "order", count,
        [pl.BlockSpec((1, SIDE, SIDE), lambda i: (i, 0, 0)), whole((2, SIDE, SIDE))],
        pl.BlockSpec((1, SIDE, SIDE), lambda i: (i, 0, 0)),
        shape(count, SIDE, SIDE),
        [],
        count * 12 * SIDE**3, 4 << 20,
    )


def shifted(block, axis, distance):
    devices = range(lax.axis_size(axis))
    route = [(i - distance, i) for i in devices if i - distance in devices]
    return lax.ppermute(block, axis, route)


def partners(block, axis, stride, count, hop):
    route = []
    for i in range(lax.axis_size(axis)):
        digit = i // stride % count
        j = i + ((digit - hop) % count - digit) * stride
        route.append((i, j))
    return lax.ppermute(block, axis, route)


CORE, Z, X, Y = ("band", 1, 2), ("band", 2, 4), ("scan", 1, 4), ("scan", 4, 4)


def scatter_sum(x, ring):
    axis, stride, count = ring
    digit = lax.axis_index(axis) // stride % count
    parts = x.reshape(count, x.shape[0] // count, *x.shape[1:])
    total = lax.dynamic_index_in_dim(parts, digit, 0, False)
    for hop in range(1, count):
        sent = lax.dynamic_index_in_dim(parts, (digit - hop) % count, 0, False)
        total = total + partners(sent, axis, stride, count, hop)
    return total


def gather(x, ring):
    axis, stride, count = ring
    digit = lax.axis_index(axis) // stride % count
    result = jnp.zeros((count, *x.shape), f32)
    result = lax.dynamic_update_index_in_dim(result, x, digit, 0)
    for hop in range(1, count):
        part = partners(x, axis, stride, count, hop)
        result = lax.dynamic_update_index_in_dim(result, part, (digit + hop) % count, 0)
    return result.reshape(count * x.shape[0], *x.shape[1:])


def ring_sum(x, ring):
    axis, stride, count = ring
    one, two, three = (partners(x, axis, stride, count, hop) for hop in (1, 2, 3))
    return (x + two) + (one + three)


def in_order(x):
    parts = x.reshape(X[2], CORE[2], -1, x.shape[1])
    return jnp.swapaxes(parts, 0, 1).reshape(x.shape)


def after(value, *others):
    return lax.optimization_barrier((value, *others))[0]


def tied(*values):
    return lax.optimization_barrier(values)


def side_by_side(*parts):
    return jnp.concatenate(parts, axis=2)


def local(objects, probe_field, propagator_phase, patterns, offset_row, offset_column, live_counts):
    width = probe_field.shape[-1]
    tile_rows, tile_cols = objects.shape[1:]
    slots = patterns.shape[2]
    inside_lower = (lax.axis_index("band") < lax.axis_size("band") - 1).astype(f32)
    inside_right = (lax.axis_index("scan") < lax.axis_size("scan") - 1).astype(f32)
    scale = jnp.stack([inside_right, inside_lower])
    mats = jnp.asarray(tables())
    index = np.arange(SIDE)
    order = np.concatenate([np.arange(0, SIDE, 2), np.arange(1, SIDE, 2)])
    swap = (index[:, None] == order[None, :]).astype(ml_dtypes.bfloat16)
    swap = jnp.asarray(np.stack([swap, swap.T]))

    spots = (offset_row[0], offset_column[0], scale)
    live_here = live_counts[0]

    own_one, own_two = objects[:2], objects[2:]
    lower = shifted(objects, "band", -1)
    right_one = shifted(own_one[:, :, :width], "scan", -1)
    right_two = shifted(own_two[:, :, :width], "scan", -1)
    lower_one, lower_two = lower[:2], lower[2:]
    images = jnp.concatenate(
        [patterns[0, 0], jnp.cos(propagator_phase)[None], jnp.sin(propagator_phase)[None]]
    )
    ordered = order_call(slots + 2)(images, swap)
    corner_one = shifted(after(right_one, ordered), "band", -1)
    corner_two = shifted(right_two, "band", -1)
    probe = probe_field

    def moved_probe(probe, summed, total):
        halves_of = summed.reshape(2, 2, width, width // 2)
        summed = side_by_side(halves_of[:, 0], halves_of[:, 1])
        moved = probe - probe_rate / total * summed
        power = jnp.sum(moved * moved)
        return moved * jnp.sqrt(width * width / (power + power_eps))

    def base_of(own, right, lower, corner, top, bottom):
        rate = object_rate
        upper = side_by_side(
            own - rate * top[:, :, :tile_cols],
            right - (rate * inside_right) * top[:, :, tile_cols:],
        )
        under = side_by_side(
            lower - (rate * inside_lower) * bottom[:, :, :tile_cols],
            corner - (rate * inside_lower * inside_right) * bottom[:, :, tile_cols:],
        )
        return jnp.concatenate([upper, under], axis=1)

    psi, piece = spread_call(slots, "pieces")(
        *spots, objects, right_one, lower, corner_one, probe, ordered, mats
    )
    back, left, middle, right = misfit_call(slots, "pieces")(
        *spots, live_here, objects, right_two, lower, corner_two, psi, ordered, mats
    )
    upper, under = slice(0, tile_rows), slice(tile_rows, 2 * tile_rows)
    two_from_left = shifted(right, "scan", 1)
    two_from_right = shifted(left, "scan", -1)
    top, bottom, gprobe = first_call(slots, 4 * SIDE + 64)(
        *spots[:2], live_here, back, piece, probe, ordered, mats
    )
    one_from_above = shifted(bottom, "band", 1)
    one_from_below = shifted(top, "band", -1)
    share, two_from_left, two_from_right = tied(gprobe, two_from_left, two_from_right)
    share = scatter_sum(share, CORE)
    share = scatter_sum(share, X)
    share, one_from_above, one_from_below = tied(share, one_from_above, one_from_below)
    share = ring_sum(share, Y)
    share = ring_sum(share, Z)
    share = gather(share, CORE)
    one_left = jnp.concatenate(
        [
            top[:, :, :width] + one_from_above[:, :, :width],
            bottom[:, :, :width] + one_from_below[:, :, :width],
        ],
        axis=1,
    )
    one_right = jnp.concatenate(
        [
            top[:, :, tile_cols:] + one_from_above[:, :, tile_cols:],
            bottom[:, :, tile_cols:] + one_from_below[:, :, tile_cols:],
        ],
        axis=1,
    )
    share, one_left, one_right = tied(share, one_left, one_right)
    share = gather(share, X)
    one_from_left = shifted(after(one_right, share), "scan", 1)
    one_from_right = shifted(after(one_left, share), "scan", -1)
    both = in_order(share)
    total = both[-1, 0]
    left, middle, right, both = tied(left, middle, right, both)
    two_ends = [
        side_by_side(
            left[:, part] + two_from_left[:, part],
            middle[:, part],
            right[:, part] + two_from_right[:, part],
        )
        for part in (upper, under)
    ]
    two_from_above = shifted(two_ends[1], "band", 1)
    two_from_below = shifted(two_ends[0], "band", -1)
    probe = moved_probe(probe, both[: 4 * width], total)
    top, bottom, probe = tied(top, bottom, probe)
    base_one = base_of(
        own_one, right_one, lower_one, corner_one, top + one_from_above, bottom + one_from_below
    )
    base_two = base_of(own_two, right_two, lower_two, corner_two, *two_ends)

    psi, piece, own_one = spread_call(slots, "sides")(
        *spots, base_one, one_from_left, one_from_right, probe, ordered, mats
    )
    back, left, middle, right, own_two = misfit_call(slots, "ends")(
        *spots, live_here, base_two, two_from_above, two_from_below, psi, ordered, mats
    )
    two_from_left = shifted(right, "scan", 1)
    top, bottom, gprobe = first_call(slots, 4 * SIDE)(
        *spots[:2], live_here, back, piece, probe, ordered, mats
    )
    one_from_above = shifted(bottom, "band", 1)
    share, two_from_left = tied(gprobe, two_from_left)
    share = scatter_sum(share, CORE)
    share = scatter_sum(share, X)
    two_bottom = side_by_side(left[:, under] + two_from_left[:, under], middle[:, under])
    two_from_above = shifted(two_bottom, "band", 1)
    share = ring_sum(share, Y)
    share, one_from_above = tied(share, one_from_above)
    share = gather(share, X)
    one_right = top[:, :, tile_cols:] + one_from_above[:, :, tile_cols:]
    one_from_left = shifted(after(one_right, share), "scan", 1)
    share, two_from_above = tied(share, two_from_above)
    share = ring_sum(share, Z)
    share, one_from_left = tied(share, one_from_left)
    probe = moved_probe(probe, gather(share, CORE), total)
    top = top + one_from_above
    two_top = side_by_side(left[:, upper] + two_from_left[:, upper], middle[:, upper])

    own_one = own_one - object_rate * side_by_side(
        top[:, :, :width] + one_from_left, top[:, :, width:tile_cols]
    )
    own_two = own_two - object_rate * (two_top + two_from_above)
    return (jnp.concatenate([own_one, own_two]), probe)


def solution(mesh):
    return jax.shard_map(
        local,
        mesh=mesh,
        in_specs=(
            P(None, "band", "scan"),
            P(),
            P(),
            P("band", "scan", None, None, None),
            P("band", "scan"),
            P("band", "scan"),
            P("band", "scan"),
        ),
        out_specs=(P(None, "band", "scan"), P()),
        check_vma=False,
    )
```
